32 devices in a mesh: dp: 16 (over z, y, x), tensor: 2 (over core).
Axes of the slice: x: 2, y: 2, z: 4, core: 2. Of those that a mesh axis runs over, the one named last changes fastest.
Arguments:
- images: bfloat16 [16, 584, 1024], P('dp'), may hold values from -6 to 6
- image_mask: int32 [16], P('dp'), may hold values 0 or 1
- cotangent: bfloat16 [16, 584, 1024], P('dp'), may hold values from -6 to 6
- ln1_gain: bfloat16 [1024], replicated, may hold values from 0.5 to 1.5
- ln1_bias: bfloat16 [1024], replicated, may hold values from -1.25 to 1.25
- w_qkv: bfloat16 [1024, 3, 1024], P(None, None, 'tensor'), may hold values from -0.1875 to 0.1875
- qv_bias: bfloat16 [2, 1024], P(None, 'tensor'), may hold values from -1.75 to 1.75
- w_out: bfloat16 [1024, 1024], P('tensor'), may hold values from -3 to 3
- out_bias: bfloat16 [1024], replicated, may hold values from -1.75 to 1.75
- ln2_gain: bfloat16 [1024], replicated, may hold values from 0.5 to 1.5
- ln2_bias: bfloat16 [1024], replicated, may hold values from -1.25 to 1.25
- w_up: bfloat16 [1024, 4096], P(None, 'tensor'), may hold values from -0.1875 to 0.1875
- up_bias: bfloat16 [4096], P('tensor'), may hold values from -1.75 to 1.75
- w_down: bfloat16 [4096, 1024], P('tensor'), may hold values from -0.09375 to 0.09375
- down_bias: bfloat16 [1024], replicated, may hold values from -1.75 to 1.75
Outputs:
- block_output: bfloat16 [16, 584, 1024], P('dp')
- images_grad: bfloat16 [16, 584, 1024], P('dp')
- ln1_gain_grad: float32 [1024], replicated
- ln1_bias_grad: float32 [1024], replicated
- w_qkv_grad: float32 [1024, 3, 1024], P(None, None, 'tensor')
- qv_bias_grad: float32 [2, 1024], P(None, 'tensor')
- w_out_grad: float32 [1024, 1024], P('tensor')
- out_bias_grad: float32 [1024], replicated
- ln2_gain_grad: float32 [1024], replicated
- ln2_bias_grad: float32 [1024], replicated
- w_up_grad: float32 [1024, 4096], P(None, 'tensor')
- up_bias_grad: float32 [4096], P('tensor')
- w_down_grad: float32 [4096, 1024], P('tensor')
- down_bias_grad: float32 [1024], replicated
The draws below stay inside these ranges and needn't reach their ends.
All inputs are finite; a program needn't handle non-finite values. No bound on the sum of `image_mask` on one device may be relied on, other than what follows from the above.
Results may differ from the reference program's by a relative error of at most 0.017.
Values may be sent and summed in bfloat16 or wider, within the bound.
No kernel may reach another device: no remote copies, remote signals or barrier semaphores. Data moves between devices by JAX's collectives and lax.ppermute only.
A program may use at most 192 MiB of HBM per device.

```python
import jax
import jax.numpy as jnp
from jax import lax

D = 1024
HEADS = 16
HD = 64
FF = 4096
VALID = 577
SEQ = 584
IMG_DEV = 1
IMAGES = 16
N_DP = 16


def set_ends(drawn, stream_key, low, largest):
    longest = drawn.shape.index(max(drawn.shape))
    spots = []
    for shift in (0, 1):
        where = [jax.random.randint(jax.random.fold_in(stream_key, axis), (), 0, length) for axis, length in enumerate(drawn.shape)]
        where[longest] = (where[longest] + shift) % drawn.shape[longest]
        spots.append(tuple(where))
    return drawn.at[spots[0]].set(low).at[spots[1]].set(largest)


def block_levels(key, dims, cuts, low, high):
    level, own = 1.0, jax.random.fold_in(key, 6)
    for position, blocks in cuts:
        draws = jnp.exp(jax.random.uniform(jax.random.fold_in(own, position), (blocks,), jnp.float32, low / len(cuts), high / len(cuts)))
        level = level * jnp.repeat(draws, dims[position] // blocks).reshape([-1 if axis == position else 1 for axis in range(len(dims))])
    return level


def normal_values(key, shape, width, reach, pieces=(), held_as=jnp.bfloat16):
    level = block_levels(key, shape, pieces, -0.22, 0.18) if pieces else 1.0
    drawn = jax.random.normal(key, shape, jnp.float32) * width * level
    return jnp.minimum(jnp.maximum(drawn, -reach), reach).astype(held_as)


def setup_inputs(seed: int = 0) -> dict:
    seeds = jax.random.split(jax.random.key(seed), 16)
    return {
        "images": normal_values(seeds[0], (IMAGES, SEQ, D), 1.0, 6.0, ((0, 16),)),
        "image_mask": set_ends((jax.random.randint(seeds[1], (IMAGES,), 0, 8) < 7).astype(jnp.int32), jax.random.fold_in(seeds[1], 1), 0, 1),
        "cotangent": normal_values(seeds[2], (IMAGES, SEQ, D), 1.0, 6.0, ((0, 16),)),
        "ln1_gain": jnp.clip(1.0 + 0.1 * jax.random.normal(seeds[3], (D,), jnp.float32), 0.5, 1.5).astype(jnp.bfloat16),
        "ln1_bias": normal_values(seeds[4], (D,), 0.2, 1.25),
        "w_qkv": normal_values(seeds[5], (D, 3, D), D ** -0.5, 0.1875, ((2, 2),)),
        "qv_bias": normal_values(seeds[6], (2, D), 0.3, 1.75, ((1, 2),)),
        "w_out": normal_values(seeds[7], (D, D), (max(D // 256, 1)) ** -0.5, 3.0, ((0, 2),)),
        "out_bias": normal_values(seeds[8], (D,), 0.3, 1.75),
        "ln2_gain": jnp.clip(1.0 + 0.1 * jax.random.normal(seeds[9], (D,), jnp.float32), 0.5, 1.5).astype(jnp.bfloat16),
        "ln2_bias": normal_values(seeds[10], (D,), 0.2, 1.25),
        "w_up": normal_values(seeds[11], (D, FF), D ** -0.5, 0.1875, ((1, 2),)),
        "up_bias": normal_values(seeds[12], (FF,), 0.3, 1.75, ((0, 2),)),
        "w_down": normal_values(seeds[13], (FF, D), FF ** -0.5, 0.09375, ((0, 2),)),
        "down_bias": normal_values(seeds[14], (D,), 0.3, 1.75),
    }


@jax.custom_vjp
def low(v):
    return lax.optimization_barrier(v.astype(jnp.bfloat16)).astype(jnp.float32)

@jax.custom_vjp
def low_back(v):
    return v

def low_keep(v):
    return (low(v), None)

def low_pass(kept, grad):
    return (grad,)

def back_keep(v):
    return (v, None)

def back_low(kept, grad):
    return (low(grad),)
low.defvjp(low_keep, low_pass)
low_back.defvjp(back_keep, back_low)
eps_norm = 1e-06
highest = lax.Precision.HIGHEST

def normalize(values, gain, shift):
    mean = lax.optimization_barrier(jnp.mean(values, axis=-1, keepdims=True))
    centred = values - mean
    spread = lax.optimization_barrier(jnp.mean(centred * centred, axis=-1, keepdims=True))
    return centred * lax.rsqrt(spread + eps_norm) * gain + shift

def attend(inputs):
    query, keyset, valueset = inputs
    raw = jnp.einsum('qhd,khd->hqk', query, keyset, precision=highest)
    scores = low_back(raw) * HD ** (-0.5)
    live = jnp.arange(SEQ) < VALID
    scores = jnp.where(live, scores, -1e+30)
    peak = lax.optimization_barrier(jnp.max(scores, axis=-1, keepdims=True))
    expo = jnp.exp(scores - peak)
    probs = low(expo / lax.optimization_barrier(jnp.sum(expo, axis=-1, keepdims=True)))
    return jnp.einsum('hqk,khd->qhd', probs, valueset, precision=highest)

def block(slab, params):
    gain1, shift1, w_qkv, qv_bias, w_out, out_bias, gain2, shift2, w_up, up_bias, w_down, down_bias = params
    count = slab.shape[0]
    normed1 = low(normalize(slab, gain1, shift1))
    bias_rows = jnp.stack([qv_bias[0], jnp.zeros_like(qv_bias[0]), qv_bias[1]])
    qkv = jnp.einsum('gsd,dce->gsce', normed1, w_qkv, precision=highest) + bias_rows
    qkv = low_back(low(qkv)).reshape(count, SEQ, 3, HEADS, HD)
    mixed = lax.map(jax.checkpoint(attend), (qkv[:, :, 0], qkv[:, :, 1], qkv[:, :, 2]))
    mixed = low_back(low(mixed.reshape(count, SEQ, D)))
    attn = low_back(jnp.einsum('gse,ed->gsd', mixed, w_out, precision=highest))
    resid = slab + attn + out_bias
    normed2 = low(normalize(resid, gain2, shift2))
    pre = low_back(jnp.einsum('gsd,df->gsf', normed2, w_up, precision=highest) + up_bias)
    act = low(jax.nn.gelu(pre, approximate=False))
    return resid + jnp.einsum('gsf,fd->gsd', act, w_down, precision=highest) + down_bias

def reference(images, image_mask, cotangent, ln1_gain, ln1_bias, w_qkv, qv_bias, w_out, out_bias, ln2_gain, ln2_bias, w_up, up_bias, w_down, down_bias):
    params = tuple((p.astype(jnp.float32) for p in (ln1_gain, ln1_bias, w_qkv, qv_bias, w_out, out_bias, ln2_gain, ln2_bias, w_up, up_bias, w_down, down_bias)))
    slabs = images.astype(jnp.float32).reshape(N_DP, IMG_DEV, SEQ, D)
    grads_in = cotangent.astype(jnp.float32).reshape(N_DP, IMG_DEV, SEQ, D)
    masks = image_mask.reshape(N_DP, IMG_DEV)

    def step(totals, inputs):
        slab, grad_slab, mask_slab = inputs
        result, backward = jax.vjp(block, slab, params)
        grad_x, grad_params = backward(grad_slab * mask_slab.astype(jnp.float32)[:, None, None])
        totals = jax.tree.map(lambda a, b: a + b, totals, grad_params)
        return (totals, (result.astype(jnp.bfloat16), grad_x.astype(jnp.bfloat16)))
    zeros = jax.tree.map(jnp.zeros_like, params)
    totals, (results, grads_x) = lax.scan(step, zeros, (slabs, grads_in, masks))
    return (results.reshape(IMAGES, SEQ, D), grads_x.reshape(IMAGES, SEQ, D), totals[0], totals[1], totals[2], totals[3], totals[4], totals[5], totals[6], totals[7], totals[8], totals[9], totals[10], totals[11])
```

```python
import jax
import jax.numpy as jnp
from jax import lax
from jax.sharding import PartitionSpec as P

HD = 64
VALID = 577
EPS = 1e-06
BF = jnp.bfloat16
F32 = jnp.float32


def stats(values):
    mean = jnp.mean(values, axis=-1, keepdims=True)
    centred = values - mean
    spread = jnp.mean(centred * centred, axis=-1, keepdims=True)
    inv = lax.rsqrt(spread + EPS)
    return centred * inv, inv


def norm_back(unit, inv, gain, grad):
    scaled = grad * gain
    mean_a = jnp.mean(scaled, axis=-1, keepdims=True)
    mean_b = jnp.mean(scaled * unit, axis=-1, keepdims=True)
    return inv * (scaled - mean_a - unit * mean_b)


def inner_rows(left, right):
    return lax.dot_general(
        left, right, (((0,), (0,)), ((), ())), preferred_element_type=F32
    )


def times_back(left, weight):
    return lax.dot_general(
        left, weight, (((1,), (1,)), ((), ())), preferred_element_type=F32
    )


def score_block(query, keyset):
    raw = jnp.einsum("qhd,khd->hqk", query, keyset, preferred_element_type=F32)
    live = jnp.arange(raw.shape[-1]) < VALID
    return jnp.where(live, raw * HD ** (-0.5), -1e30)


def attend_forward(query, keyset, valueset):
    scores = score_block(query, keyset)
    peak = jnp.max(scores, axis=-1, keepdims=True)
    expo = jnp.exp(scores - peak)
    total = jnp.sum(expo, axis=-1, keepdims=True)
    probs = (expo / total).astype(BF)
    mixed = jnp.einsum("hqk,khd->qhd", probs, valueset, preferred_element_type=F32)
    return mixed.astype(BF), peak[..., 0] + jnp.log(total[..., 0])


def attend_backward(query, keyset, valueset, grad_mixed, logsum):
    scores = score_block(query, keyset)
    probs = jnp.exp(scores - logsum[..., None])
    grad_probs = jnp.einsum("qhd,khd->hqk", grad_mixed, valueset, preferred_element_type=F32)
    delta = jnp.sum(probs * grad_probs, axis=-1, keepdims=True)
    grad_scores = (probs * (grad_probs - delta) * HD ** (-0.5)).astype(BF)
    low_probs = probs.astype(BF)
    grad_value = jnp.einsum("hqk,qhd->khd", low_probs, grad_mixed, preferred_element_type=F32)
    grad_query = jnp.einsum("hqk,khd->qhd", grad_scores, keyset, preferred_element_type=F32)
    grad_key = jnp.einsum("hqk,qhd->khd", grad_scores, query, preferred_element_type=F32)
    return jnp.stack([grad_query, grad_key, grad_value], axis=1).astype(BF)


def swap_sum(part):
    if lax.axis_size("tensor") == 2:
        other = lax.ppermute(part, "tensor", [(0, 1), (1, 0)])
        return part.astype(F32) + other.astype(F32)
    return lax.psum(part.astype(F32), "tensor")


def xor_pairs(bit):
    return [(i, i ^ bit) for i in range(lax.axis_size("dp"))]


def bits_of():
    count = lax.axis_size("dp")
    bits = []
    while count > 1:
        if count % 2:
            raise ValueError("dp")
        bits.append(1 << len(bits))
        count //= 2
    return bits


def sum_small(vector):
    for bit in bits_of():
        vector = vector + lax.ppermute(vector, "dp", xor_pairs(bit))
    return vector


def cut_thirds(rows, turn):
    unit = 128
    whole = rows // unit
    base = whole // 3
    counts = [base + (1 if (i - turn) % 3 < whole % 3 else 0) for i in range(3)]
    return [c * unit for c in counts]


def sum_over_dp(matrix, turn):
    bits = bits_of()
    index = lax.axis_index("dp")
    halving = bits[: min(3, len(bits) - 1)]
    swaps = bits[len(halving) :]
    pieces, orders, start = [], [], 0
    for lane, rows in enumerate(cut_thirds(matrix.shape[0], turn)):
        if rows == 0:
            continue
        pieces.append(lax.slice_in_dim(matrix, start, start + rows, axis=0))
        turned = lane % len(halving)
        orders.append(halving[turned:] + halving[:turned])
        start += rows
    for step in range(len(halving)):
        for lane in range(len(pieces)):
            piece, bit = pieces[lane], orders[lane][step]
            half = piece.shape[0] // 2
            side = (index // bit) & 1
            kept = lax.dynamic_slice_in_dim(piece, side * half, half, 0)
            sent = lax.dynamic_slice_in_dim(piece, (1 - side) * half, half, 0)
            pieces[lane] = kept + lax.ppermute(sent, "dp", xor_pairs(bit))
    for bit in swaps:
        for lane in range(len(pieces)):
            pieces[lane] = pieces[lane] + lax.ppermute(pieces[lane], "dp", xor_pairs(bit))
    for step in reversed(range(len(halving))):
        for lane in range(len(pieces)):
            piece, bit = pieces[lane], orders[lane][step]
            other = lax.ppermute(piece, "dp", xor_pairs(bit))
            side = (index // bit) & 1
            pieces[lane] = jnp.where(
                side == 0,
                jnp.concatenate([piece, other], axis=0),
                jnp.concatenate([other, piece], axis=0),
            )
    return jnp.concatenate(pieces, axis=0).astype(F32)


def shards(
    images,
    image_mask,
    cotangent,
    ln1_gain,
    ln1_bias,
    w_qkv,
    qv_bias,
    w_out,
    out_bias,
    ln2_gain,
    ln2_bias,
    w_up,
    up_bias,
    w_down,
    down_bias,
):
    count, seq, width = images.shape
    rows = count * seq
    local = w_qkv.shape[2]
    heads = local // HD
    gain1 = ln1_gain.astype(F32)
    gain2 = ln2_gain.astype(F32)
    inputs = images.reshape(rows, width).astype(F32)
    keep = image_mask.astype(BF)[:, None, None]
    grad_out = (cotangent * keep).reshape(rows, width)
    w_qkv_flat = w_qkv.reshape(width, 3 * local)
    bias_row = jnp.concatenate([qv_bias[0], jnp.zeros_like(qv_bias[0]), qv_bias[1]]).astype(F32)

    unit1, inv1 = stats(inputs)
    normed1 = (unit1 * gain1 + ln1_bias.astype(F32)).astype(BF)
    qkv = (jnp.dot(normed1, w_qkv_flat, preferred_element_type=F32) + bias_row).astype(BF)
    split = qkv.reshape(count, seq, 3, heads, HD)
    attended = [attend_forward(split[i, :, 0], split[i, :, 1], split[i, :, 2]) for i in range(count)]
    mixed = jnp.concatenate([a[0] for a in attended], axis=0).reshape(rows, local)
    attn = swap_sum(jnp.dot(mixed, w_out, preferred_element_type=F32).astype(BF))
    grad_act = times_back(grad_out, w_down)
    resid = inputs + attn + out_bias.astype(F32)
    unit2, inv2 = stats(resid)
    normed2 = (unit2 * gain2 + ln2_bias.astype(F32)).astype(BF)
    pre = jnp.dot(normed2, w_up, preferred_element_type=F32) + up_bias.astype(F32)
    cdf = 0.5 * (1.0 + lax.erf(pre * (0.5**0.5)))
    act = (pre * cdf).astype(BF)
    slope = cdf + pre * jnp.exp(-0.5 * pre * pre) * ((0.5 / jnp.pi) ** 0.5)
    grad_pre = (grad_act * slope).astype(BF)
    grad_wdown = inner_rows(act, grad_out).astype(BF)
    summed_wdown = sum_over_dp(grad_wdown, 0)
    grad_wup = inner_rows(normed2, grad_pre).astype(BF)
    summed_wup = sum_over_dp(grad_wup, 1)
    grad_normed2 = swap_sum(times_back(grad_pre, w_up).astype(BF))
    mlp = swap_sum(jnp.dot(act, w_down, preferred_element_type=F32).astype(BF))
    block_output = (resid + mlp + down_bias.astype(F32)).astype(BF).reshape(images.shape)
    grad_resid = grad_out.astype(F32) + norm_back(unit2, inv2, gain2, grad_normed2)
    resid_low = grad_resid.astype(BF)
    grad_wout = inner_rows(mixed, resid_low).astype(BF)
    summed_wout = sum_over_dp(grad_wout, 2)
    grad_mixed = times_back(resid_low, w_out).astype(BF).reshape(count, seq, heads, HD)
    grad_qkv = jnp.concatenate(
        [
            attend_backward(split[i, :, 0], split[i, :, 1], split[i, :, 2], grad_mixed[i], attended[i][1])
            for i in range(count)
        ],
        axis=0,
    ).reshape(rows, 3 * local)
    grad_wqkv = inner_rows(normed1, grad_qkv).astype(BF)
    summed_wqkv = sum_over_dp(grad_wqkv, 0).reshape(width, 3, local)
    bias_sums = jnp.sum(grad_qkv.astype(F32), axis=0)
    grad_normed1 = swap_sum(times_back(grad_qkv, w_qkv_flat).astype(BF))
    images_grad = (
        (grad_resid + norm_back(unit1, inv1, gain1, grad_normed1)).astype(BF).reshape(images.shape)
    )

    small = [
        jnp.sum(grad_normed1 * unit1, axis=0),
        jnp.sum(grad_normed1, axis=0),
        jnp.sum(grad_resid, axis=0),
        jnp.sum(grad_normed2 * unit2, axis=0),
        jnp.sum(grad_normed2, axis=0),
        jnp.sum(grad_out.astype(F32), axis=0),
        jnp.sum(grad_pre.astype(F32), axis=0),
        bias_sums[:local],
        bias_sums[2 * local :],
    ]
    flat = jnp.concatenate(small)
    length = flat.shape[0]
    padded = -(-length // 1024) * 1024
    flat = sum_small(jnp.pad(flat, (0, padded - length)).reshape(padded // 128, 128)).reshape(-1)
    out, at = [], 0
    for part in small:
        out.append(flat[at : at + part.shape[0]])
        at += part.shape[0]
    return (
        block_output,
        images_grad,
        out[0],
        out[1],
        summed_wqkv,
        jnp.stack([out[7], out[8]]),
        summed_wout,
        out[2],
        out[3],
        out[4],
        summed_wup,
        out[6],
        summed_wdown,
        out[5],
    )


def solution(mesh):
    in_specs = (
        P("dp", None, None),
        P("dp"),
        P("dp", None, None),
        P(),
        P(),
        P(None, None, "tensor"),
        P(None, "tensor"),
        P("tensor", None),
        P(),
        P(),
        P(),
        P(None, "tensor"),
        P("tensor"),
        P("tensor", None),
        P(),
    )
    out_specs = (
        P("dp", None, None),
        P("dp", None, None),
        P(),
        P(),
        P(None, None, "tensor"),
        P(None, "tensor"),
        P("tensor", None),
        P(),
        P(),
        P(),
        P(None, "tensor"),
        P("tensor"),
        P("tensor", None),
        P(),
    )
    return jax.shard_map(shards, mesh=mesh, in_specs=in_specs, out_specs=out_specs, check_vma=False)
```

```python
import jax
import jax.numpy as jnp
from jax import lax
from jax.experimental import pallas as pl
from jax.experimental.pallas import tpu as pltpu
from jax.sharding import PartitionSpec as P

HD = 64
VALID = 577
EPS = 1e-06
BF = jnp.bfloat16
F32 = jnp.float32


def stats(values):
    mean = jnp.mean(values, axis=-1, keepdims=True)
    centred = values - mean
    spread = jnp.mean(centred * centred, axis=-1, keepdims=True)
    inv = lax.rsqrt(spread + EPS)
    return centred * inv, inv


def norm_back(unit, inv, gain, grad):
    scaled = grad * gain
    mean_a = jnp.mean(scaled, axis=-1, keepdims=True)
    mean_b = jnp.mean(scaled * unit, axis=-1, keepdims=True)
    return inv * (scaled - mean_a - unit * mean_b)


def inner_rows(left, right):
    return lax.dot_general(
        left, right, (((0,), (0,)), ((), ())), preferred_element_type=F32
    )


def times_back(left, weight):
    return lax.dot_general(
        left, weight, (((1,), (1,)), ((), ())), preferred_element_type=F32
    )


def score_block(query, keyset):
    raw = jnp.einsum("qhd,khd->hqk", query, keyset, preferred_element_type=F32)
    live = jnp.arange(raw.shape[-1]) < VALID
    return jnp.where(live, raw * HD ** (-0.5), -1e30)


def attend_forward(query, keyset, valueset):
    scores = score_block(query, keyset)
    peak = jnp.max(scores, axis=-1, keepdims=True)
    expo = jnp.exp(scores - peak)
    total = jnp.sum(expo, axis=-1, keepdims=True)
    probs = (expo / total).astype(BF)
    mixed = jnp.einsum("hqk,khd->qhd", probs, valueset, preferred_element_type=F32)
    return mixed.astype(BF), peak[..., 0] + jnp.log(total[..., 0])


def attend_backward(query, keyset, valueset, grad_mixed, logsum):
    scores = score_block(query, keyset)
    probs = jnp.exp(scores - logsum[..., None])
    grad_probs = jnp.einsum("qhd,khd->hqk", grad_mixed, valueset, preferred_element_type=F32)
    delta = jnp.sum(probs * grad_probs, axis=-1, keepdims=True)
    grad_scores = (probs * (grad_probs - delta) * HD ** (-0.5)).astype(BF)
    low_probs = probs.astype(BF)
    grad_value = jnp.einsum("hqk,qhd->khd", low_probs, grad_mixed, preferred_element_type=F32)
    grad_query = jnp.einsum("hqk,khd->qhd", grad_scores, keyset, preferred_element_type=F32)
    grad_key = jnp.einsum("hqk,qhd->khd", grad_scores, query, preferred_element_type=F32)
    return jnp.stack([grad_query, grad_key, grad_value], axis=1).astype(BF)


def swap_sum(part):
    if lax.axis_size("tensor") == 2:
        other = lax.ppermute(part, "tensor", [(0, 1), (1, 0)])
        return part.astype(F32) + other.astype(F32)
    return lax.psum(part.astype(F32), "tensor")


def xor_pairs(bit):
    return [(i, i ^ bit) for i in range(lax.axis_size("dp"))]


def bits_of():
    count = lax.axis_size("dp")
    bits = []
    while count > 1:
        if count % 2:
            raise ValueError("dp")
        bits.append(1 << len(bits))
        count //= 2
    return bits


def sum_small(vector):
    for bit in bits_of():
        vector = vector + lax.ppermute(vector, "dp", xor_pairs(bit))
    return vector


def cut_thirds(rows, turn):
    unit = 128
    whole = rows // unit
    base = whole // 3
    counts = [base + (1 if (i - turn) % 3 < whole % 3 else 0) for i in range(3)]
    return [c * unit for c in counts]


def sum_over_dp(matrix, turn):
    bits = bits_of()
    index = lax.axis_index("dp")
    halving = bits[: min(3, len(bits) - 1)]
    swaps = bits[len(halving) :]
    pieces, orders, start = [], [], 0
    for lane, rows in enumerate(cut_thirds(matrix.shape[0], turn)):
        if rows == 0:
            continue
        pieces.append(lax.slice_in_dim(matrix, start, start + rows, axis=0))
        turned = lane % len(halving)
        orders.append(halving[turned:] + halving[:turned])
        start += rows
    for step in range(len(halving)):
        for lane in range(len(pieces)):
            piece, bit = pieces[lane], orders[lane][step]
            half = piece.shape[0] // 2
            side = (index // bit) & 1
            kept = lax.dynamic_slice_in_dim(piece, side * half, half, 0)
            sent = lax.dynamic_slice_in_dim(piece, (1 - side) * half, half, 0)
            pieces[lane] = kept + lax.ppermute(sent, "dp", xor_pairs(bit))
    for bit in swaps:
        for lane in range(len(pieces)):
            pieces[lane] = pieces[lane] + lax.ppermute(pieces[lane], "dp", xor_pairs(bit))
    for step in reversed(range(len(halving))):
        for lane in range(len(pieces)):
            piece, bit = pieces[lane], orders[lane][step]
            other = lax.ppermute(piece, "dp", xor_pairs(bit))
            side = (index // bit) & 1
            pieces[lane] = jnp.where(
                side == 0,
                jnp.concatenate([piece, other], axis=0),
                jnp.concatenate([other, piece], axis=0),
            )
    return jnp.concatenate(pieces, axis=0).astype(F32)


def shards_any(
    images,
    image_mask,
    cotangent,
    ln1_gain,
    ln1_bias,
    w_qkv,
    qv_bias,
    w_out,
    out_bias,
    ln2_gain,
    ln2_bias,
    w_up,
    up_bias,
    w_down,
    down_bias,
):
    count, seq, width = images.shape
    rows = count * seq
    local = w_qkv.shape[2]
    heads = local // HD
    gain1 = ln1_gain.astype(F32)
    gain2 = ln2_gain.astype(F32)
    inputs = images.reshape(rows, width).astype(F32)
    keep = image_mask.astype(BF)[:, None, None]
    grad_out = (cotangent * keep).reshape(rows, width)
    w_qkv_flat = w_qkv.reshape(width, 3 * local)
    bias_row = jnp.concatenate([qv_bias[0], jnp.zeros_like(qv_bias[0]), qv_bias[1]]).astype(F32)

    unit1, inv1 = stats(inputs)
    normed1 = (unit1 * gain1 + ln1_bias.astype(F32)).astype(BF)
    qkv = (jnp.dot(normed1, w_qkv_flat, preferred_element_type=F32) + bias_row).astype(BF)
    split = qkv.reshape(count, seq, 3, heads, HD)
    attended = [attend_forward(split[i, :, 0], split[i, :, 1], split[i, :, 2]) for i in range(count)]
    mixed = jnp.concatenate([a[0] for a in attended], axis=0).reshape(rows, local)
    attn = swap_sum(jnp.dot(mixed, w_out, preferred_element_type=F32).astype(BF))
    grad_act = times_back(grad_out, w_down)
    resid = inputs + attn + out_bias.astype(F32)
    unit2, inv2 = stats(resid)
    normed2 = (unit2 * gain2 + ln2_bias.astype(F32)).astype(BF)
    pre = jnp.dot(normed2, w_up, preferred_element_type=F32) + up_bias.astype(F32)
    cdf = 0.5 * (1.0 + lax.erf(pre * (0.5**0.5)))
    act = (pre * cdf).astype(BF)
    slope = cdf + pre * jnp.exp(-0.5 * pre * pre) * ((0.5 / jnp.pi) ** 0.5)
    grad_pre = (grad_act * slope).astype(BF)
    grad_wdown = inner_rows(act, grad_out).astype(BF)
    summed_wdown = sum_over_dp(grad_wdown, 0)
    grad_wup = inner_rows(normed2, grad_pre).astype(BF)
    summed_wup = sum_over_dp(grad_wup, 1)
    grad_normed2 = swap_sum(times_back(grad_pre, w_up).astype(BF))
    mlp = swap_sum(jnp.dot(act, w_down, preferred_element_type=F32).astype(BF))
    block_output = (resid + mlp + down_bias.astype(F32)).astype(BF).reshape(images.shape)
    grad_resid = grad_out.astype(F32) + norm_back(unit2, inv2, gain2, grad_normed2)
    resid_low = grad_resid.astype(BF)
    grad_wout = inner_rows(mixed, resid_low).astype(BF)
    summed_wout = sum_over_dp(grad_wout, 2)
    grad_mixed = times_back(resid_low, w_out).astype(BF).reshape(count, seq, heads, HD)
    grad_qkv = jnp.concatenate(
        [
            attend_backward(split[i, :, 0], split[i, :, 1], split[i, :, 2], grad_mixed[i], attended[i][1])
            for i in range(count)
        ],
        axis=0,
    ).reshape(rows, 3 * local)
    grad_wqkv = inner_rows(normed1, grad_qkv).astype(BF)
    summed_wqkv = sum_over_dp(grad_wqkv, 0).reshape(width, 3, local)
    bias_sums = jnp.sum(grad_qkv.astype(F32), axis=0)
    grad_normed1 = swap_sum(times_back(grad_qkv, w_qkv_flat).astype(BF))
    images_grad = (
        (grad_resid + norm_back(unit1, inv1, gain1, grad_normed1)).astype(BF).reshape(images.shape)
    )

    small = [
        jnp.sum(grad_normed1 * unit1, axis=0),
        jnp.sum(grad_normed1, axis=0),
        jnp.sum(grad_resid, axis=0),
        jnp.sum(grad_normed2 * unit2, axis=0),
        jnp.sum(grad_normed2, axis=0),
        jnp.sum(grad_out.astype(F32), axis=0),
        jnp.sum(grad_pre.astype(F32), axis=0),
        bias_sums[:local],
        bias_sums[2 * local :],
    ]
    flat = jnp.concatenate(small)
    length = flat.shape[0]
    padded = -(-length // 1024) * 1024
    flat = sum_small(jnp.pad(flat, (0, padded - length)).reshape(padded // 128, 128)).reshape(-1)
    out, at = [], 0
    for part in small:
        out.append(flat[at : at + part.shape[0]])
        at += part.shape[0]
    return (
        block_output,
        images_grad,
        out[0],
        out[1],
        summed_wqkv,
        jnp.stack([out[7], out[8]]),
        summed_wout,
        out[2],
        out[3],
        out[4],
        summed_wup,
        out[6],
        summed_wdown,
        out[5],
    )


ANY = pl.BlockSpec(memory_space=pl.ANY)
VM = pl.BlockSpec(memory_space=pltpu.VMEM)
SM = pl.BlockSpec(memory_space=pltpu.SMEM)
MIB = 1024 * 1024


def shape_of(shape, dtype):
    return jax.ShapeDtypeStruct(shape, dtype)


def nn(left, right):
    return jnp.dot(left, right, preferred_element_type=F32)


def normal_unit(values):
    mean = jnp.mean(values, axis=-1, keepdims=True)
    centred = values - mean
    spread = jnp.mean(centred * centred, axis=-1, keepdims=True)
    inv = lax.rsqrt(spread + EPS)
    return centred * inv, inv


def call(body, args, in_specs, outs, out_specs, scratch=(), grid=(), vmem=40, aliases=None, name=None, prefetch=0):
    spec = pltpu.PrefetchScalarGridSpec(
        num_scalar_prefetch=prefetch,
        grid=grid,
        in_specs=in_specs,
        out_specs=out_specs,
        scratch_shapes=list(scratch),
    )
    return pl.pallas_call(
        body,
        out_shape=outs,
        grid_spec=spec,
        input_output_aliases=aliases or {},
        compiler_params=pltpu.CompilerParams(vmem_limit_bytes=vmem * MIB),
        name=name,
    )(*args)


def row_chunks(rows):
    units, parts = rows // 16, 4
    cuts = [16 * (units * i // parts) for i in range(parts)] + [rows]
    return [(cuts[i], cuts[i + 1] - cuts[i]) for i in range(parts)]


def lane_halves():
    return lax.broadcasted_iota(jnp.int32, (1, 2 * HD), 1) < HD


def key_mask(length):
    return jnp.where(lax.broadcasted_iota(jnp.int32, (1, length), 1) < VALID, 0.0, -1e30)


def attend_kernel(
    x_ref, vec_ref, bias_ref, w_ref, wo_ref, part_ref, q_ref, k_ref, v_ref, mixed_ref, n1_ref, lse_ref, w_buf, sems
):
    rows, width = x_ref.shape
    padded = q_ref.shape[0]
    local = q_ref.shape[1]
    copies = [pltpu.make_async_copy(w_ref.at[c], w_buf.at[c], sems.at[c]) for c in range(3)]
    for copy in copies:
        copy.start()
    unit, _ = normal_unit(x_ref[...].astype(F32))
    normed = unit * vec_ref[0:1, :] + vec_ref[1:2, :]
    n1_ref[...] = jnp.concatenate([normed, jnp.zeros((padded - rows, width), F32)], axis=0).astype(BF)
    lse_ref[...] = jnp.zeros(lse_ref.shape, F32)
    live = lax.broadcasted_iota(jnp.int32, (padded, 1), 0) < rows
    for c, (ref, scale) in enumerate(((q_ref, HD ** (-0.5)), (k_ref, 1.0), (v_ref, 1.0))):
        copies[c].wait()
        for at in range(0, local, 256):
            made = nn(n1_ref[...], w_buf[c, :, at : at + 256]) + bias_ref[c : c + 1, at : at + 256]
            made = jnp.where(live, made, 0.0).astype(BF)
            ref[:, at : at + 256] = made * jnp.asarray(scale, BF)
    mask = key_mask(padded)
    first = lane_halves()
    lane = lax.broadcasted_iota(jnp.int32, (1, 128), 1)

    def pair(p, carry):
        cols = pl.ds(pl.multiple_of(p * 128, 128), 128)
        keys, vals = k_ref[:, cols], v_ref[:, cols]
        zero = jnp.zeros_like(keys)
        own = (jnp.where(first, keys, zero), jnp.where(first, zero, keys))
        for at, size in row_chunks(padded):
            query = q_ref[at : at + size, cols]
            outs = []
            logs = lse_ref[at : at + size, :]
            for h in range(2):
                scores = times_back(query, own[h]) + mask
                peak = jnp.max(scores, axis=-1, keepdims=True)
                expo = jnp.exp(scores - peak)
                total = jnp.sum(expo, axis=-1, keepdims=True)
                probs = (expo * (1.0 / total)).astype(BF)
                outs.append(nn(probs, vals))
                logs = jnp.where(lane == 2 * p + h, peak + jnp.log(total), logs)
            lse_ref[at : at + size, :] = logs
            mixed_ref[at : at + size, cols] = jnp.where(first, outs[0], outs[1]).astype(BF)
        return carry

    lax.fori_loop(0, local // 128, pair, 0)
    for at in range(0, width, 256):
        made = nn(mixed_ref[...], wo_ref[:, at : at + 256])
        part_ref[:, at : at + 256] = made[:rows].astype(BF)


def attend(x, vec, bias, w3, w_out):
    rows, width = x.shape
    local = w3.shape[2]
    padded = -(-rows // 16) * 16
    wide = shape_of((padded, local), BF)
    outs = (
        shape_of((rows, width), BF),
        wide,
        wide,
        wide,
        wide,
        shape_of((padded, width), BF),
        shape_of((padded, 128), F32),
    )
    return call(
        attend_kernel,
        (x, vec, bias, w3, w_out),
        [VM, VM, VM, ANY, VM],
        outs,
        (VM,) * 7,
        [pltpu.VMEM((3, width, local), BF), pltpu.SemaphoreType.DMA((3,))],
        name="attend",
    )


def grad_act_kernel(mask_ref, cot_ref, wd_ref, ga_ref, bd_ref, go):
    @pl.when(pl.program_id(0) == 0)
    def _():
        masked = cot_ref[...].astype(F32) * mask_ref[0].astype(F32)
        go[...] = masked.astype(BF)
        bd_ref[...] = jnp.sum(masked, axis=0, keepdims=True)

    ga_ref[...] = times_back(go[...], wd_ref[...]).astype(BF)


def grad_act_of(mask, cot, w_down):
    rows, width = cot.shape
    hidden = w_down.shape[0]
    tile = 512
    return call(
        grad_act_kernel,
        (mask, cot, w_down),
        [pl.BlockSpec((rows, width), lambda j, m: (0, 0)), pl.BlockSpec((tile, width), lambda j, m: (j, 0))],
        (shape_of((rows, hidden), BF), shape_of((1, width), F32)),
        (pl.BlockSpec((rows, tile), lambda j, m: (0, j)), pl.BlockSpec((1, width), lambda j, m: (0, 0))),
        [pltpu.VMEM((rows, width), BF)],
        (hidden // tile,),
        name="grad_act",
        prefetch=1,
    )


LANES = ((0, 20, 0), (20, 24, 1), (44, 20, 2))


def feed_kernel(
    mask_ref, sides_ref, x_ref, pa_ref, pb_ref, vec_ref, cot_ref, wu_ref, ub_ref, ga_ref,
    act_ref, gp_ref, bu_ref, ka_ref, sa_ref, kb_ref, sb_ref, kc_ref, sc_ref, n2, go, grads, sems,
):
    step = pl.program_id(0)
    steps = pl.num_programs(0)
    tile = wu_ref.shape[1]
    width = x_ref.shape[1]
    blocks = tile // 64

    @pl.when(step == 0)
    def _():
        resid = x_ref[...].astype(F32) + (pa_ref[...].astype(F32) + pb_ref[...].astype(F32)) + vec_ref[2:3, :]
        unit, _ = normal_unit(resid)
        n2[...] = (unit * vec_ref[3:4, :] + vec_ref[4:5, :]).astype(BF)
        go[...] = (cot_ref[...].astype(F32) * mask_ref[0].astype(F32)).astype(BF)

    pre = nn(n2[...], wu_ref[...]) + ub_ref[...].astype(F32)
    cdf = 0.5 * (1.0 + lax.erf(pre * (0.5**0.5)))
    act = (pre * cdf).astype(BF)
    slope = cdf + pre * jnp.exp(-0.5 * pre * pre) * ((0.5 / jnp.pi) ** 0.5)
    grad_pre = (ga_ref[...].astype(F32) * slope).astype(BF)
    act_ref[...] = act
    gp_ref[...] = grad_pre
    bu_ref[...] = jnp.sum(grad_pre.astype(F32), axis=0, keepdims=True)
    down = inner_rows(act, go[...]).astype(BF)
    grads[pl.ds(step * blocks, blocks)] = down.reshape(blocks, 2, 32, width)
    up = inner_rows(n2[...], grad_pre).astype(BF)
    per = width // tile
    cols = pl.ds(pl.multiple_of(lax.rem(step, per) * tile, tile), tile)
    grads[pl.ds(steps * blocks, width // 32), step // per, :, cols] = up.reshape(width // 32, 32, tile)

    def pieces(lane, keep, send):
        first, count, bit = LANES[lane]
        half, side = count // 2, sides_ref[bit]
        return (
            pltpu.make_async_copy(grads.at[pl.ds(first + side * half, half)], keep, sems.at[2 * lane]),
            pltpu.make_async_copy(grads.at[pl.ds(first + (1 - side) * half, half)], send, sems.at[2 * lane + 1]),
        )

    early = pieces(0, ka_ref, sa_ref)

    @pl.when(step == LANES[0][1] // blocks)
    def _():
        for copy in early:
            copy.start()

    @pl.when(step == steps - 1)
    def _():
        late = pieces(2, kc_ref, sc_ref) + pieces(1, kb_ref, sb_ref)
        for copy in late:
            copy.start()
        for copy in early + late:
            copy.wait()


def feed(mask, sides, x, pa, pb, vec, cot, w_up, up_bias, ga):
    rows, width = x.shape
    hidden = w_up.shape[1]
    tile = 256
    fixed = pl.BlockSpec((rows, width), lambda j, m, s: (0, 0))
    cols = pl.BlockSpec((rows, tile), lambda j, m, s: (0, j))
    bias = pl.BlockSpec((1, tile), lambda j, m, s: (0, j))
    lanes = []
    for _, count, _ in LANES:
        lanes += [shape_of((count // 2, 2, 32, width), BF)] * 2
    return call(
        feed_kernel,
        (mask, sides, x, pa, pb, vec, cot, w_up, up_bias, ga),
        [
            fixed,
            fixed,
            fixed,
            pl.BlockSpec((8, width), lambda j, m, s: (0, 0)),
            fixed,
            pl.BlockSpec((width, tile), lambda j, m, s: (0, j)),
            bias,
            cols,
        ],
        (shape_of((rows, hidden), BF), shape_of((rows, hidden), BF), shape_of((1, hidden), F32), *lanes),
        (cols, cols, bias) + (ANY,) * 6,
        [
            pltpu.VMEM((rows, width), BF),
            pltpu.VMEM((rows, width), BF),
            pltpu.VMEM((2 * hidden // 64, 2, 32, width), BF),
            pltpu.SemaphoreType.DMA((6,)),
        ],
        (hidden // tile,),
        name="feed",
        prefetch=2,
    )


def back_up_kernel(gp_ref, wu_ref, out_ref):
    out_ref[...] = times_back(gp_ref[...], wu_ref[...]).astype(BF)


def back_up(gp, w_up):
    rows, hidden = gp.shape
    width = w_up.shape[0]
    return call(
        back_up_kernel,
        (gp, w_up),
        [pl.BlockSpec((rows, hidden), lambda j: (0, 0)), pl.BlockSpec((256, hidden), lambda j: (j, 0))],
        shape_of((rows, width), BF),
        pl.BlockSpec((rows, 256), lambda j: (0, j)),
        grid=(width // 256,),
        name="back_up",
    )


def down_kernel(act_ref, wd_ref, out_ref):
    out_ref[...] = nn(act_ref[...], wd_ref[...]).astype(BF)


def down(act, w_down):
    rows, hidden = act.shape
    width = w_down.shape[1]
    return call(
        down_kernel,
        (act, w_down),
        [pl.BlockSpec((rows, hidden), lambda j: (0, 0)), pl.BlockSpec((hidden, 256), lambda j: (0, j))],
        shape_of((rows, width), BF),
        pl.BlockSpec((rows, 256), lambda j: (0, j)),
        grid=(width // 256,),
        name="down",
    )


def resid_back_kernel(
    mask_ref, sides_ref, x_ref, pa_ref, pb_ref, vec_ref, ga_ref, gb_ref, cot_ref, mixed_ref, wo_ref,
    gr_ref, gm_ref, sums_ref, keep_ref, send_ref, low, grads, sems,
):
    rows, width = x_ref.shape
    padded, local = mixed_ref.shape
    resid = x_ref[...].astype(F32) + (pa_ref[...].astype(F32) + pb_ref[...].astype(F32)) + vec_ref[2:3, :]
    unit, inv = normal_unit(resid)
    grad = ga_ref[...].astype(F32) + gb_ref[...].astype(F32)
    total = cot_ref[...].astype(F32) * mask_ref[0].astype(F32) + norm_back(unit, inv, vec_ref[3:4, :], grad)
    gr_ref[...] = total
    low[...] = jnp.concatenate([total, jnp.zeros((padded - rows, width), F32)], axis=0).astype(BF)
    sums_ref[...] = jnp.concatenate(
        [
            jnp.sum(total, axis=0, keepdims=True),
            jnp.sum(grad * unit, axis=0, keepdims=True),
            jnp.sum(grad, axis=0, keepdims=True),
            jnp.zeros((5, width), F32),
        ],
        axis=0,
    )
    for at in range(0, width, 256):
        grads[:, at : at + 256] = inner_rows(mixed_ref[...], low[:, at : at + 256]).astype(BF)
    half, side = local // 2, sides_ref[1]
    copies = (
        pltpu.make_async_copy(grads.at[pl.ds(pl.multiple_of(side * half, half), half)], keep_ref, sems.at[0]),
        pltpu.make_async_copy(grads.at[pl.ds(pl.multiple_of((1 - side) * half, half), half)], send_ref, sems.at[1]),
    )
    for copy in copies:
        copy.start()
    for at in range(0, local, 256):
        gm_ref[:, at : at + 256] = times_back(low[...], wo_ref[at : at + 256, :]).astype(BF)
    for copy in copies:
        copy.wait()


def resid_back(mask, sides, x, pa, pb, vec, ga, gb, cot, mixed, w_out):
    rows, width = x.shape
    padded, local = mixed.shape
    return call(
        resid_back_kernel,
        (mask, sides, x, pa, pb, vec, ga, gb, cot, mixed, w_out),
        [VM] * 9,
        (
            shape_of((rows, width), F32),
            shape_of((padded, local), BF),
            shape_of((8, width), F32),
            shape_of((local // 2, width), BF),
            shape_of((local // 2, width), BF),
        ),
        (VM, VM, VM, ANY, ANY),
        [pltpu.VMEM((padded, width), BF), pltpu.VMEM((local, width), BF), pltpu.SemaphoreType.DMA((2,))],
        name="resid_back",
        prefetch=2,
    )


def attend_back_kernel(q_ref, k_ref, v_ref, mixed_ref, gm_ref, lse_ref, out_ref, probs_s, slopes_s):
    padded, local = q_ref.shape
    mask = key_mask(padded)
    first = lane_halves()
    lane = lax.broadcasted_iota(jnp.int32, (1, 128), 1)

    def pair(p, carry):
        cols = pl.ds(pl.multiple_of(p * 128, 128), 128)
        keys, vals = k_ref[:, cols], v_ref[:, cols]
        zero = jnp.zeros_like(keys)
        own_k = (jnp.where(first, keys, zero), jnp.where(first, zero, keys))
        own_v = (jnp.where(first, vals, zero), jnp.where(first, zero, vals))
        for at, size in row_chunks(padded):
            query = q_ref[at : at + size, cols]
            grad = gm_ref[at : at + size, cols]
            both = grad.astype(F32) * mixed_ref[at : at + size, cols].astype(F32)
            logs = lse_ref[at : at + size, :]
            outs = []
            for h in range(2):
                own_lanes = first if h == 0 else jnp.logical_not(first)
                delta = jnp.sum(jnp.where(own_lanes, both, 0.0), axis=-1, keepdims=True)
                log = jnp.sum(jnp.where(lane == 2 * p + h, logs, 0.0), axis=-1, keepdims=True)
                probs = jnp.exp(times_back(query, own_k[h]) + mask - log)
                slope = (probs * (times_back(grad, own_v[h]) - delta)).astype(BF)
                probs_s[h, at : at + size, :] = probs.astype(BF)
                slopes_s[h, at : at + size, :] = slope
                outs.append(nn(slope, keys))
            out_ref[at : at + size, cols] = (jnp.where(first, outs[0], outs[1]) * HD ** (-0.5)).astype(BF)
        grad_t = gm_ref[:, cols].astype(F32).T.astype(BF)
        query_t = q_ref[:, cols].astype(F32).T.astype(BF)
        grad_k = [nn(query_t[HD * h : HD * h + HD], slopes_s[h]) for h in range(2)]
        grad_v = [nn(grad_t[HD * h : HD * h + HD], probs_s[h]) for h in range(2)]
        cols_k = pl.ds(pl.multiple_of(local + p * 128, 128), 128)
        cols_v = pl.ds(pl.multiple_of(2 * local + p * 128, 128), 128)
        out_ref[:, cols_k] = jnp.concatenate(grad_k, axis=0).T.astype(BF)
        out_ref[:, cols_v] = jnp.concatenate(grad_v, axis=0).T.astype(BF)
        return carry

    lax.fori_loop(0, local // 128, pair, 0)


def attend_back(q, k, v, mixed, gm, lse):
    padded, local = q.shape
    return call(
        attend_back_kernel,
        (q, k, v, mixed, gm, lse),
        [VM] * 6,
        shape_of((padded, 3 * local), BF),
        VM,
        [pltpu.VMEM((2, padded, padded), BF), pltpu.VMEM((2, padded, padded), BF)],
        name="attend_back",
    )


def qkv_grad_kernel(sides_ref, n1_ref, g_ref, bias_ref, ka_ref, sa_ref, kb_ref, sb_ref, grads, sems):
    width = n1_ref.shape[1]
    local = g_ref.shape[1] // 3
    for at in range(0, width, 256):
        made = inner_rows(n1_ref[:, at : at + 256], g_ref[...]).astype(BF)
        for c in range(3):
            grads[c * width + at : c * width + at + 256, :] = made[:, c * local : (c + 1) * local]
    half = 3 * width // 4
    sx, sz = sides_ref[0], sides_ref[2]
    copies = [
        pltpu.make_async_copy(grads.at[pl.ds(pl.multiple_of(start, 256), half)], ref, sems.at[i])
        for i, (start, ref) in enumerate(
            (
                (sx * half, ka_ref),
                ((1 - sx) * half, sa_ref),
                ((2 + sz) * half, kb_ref),
                ((3 - sz) * half, sb_ref),
            )
        )
    ]
    for copy in copies:
        copy.start()
    bias_ref[...] = jnp.sum(g_ref[...].astype(F32), axis=0, keepdims=True)
    for copy in copies:
        copy.wait()


def qkv_grad(sides, n1, grads):
    width = n1.shape[1]
    local = grads.shape[1] // 3
    part = shape_of((3 * width // 4, local), BF)
    return call(
        qkv_grad_kernel,
        (sides, n1, grads),
        [VM, VM],
        (shape_of((1, 3 * local), F32), part, part, part, part),
        (VM, ANY, ANY, ANY, ANY),
        [pltpu.VMEM((3 * width, local), BF), pltpu.SemaphoreType.DMA((4,))],
        name="qkv_grad",
        prefetch=1,
    )


def back_in_kernel(g_ref, w_ref, out_ref):
    rows = out_ref.shape[0]
    local = w_ref.shape[2]
    total = times_back(g_ref[:, :local], w_ref[0])
    for c in range(1, 3):
        total += times_back(g_ref[:, c * local : (c + 1) * local], w_ref[c])
    out_ref[...] = total[:rows].astype(BF)


def back_in(grads, w3, rows):
    padded = grads.shape[0]
    _, width, local = w3.shape
    return call(
        back_in_kernel,
        (grads, w3),
        [
            pl.BlockSpec((padded, 3 * local), lambda j: (0, 0)),
            pl.BlockSpec((3, 256, local), lambda j: (0, j, 0)),
        ],
        shape_of((rows, width), BF),
        pl.BlockSpec((rows, 256), lambda j: (0, j)),
        grid=(width // 256,),
        name="back_in",
    )


def images_back_kernel(x_ref, vec_ref, gr_ref, ga_ref, gb_ref, bd_ref, bu_ref, s2_ref, bq_ref, out_ref, pack_ref):
    unit, inv = normal_unit(x_ref[...].astype(F32))
    grad = ga_ref[...].astype(F32) + gb_ref[...].astype(F32)
    out_ref[...] = (gr_ref[...] + norm_back(unit, inv, vec_ref[0:1, :], grad)).astype(BF)
    width = x_ref.shape[1]
    hidden = bu_ref.shape[1]
    local = bq_ref.shape[1] // 3
    pack_ref[0:1, :] = jnp.sum(grad * unit, axis=0, keepdims=True)
    pack_ref[1:2, :] = jnp.sum(grad, axis=0, keepdims=True)
    pack_ref[2:5, :] = s2_ref[0:3, :]
    pack_ref[5:6, :] = bd_ref[...]
    for i in range(hidden // width):
        pack_ref[6 + i : 7 + i, :] = bu_ref[:, i * width : (i + 1) * width]
    after = 6 + hidden // width
    pack_ref[after : after + 1, :local] = bq_ref[:, :local]
    pack_ref[after : after + 1, local:] = bq_ref[:, 2 * local :]
    pack_ref[after + 1 :, :] = jnp.zeros((pack_ref.shape[0] - after - 1, width), F32)


def images_back(x, vec, gr, ga, gb, bd, bu, s2, bq):
    return call(
        images_back_kernel,
        (x, vec, gr, ga, gb, bd, bu, s2, bq),
        [VM] * 9,
        (shape_of(x.shape, BF), shape_of((16, x.shape[1]), F32)),
        (VM, VM),
        name="images_back",
    )


def block_out_kernel(x_ref, pa_ref, pb_ref, vec_ref, ma_ref, mb_ref, out_ref):
    resid = x_ref[...].astype(F32) + (pa_ref[...].astype(F32) + pb_ref[...].astype(F32)) + vec_ref[2:3, :]
    out_ref[...] = (resid + (ma_ref[...].astype(F32) + mb_ref[...].astype(F32)) + vec_ref[5:6, :]).astype(BF)


def block_out(x, pa, pb, vec, ma, mb):
    return call(block_out_kernel, (x, pa, pb, vec, ma, mb), [VM] * 6, shape_of(x.shape, BF), VM, name="block_out")


def add_split_kernel(sides_ref, k0_ref, k1_ref, r0_ref, r1_ref, keep_ref, send_ref):
    keep_ref[...] = (k0_ref[...].astype(F32) + r0_ref[...].astype(F32)).astype(BF)
    send_ref[...] = (k1_ref[...].astype(F32) + r1_ref[...].astype(F32)).astype(BF)


def add_split(sides, bit, keep, recv):
    rows, width = keep.shape
    half = rows // 2
    count = 2 if half % 32 == 0 and half >= 256 else 1
    block = (half // count, width)
    own = pl.BlockSpec(block, lambda i, s: (s[bit] * count + i, 0))
    other = pl.BlockSpec(block, lambda i, s: ((1 - s[bit]) * count + i, 0))
    out = pl.BlockSpec(block, lambda i, s: (i, 0))
    return call(
        add_split_kernel,
        (sides, keep, keep, recv, recv),
        [own, other, own, other],
        (shape_of((half, width), BF),) * 2,
        (out, out),
        grid=(count,),
        name="add_split",
        prefetch=1,
        vmem=16,
    )


def add_kernel(a_ref, b_ref, out_ref):
    out_ref[...] = (a_ref[...].astype(F32) + b_ref[...].astype(F32)).astype(out_ref.dtype)


def add(a, b):
    return call(add_kernel, (a, b), [VM, VM], shape_of(a.shape, a.dtype), VM, name="add", vmem=16)


def join_kernel(sides_ref, own_ref, other_ref, out_ref, sems, *, bit):
    half = own_ref.shape[0]
    side = sides_ref[bit]
    copies = (
        pltpu.make_async_copy(own_ref, out_ref.at[pl.ds(pl.multiple_of(side * half, 16), half)], sems.at[0]),
        pltpu.make_async_copy(other_ref, out_ref.at[pl.ds(pl.multiple_of((1 - side) * half, 16), half)], sems.at[1]),
    )
    for copy in copies:
        copy.start()
    for copy in copies:
        copy.wait()


def join(sides, bit, own, other):
    half, width = own.shape

    def body(*refs):
        join_kernel(*refs, bit=bit)

    return call(
        body,
        (sides, own, other),
        [ANY, ANY],
        shape_of((2 * half, width), BF),
        ANY,
        [pltpu.SemaphoreType.DMA((2,))],
        name="join",
        prefetch=1,
        vmem=8,
    )


def finish_kernel(sides_ref, own_ref, other_ref, *rest):
    out_ref = rest[-1]

    @pl.when(pl.program_id(0) == 0)
    def _():
        out_ref[...] = own_ref[...].astype(F32).reshape(out_ref.shape)

    @pl.when(pl.program_id(0) == 1)
    def _():
        out_ref[...] = other_ref[...].astype(F32).reshape(out_ref.shape)


def finish(sides, bit, own, other, target, shape, start, block):
    half, width = own.shape
    count = half // block
    base = start // block
    spec_own = pl.BlockSpec((block, width), lambda t, i, s: (jnp.where(t == 0, i, count - 1), 0))
    spec_other = pl.BlockSpec((block, width), lambda t, i, s: (jnp.where(t == 0, 0, i), 0))
    out = pl.BlockSpec(
        (block, width), lambda t, i, s: (base + jnp.where(t == 0, s[bit], 1 - s[bit]) * count + i, 0)
    )
    args, specs, aliases = (sides, own, other), [spec_own, spec_other], {}
    if target is not None:
        args, specs, aliases = args + (target,), specs + [ANY], {3: 0}
    return call(
        finish_kernel, args, specs, shape_of(shape, F32), out, grid=(2, count), aliases=aliases, name="finish", prefetch=1
    )


def rows_pair(values):
    rows, width = values.shape
    split = values.reshape(rows // 64, 2, 32, width)
    return jnp.concatenate([split[:, 0], split[:, 1]], axis=-1).reshape(rows // 2, 2 * width)


def finish_up_kernel(sides_ref, own_ref, other_ref, *rest):
    out_ref = rest[-1]

    @pl.when(pl.program_id(0) == 0)
    def _():
        out_ref[...] = rows_pair(own_ref[...].astype(F32))

    @pl.when(pl.program_id(0) == 1)
    def _():
        out_ref[...] = rows_pair(other_ref[...].astype(F32))


def finish_up(sides, bit, own, other, shape, start, block):
    half, width = own.shape
    count = half // block
    base = start // (block // 2)
    spec_own = pl.BlockSpec((block, width), lambda t, i, s: (jnp.where(t == 0, i, count - 1), 0))
    spec_other = pl.BlockSpec((block, width), lambda t, i, s: (jnp.where(t == 0, 0, i), 0))
    out = pl.BlockSpec(
        (block // 2, 2 * width), lambda t, i, s: (base + jnp.where(t == 0, s[bit], 1 - s[bit]) * count + i, 0)
    )
    return call(
        finish_up_kernel,
        (sides, own, other),
        [spec_own, spec_other],
        shape_of(shape, F32),
        out,
        grid=(2, count),
        name="finish_up",
        prefetch=1,
    )


def finish_both(sides, bit, own, other, down_target, up_target, start, block):
    half, width = own.shape
    count = half // block
    base = start // block
    spec = pl.BlockSpec((block, width), lambda i, s: (i, 0))

    def body(sides_ref, own_ref, other_ref, d_in, u_in, d_ref, u_ref):
        @pl.when(sides_ref[bit] == 0)
        def _():
            d_ref[...] = own_ref[...].astype(F32)
            u_ref[...] = rows_pair(other_ref[...].astype(F32))

        @pl.when(sides_ref[bit] == 1)
        def _():
            d_ref[...] = other_ref[...].astype(F32)
            u_ref[...] = rows_pair(own_ref[...].astype(F32))

    return call(
        body,
        (sides, own, other, down_target, up_target),
        [spec, spec, ANY, ANY],
        (shape_of(down_target.shape, F32), shape_of(up_target.shape, F32)),
        (
            pl.BlockSpec((block, width), lambda i, s: (base + i, 0)),
            pl.BlockSpec((block // 2, 2 * width), lambda i, s: (i, 0)),
        ),
        grid=(count,),
        aliases={3: 0, 4: 1},
        name="finish_both",
        prefetch=1,
    )


class Lane:
    def __init__(self, sides, keep, send, order, swap):
        self.sides, self.order, self.swap = sides, order, swap
        self.keep, self.send = keep, send
        self.stage = 0

    def step(self):
        stage, order = self.stage, self.order
        self.stage += 1
        if stage < 2:
            recv = lax.ppermute(self.send, "dp", xor_pairs(1 << order[stage]))
            self.keep, self.send = add_split(self.sides, order[stage + 1], self.keep, recv)
        elif stage == 2:
            self.keep = add(self.keep, lax.ppermute(self.send, "dp", xor_pairs(1 << order[2])))
        elif stage == 3:
            self.keep = add(self.keep, lax.ppermute(self.keep, "dp", xor_pairs(self.swap)))
        elif stage < 6:
            bit = order[6 - stage]
            recv = lax.ppermute(self.keep, "dp", xor_pairs(1 << bit))
            self.keep = join(self.sides, bit, self.keep, recv)
        else:
            self.send = lax.ppermute(self.keep, "dp", xor_pairs(1 << order[0]))


def shards_cube(
    images,
    image_mask,
    cotangent,
    ln1_gain,
    ln1_bias,
    w_qkv,
    qv_bias,
    w_out,
    out_bias,
    ln2_gain,
    ln2_bias,
    w_up,
    up_bias,
    w_down,
    down_bias,
):
    _, rows, width = images.shape
    local = w_qkv.shape[2]
    hidden = w_up.shape[1]
    x = images.reshape(rows, width)
    cot = cotangent.reshape(rows, width)
    index = lax.axis_index("dp")
    sides = jnp.stack([index & 1, (index >> 1) & 1, (index >> 2) & 1]).astype(jnp.int32)
    zeros = jnp.zeros((width,), BF)
    vec = jnp.stack(
        [ln1_gain, ln1_bias, out_bias, ln2_gain, ln2_bias, down_bias, zeros, zeros]
    ).astype(F32)
    bias = jnp.stack([qv_bias[0], jnp.zeros_like(qv_bias[0]), qv_bias[1]]).astype(F32)
    w3 = jnp.transpose(w_qkv, (1, 0, 2))
    swap = [(0, 1), (1, 0)]

    part, q, k, v, mixed, n1, lse = attend(x, vec, bias, w3, w_out)
    part_b = lax.ppermute(part, "tensor", swap)
    ga, bd = grad_act_of(image_mask, cot, w_down)
    act, gp, bu, ka, sa, kb, sb, kc, sc = feed(
        image_mask, sides, x, part, part_b, vec, cot, w_up, up_bias.reshape(1, hidden), ga
    )
    flat = [piece.reshape(-1, width) for piece in (ka, sa, kb, sb, kc, sc)]
    lane_a = Lane(sides, flat[0], flat[1], (0, 1, 2), 8)
    lane_b = Lane(sides, flat[2], flat[3], (1, 2, 0), 8)
    lane_c = Lane(sides, flat[4], flat[5], (2, 0, 1), 8)
    gn2 = back_up(gp, w_up)
    gn2_b = lax.ppermute(gn2, "tensor", swap)
    mlp = down(act, w_down)
    mlp_b = lax.ppermute(mlp, "tensor", swap)
    gr, gm, s2, ko, so = resid_back(image_mask, sides, x, part, part_b, vec, gn2, gn2_b, cot, mixed, w_out)
    lane_o = Lane(sides, ko, so, (1, 2, 0), 8)
    grads = attend_back(q, k, v, mixed, gm, lse)
    bq, kqa, sqa, kqb, sqb = qkv_grad(sides, n1, grads)
    lane_qa = Lane(sides, kqa, sqa, (0, 1, 2), 8)
    lane_qb = Lane(sides, kqb, sqb, (2, 0, 1), 8)
    gn1 = back_in(grads, w3, rows)
    gn1_b = lax.ppermute(gn1, "tensor", swap)
    images_grad, pack = images_back(x, vec, gr, gn1, gn1_b, bd, bu, s2, bq)
    block_output = block_out(x, part, part_b, vec, mlp, mlp_b)

    for _ in range(7):
        for lane in (lane_a, lane_c, lane_b, lane_o, lane_qa, lane_qb):
            lane.step()
    for bit in (1, 2, 4, 8):
        pack = add(pack, lax.ppermute(pack, "dp", xor_pairs(bit)))
    g_down = finish(sides, 0, lane_a.keep, lane_a.send, None, (hidden, width), 0, 128)
    g_up = finish_up(sides, 2, lane_c.keep, lane_c.send, (width, hidden), 384, 128)
    g_down, g_up = finish_both(sides, 1, lane_b.keep, lane_b.send, g_down, g_up, 1280, 128)
    g_out = finish(sides, 1, lane_o.keep, lane_o.send, None, (local, width), 0, 128)
    g_qkv = finish(sides, 0, lane_qa.keep, lane_qa.send, None, (3 * width, local), 0, 256)
    g_qkv = finish(sides, 2, lane_qb.keep, lane_qb.send, g_qkv, (3 * width, local), 3 * width // 2, 256)
    g_qkv = jnp.transpose(g_qkv.reshape(3, width, local), (1, 0, 2))
    after = 6 + hidden // width
    return (
        block_output.reshape(images.shape),
        images_grad.reshape(images.shape),
        pack[0],
        pack[1],
        g_qkv,
        pack[after].reshape(2, local),
        g_out,
        pack[2],
        pack[3],
        pack[4],
        g_up,
        pack[6:after].reshape(hidden),
        g_down,
        pack[5],
    )


def shards(*args):
    images, w_up = args[0], args[11]
    cube = lax.axis_size("dp") == 16 and lax.axis_size("tensor") == 2
    if cube and images.shape[0] == 1 and w_up.shape[1] == 2 * w_up.shape[0]:
        return shards_cube(*args)
    return shards_any(*args)


def solution(mesh):
    in_specs = (
        P("dp", None, None),
        P("dp"),
        P("dp", None, None),
        P(),
        P(),
        P(None, None, "tensor"),
        P(None, "tensor"),
        P("tensor", None),
        P(),
        P(),
        P(),
        P(None, "tensor"),
        P("tensor"),
        P("tensor", None),
        P(),
    )
    out_specs = (
        P("dp", None, None),
        P("dp", None, None),
        P(),
        P(),
        P(None, None, "tensor"),
        P(None, "tensor"),
        P("tensor", None),
        P(),
        P(),
        P(),
        P(None, "tensor"),
        P("tensor"),
        P("tensor", None),
        P(),
    )
    return jax.shard_map(shards, mesh=mesh, in_specs=in_specs, out_specs=out_specs, check_vma=False)
```

```python
import jax
import jax.numpy as jnp
from jax import lax
from jax.experimental import pallas as pl
from jax.experimental.pallas import tpu as pltpu
from jax.sharding import PartitionSpec as P

HD = 64
VALID = 577
EPS = 1e-06
BF = jnp.bfloat16
F32 = jnp.float32


def stats(values):
    mean = jnp.mean(values, axis=-1, keepdims=True)
    centred = values - mean
    spread = jnp.mean(centred * centred, axis=-1, keepdims=True)
    inv = lax.rsqrt(spread + EPS)
    return centred * inv, inv


def norm_back(unit, inv, gain, grad):
    scaled = grad * gain
    mean_a = jnp.mean(scaled, axis=-1, keepdims=True)
    mean_b = jnp.mean(scaled * unit, axis=-1, keepdims=True)
    return inv * (scaled - mean_a - unit * mean_b)


def inner_rows(left, right):
    return lax.dot_general(
        left, right, (((0,), (0,)), ((), ())), preferred_element_type=F32
    )


def times_back(left, weight):
    return lax.dot_general(
        left, weight, (((1,), (1,)), ((), ())), preferred_element_type=F32
    )


def score_block(query, keyset):
    raw = jnp.einsum("qhd,khd->hqk", query, keyset, preferred_element_type=F32)
    live = jnp.arange(raw.shape[-1]) < VALID
    return jnp.where(live, raw * HD ** (-0.5), -1e30)


def attend_forward(query, keyset, valueset):
    scores = score_block(query, keyset)
    peak = jnp.max(scores, axis=-1, keepdims=True)
    expo = jnp.exp(scores - peak)
    total = jnp.sum(expo, axis=-1, keepdims=True)
    probs = (expo / total).astype(BF)
    mixed = jnp.einsum("hqk,khd->qhd", probs, valueset, preferred_element_type=F32)
    return mixed.astype(BF), peak[..., 0] + jnp.log(total[..., 0])


def attend_backward(query, keyset, valueset, grad_mixed, logsum):
    scores = score_block(query, keyset)
    probs = jnp.exp(scores - logsum[..., None])
    grad_probs = jnp.einsum("qhd,khd->hqk", grad_mixed, valueset, preferred_element_type=F32)
    delta = jnp.sum(probs * grad_probs, axis=-1, keepdims=True)
    grad_scores = (probs * (grad_probs - delta) * HD ** (-0.5)).astype(BF)
    low_probs = probs.astype(BF)
    grad_value = jnp.einsum("hqk,qhd->khd", low_probs, grad_mixed, preferred_element_type=F32)
    grad_query = jnp.einsum("hqk,khd->qhd", grad_scores, keyset, preferred_element_type=F32)
    grad_key = jnp.einsum("hqk,qhd->khd", grad_scores, query, preferred_element_type=F32)
    return jnp.stack([grad_query, grad_key, grad_value], axis=1).astype(BF)


def swap_sum(part):
    if lax.axis_size("tensor") == 2:
        other = lax.ppermute(part, "tensor", [(0, 1), (1, 0)])
        return part.astype(F32) + other.astype(F32)
    return lax.psum(part.astype(F32), "tensor")


def xor_pairs(bit):
    return [(i, i ^ bit) for i in range(lax.axis_size("dp"))]


def bits_of():
    count = lax.axis_size("dp")
    bits = []
    while count > 1:
        if count % 2:
            raise ValueError("dp")
        bits.append(1 << len(bits))
        count //= 2
    return bits


def sum_small(vector):
    for bit in bits_of():
        vector = vector + lax.ppermute(vector, "dp", xor_pairs(bit))
    return vector


def cut_thirds(rows, turn):
    unit = 128
    whole = rows // unit
    base = whole // 3
    counts = [base + (1 if (i - turn) % 3 < whole % 3 else 0) for i in range(3)]
    return [c * unit for c in counts]


def sum_over_dp(matrix, turn):
    bits = bits_of()
    index = lax.axis_index("dp")
    halving = bits[: min(3, len(bits) - 1)]
    swaps = bits[len(halving) :]
    pieces, orders, start = [], [], 0
    for lane, rows in enumerate(cut_thirds(matrix.shape[0], turn)):
        if rows == 0:
            continue
        pieces.append(lax.slice_in_dim(matrix, start, start + rows, axis=0))
        turned = lane % len(halving)
        orders.append(halving[turned:] + halving[:turned])
        start += rows
    for step in range(len(halving)):
        for lane in range(len(pieces)):
            piece, bit = pieces[lane], orders[lane][step]
            half = piece.shape[0] // 2
            side = (index // bit) & 1
            kept = lax.dynamic_slice_in_dim(piece, side * half, half, 0)
            sent = lax.dynamic_slice_in_dim(piece, (1 - side) * half, half, 0)
            pieces[lane] = kept + lax.ppermute(sent, "dp", xor_pairs(bit))
    for bit in swaps:
        for lane in range(len(pieces)):
            pieces[lane] = pieces[lane] + lax.ppermute(pieces[lane], "dp", xor_pairs(bit))
    for step in reversed(range(len(halving))):
        for lane in range(len(pieces)):
            piece, bit = pieces[lane], orders[lane][step]
            other = lax.ppermute(piece, "dp", xor_pairs(bit))
            side = (index // bit) & 1
            pieces[lane] = jnp.where(
                side == 0,
                jnp.concatenate([piece, other], axis=0),
                jnp.concatenate([other, piece], axis=0),
            )
    return jnp.concatenate(pieces, axis=0).astype(F32)


def shards_any(
    images,
    image_mask,
    cotangent,
    ln1_gain,
    ln1_bias,
    w_qkv,
    qv_bias,
    w_out,
    out_bias,
    ln2_gain,
    ln2_bias,
    w_up,
    up_bias,
    w_down,
    down_bias,
):
    count, seq, width = images.shape
    rows = count * seq
    local = w_qkv.shape[2]
    heads = local // HD
    gain1 = ln1_gain.astype(F32)
    gain2 = ln2_gain.astype(F32)
    inputs = images.reshape(rows, width).astype(F32)
    keep = image_mask.astype(BF)[:, None, None]
    grad_out = (cotangent * keep).reshape(rows, width)
    w_qkv_flat = w_qkv.reshape(width, 3 * local)
    bias_row = jnp.concatenate([qv_bias[0], jnp.zeros_like(qv_bias[0]), qv_bias[1]]).astype(F32)

    unit1, inv1 = stats(inputs)
    normed1 = (unit1 * gain1 + ln1_bias.astype(F32)).astype(BF)
    qkv = (jnp.dot(normed1, w_qkv_flat, preferred_element_type=F32) + bias_row).astype(BF)
    split = qkv.reshape(count, seq, 3, heads, HD)
    attended = [attend_forward(split[i, :, 0], split[i, :, 1], split[i, :, 2]) for i in range(count)]
    mixed = jnp.concatenate([a[0] for a in attended], axis=0).reshape(rows, local)
    attn = swap_sum(jnp.dot(mixed, w_out, preferred_element_type=F32).astype(BF))
    grad_act = times_back(grad_out, w_down)
    resid = inputs + attn + out_bias.astype(F32)
    unit2, inv2 = stats(resid)
    normed2 = (unit2 * gain2 + ln2_bias.astype(F32)).astype(BF)
    pre = jnp.dot(normed2, w_up, preferred_element_type=F32) + up_bias.astype(F32)
    cdf = 0.5 * (1.0 + lax.erf(pre * (0.5**0.5)))
    act = (pre * cdf).astype(BF)
    slope = cdf + pre * jnp.exp(-0.5 * pre * pre) * ((0.5 / jnp.pi) ** 0.5)
    grad_pre = (grad_act * slope).astype(BF)
    grad_wdown = inner_rows(act, grad_out).astype(BF)
    summed_wdown = sum_over_dp(grad_wdown, 0)
    grad_wup = inner_rows(normed2, grad_pre).astype(BF)
    summed_wup = sum_over_dp(grad_wup, 1)
    grad_normed2 = swap_sum(times_back(grad_pre, w_up).astype(BF))
    mlp = swap_sum(jnp.dot(act, w_down, preferred_element_type=F32).astype(BF))
    block_output = (resid + mlp + down_bias.astype(F32)).astype(BF).reshape(images.shape)
    grad_resid = grad_out.astype(F32) + norm_back(unit2, inv2, gain2, grad_normed2)
    resid_low = grad_resid.astype(BF)
    grad_wout = inner_rows(mixed, resid_low).astype(BF)
    summed_wout = sum_over_dp(grad_wout, 2)
    grad_mixed = times_back(resid_low, w_out).astype(BF).reshape(count, seq, heads, HD)
    grad_qkv = jnp.concatenate(
        [
            attend_backward(split[i, :, 0], split[i, :, 1], split[i, :, 2], grad_mixed[i], attended[i][1])
            for i in range(count)
        ],
        axis=0,
    ).reshape(rows, 3 * local)
    grad_wqkv = inner_rows(normed1, grad_qkv).astype(BF)
    summed_wqkv = sum_over_dp(grad_wqkv, 0).reshape(width, 3, local)
    bias_sums = jnp.sum(grad_qkv.astype(F32), axis=0)
    grad_normed1 = swap_sum(times_back(grad_qkv, w_qkv_flat).astype(BF))
    images_grad = (
        (grad_resid + norm_back(unit1, inv1, gain1, grad_normed1)).astype(BF).reshape(images.shape)
    )

    small = [
        jnp.sum(grad_normed1 * unit1, axis=0),
        jnp.sum(grad_normed1, axis=0),
        jnp.sum(grad_resid, axis=0),
        jnp.sum(grad_normed2 * unit2, axis=0),
        jnp.sum(grad_normed2, axis=0),
        jnp.sum(grad_out.astype(F32), axis=0),
        jnp.sum(grad_pre.astype(F32), axis=0),
        bias_sums[:local],
        bias_sums[2 * local :],
    ]
    flat = jnp.concatenate(small)
    length = flat.shape[0]
    padded = -(-length // 1024) * 1024
    flat = sum_small(jnp.pad(flat, (0, padded - length)).reshape(padded // 128, 128)).reshape(-1)
    out, at = [], 0
    for part in small:
        out.append(flat[at : at + part.shape[0]])
        at += part.shape[0]
    return (
        block_output,
        images_grad,
        out[0],
        out[1],
        summed_wqkv,
        jnp.stack([out[7], out[8]]),
        summed_wout,
        out[2],
        out[3],
        out[4],
        summed_wup,
        out[6],
        summed_wdown,
        out[5],
    )


ANY = pl.BlockSpec(memory_space=pl.ANY)
HBM = pl.BlockSpec(memory_space=pltpu.HBM)
VM = pl.BlockSpec(memory_space=pltpu.VMEM)
MIB = 1024 * 1024


def shape_of(shape, dtype):
    return jax.ShapeDtypeStruct(shape, dtype)


def nn(left, right):
    return jnp.dot(left, right, preferred_element_type=F32)


def normal_unit(values):
    mean = jnp.mean(values, axis=-1, keepdims=True)
    centred = values - mean
    spread = jnp.mean(centred * centred, axis=-1, keepdims=True)
    inv = lax.rsqrt(spread + EPS)
    return centred * inv, inv


def row_of(ref):
    return ref[...].astype(F32).reshape(1, ref.shape[0])


def side_of(where_ref, bit):
    return (where_ref[0] >> bit) & 1


class Chain:
    def __init__(self):
        self.last = None

    def __call__(
        self, body, args, in_specs, outs, out_specs, scratch=(), grid=(), vmem=40, aliases=None, name=None, prefetch=0, cost=0.001
    ):
        args, in_specs, run = list(args), list(in_specs), body
        if self.last is not None:
            spot = len(args)

            def run(*refs):
                body(*refs[:spot], *refs[spot + 1 :])

            args.append(self.last)
            in_specs.append(ANY)
        spec = pltpu.PrefetchScalarGridSpec(
            num_scalar_prefetch=prefetch,
            grid=grid,
            in_specs=in_specs,
            out_specs=out_specs,
            scratch_shapes=list(scratch),
        )
        made = pl.pallas_call(
            run,
            out_shape=outs,
            grid_spec=spec,
            input_output_aliases=aliases or {},
            compiler_params=pltpu.CompilerParams(vmem_limit_bytes=vmem * MIB),
            cost_estimate=pl.CostEstimate(flops=0, bytes_accessed=int(cost * 3e6), transcendentals=0),
            name=name,
        )(*args)
        self.last = made[0] if isinstance(made, (tuple, list)) else made
        return made


def row_chunks(rows):
    units, parts = rows // 16, 4
    cuts = [16 * (units * i // parts) for i in range(parts)] + [rows]
    return [(cuts[i], cuts[i + 1] - cuts[i]) for i in range(parts)]


def lane_halves():
    return lax.broadcasted_iota(jnp.int32, (1, 2 * HD), 1) < HD


def key_mask(length):
    return jnp.where(lax.broadcasted_iota(jnp.int32, (1, length), 1) < VALID, 0.0, -1e30)


def attend_kernel(
    x_ref, g_ref, s_ref, b_ref, w_ref, wo_ref,
    part_ref, q_ref, k_ref, v_ref, mixed_ref, n1_ref, lse_ref, w_buf, wo_buf, sems,
):
    rows, width = x_ref.shape
    padded, local = q_ref.shape
    copies = [pltpu.make_async_copy(w_ref.at[c], w_buf.at[c], sems.at[c]) for c in range(3)]
    copies.append(pltpu.make_async_copy(wo_ref, wo_buf, sems.at[3]))
    for copy in copies:
        copy.start()
    unit, _ = normal_unit(x_ref[...].astype(F32))
    normed = unit * row_of(g_ref) + row_of(s_ref)
    n1_ref[...] = jnp.concatenate([normed, jnp.zeros((padded - rows, width), F32)], axis=0).astype(BF)
    lse_ref[...] = jnp.zeros(lse_ref.shape, F32)
    live = lax.broadcasted_iota(jnp.int32, (padded, 1), 0) < rows
    for c, (ref, scale) in enumerate(((q_ref, HD ** (-0.5)), (k_ref, 1.0), (v_ref, 1.0))):
        copies[c].wait()
        for at in range(0, local, 256):
            made = nn(n1_ref[...], w_buf[c, :, at : at + 256])
            if c != 1:
                made = made + b_ref[c // 2 : c // 2 + 1, at : at + 256].astype(F32)
            made = jnp.where(live, made, 0.0).astype(BF)
            ref[:, at : at + 256] = made * jnp.asarray(scale, BF)
    mask = key_mask(padded)
    first = lane_halves()
    lane = lax.broadcasted_iota(jnp.int32, (1, 128), 1)

    def pair(p, carry):
        cols = pl.ds(pl.multiple_of(p * 128, 128), 128)
        keys, vals = k_ref[:, cols], v_ref[:, cols]
        zero = jnp.zeros_like(keys)
        own = (jnp.where(first, keys, zero), jnp.where(first, zero, keys))
        for at, size in row_chunks(padded):
            query = q_ref[at : at + size, cols]
            outs = []
            logs = lse_ref[at : at + size, :]
            for h in range(2):
                scores = times_back(query, own[h]) + mask
                peak = jnp.max(scores, axis=-1, keepdims=True)
                expo = jnp.exp(scores - peak)
                total = jnp.sum(expo, axis=-1, keepdims=True)
                probs = (expo * (1.0 / total)).astype(BF)
                outs.append(nn(probs, vals))
                logs = jnp.where(lane == 2 * p + h, peak + jnp.log(total), logs)
            lse_ref[at : at + size, :] = logs
            mixed_ref[at : at + size, cols] = jnp.where(first, outs[0], outs[1]).astype(BF)
        return carry

    lax.fori_loop(0, local // 128, pair, 0)
    copies[3].wait()
    for at in range(0, width, 256):
        made = nn(mixed_ref[...], wo_buf[:, at : at + 256])
        part_ref[:, at : at + 256] = made[:rows].astype(BF)


def attend(chain, x, gain, shift, bias, w3, w_out):
    rows, width = x.shape
    local = w3.shape[2]
    padded = -(-rows // 16) * 16
    wide = shape_of((padded, local), BF)
    outs = (
        shape_of((rows, width), BF),
        wide,
        wide,
        wide,
        wide,
        shape_of((padded, width), BF),
        shape_of((padded, 128), F32),
    )
    return chain(
        attend_kernel,
        (x, gain, shift, bias, w3, w_out),
        [VM, VM, VM, VM, HBM, HBM],
        outs,
        (VM,) * 7,
        [pltpu.VMEM((3, width, local), BF), pltpu.VMEM((local, width), BF), pltpu.SemaphoreType.DMA((4,))],
        name="attend",
        vmem=60,
    )


def grad_act_of(chain, mask, cot, w_down):
    rows, width = cot.shape
    hidden = w_down.shape[0]
    tile = hidden // 4

    def body(mask_ref, cot_ref, w_ref, ga_ref, go_ref, bd_ref, w_buf, sems):
        copies = [pltpu.make_async_copy(w_ref.at[pl.ds(i * tile, tile)], w_buf.at[i], sems.at[i]) for i in range(4)]
        for copy in copies:
            copy.start()
        masked = cot_ref[...].astype(F32) * mask_ref[0].astype(F32)
        go_ref[...] = masked.astype(BF)
        bd_ref[...] = jnp.sum(masked, axis=0, keepdims=True)
        for i in range(4):
            copies[i].wait()
            ga_ref[:, i * tile : (i + 1) * tile] = times_back(go_ref[...], w_buf[i]).astype(BF)

    return chain(
        body,
        (mask, cot, w_down),
        [VM, HBM],
        (shape_of((rows, hidden), BF), shape_of((rows, width), BF), shape_of((1, width), F32)),
        (VM,) * 3,
        [pltpu.VMEM((4, tile, width), BF), pltpu.SemaphoreType.DMA((4,))],
        name="grad_act",
        prefetch=1,
        vmem=60,
    )


def gelu_pair(pre):
    bell = jnp.exp(-0.5 * pre * pre)
    near = 1.0 / (1.0 + (0.3275911 * 0.5**0.5) * jnp.abs(pre))
    poly = near * (
        0.254829592 + near * (-0.284496736 + near * (1.421413741 + near * (-1.453152027 + near * 1.061405429)))
    )
    tail = 0.5 * poly * bell
    cdf = jnp.where(pre < 0, tail, 1.0 - tail)
    return cdf, cdf + pre * bell * ((0.5 / jnp.pi) ** 0.5)


def feed_kernel(
    where_ref, x_ref, pa_ref, pb_ref, ob_ref, g_ref, s_ref, go_ref, wu_ref, ub_ref, ga_ref,
    act_ref, gp_ref, n2_ref, bu_ref, k0_ref, s0_ref, k1_ref, s1_ref, last, bias, grads, sems, *, bits,
):
    step = pl.program_id(0)
    steps = pl.num_programs(0) - 1
    tile = wu_ref.shape[1]

    @pl.when(step == 0)
    def _():
        resid = x_ref[...].astype(F32) + (pa_ref[...].astype(F32) + pb_ref[...].astype(F32)) + row_of(ob_ref)
        unit, _ = normal_unit(resid)
        n2_ref[...] = (unit * row_of(g_ref) + row_of(s_ref)).astype(BF)
        bias[...] = row_of(ub_ref)
        last[...] = jnp.zeros(last.shape, BF)

    now = jnp.minimum(step, steps - 1)
    before = jnp.maximum(step - 1, 0)
    made = inner_rows(last[...], go_ref[...]).astype(BF)
    grads[pl.ds(pl.multiple_of(before * tile, tile), tile), :] = made
    pre = nn(n2_ref[...], wu_ref[...]) + bias[:, pl.ds(pl.multiple_of(now * tile, tile), tile)]
    cdf, slope = gelu_pair(pre)
    act = (pre * cdf).astype(BF)
    grad_pre = (ga_ref[...].astype(F32) * slope).astype(BF)
    act_ref[...] = act
    last[...] = act
    gp_ref[...] = grad_pre
    bu_ref[...] = jnp.sum(grad_pre.astype(F32), axis=0, keepdims=True)

    def pieces(lane, keep, send):
        half = keep.shape[0]
        side = side_of(where_ref, bits[lane])
        own = pl.multiple_of((2 * lane + side) * half, half)
        other = pl.multiple_of((2 * lane + 1 - side) * half, half)
        return (
            pltpu.make_async_copy(grads.at[pl.ds(other, half)], send, sems.at[2 * lane]),
            pltpu.make_async_copy(grads.at[pl.ds(own, half)], keep, sems.at[2 * lane + 1]),
        )

    early = pieces(0, k0_ref, s0_ref)

    @pl.when(step == 2 * k0_ref.shape[0] // tile)
    def _():
        for copy in early:
            copy.start()

    @pl.when(step == steps)
    def _():
        late = pieces(1, k1_ref, s1_ref)
        for copy in late:
            copy.start()
        for copy in early + late:
            copy.wait()


def feed(chain, where, bits, x, pa, pb, out_bias, gain, shift, go, w_up, up_bias, ga):
    rows, width = x.shape
    hidden = w_up.shape[1]
    tile = 256
    steps = hidden // tile

    def body(*refs):
        feed_kernel(*refs, bits=bits)

    fixed = pl.BlockSpec((rows, width), lambda j, w: (0, 0))
    line = pl.BlockSpec((width,), lambda j, w: (0,))
    cols = pl.BlockSpec((rows, tile), lambda j, w: (0, jnp.minimum(j, steps - 1)))
    piece = shape_of((hidden // 4, width), BF)
    return chain(
        body,
        (where, x, pa, pb, out_bias, gain, shift, go, w_up, up_bias, ga),
        [
            fixed,
            fixed,
            fixed,
            line,
            line,
            line,
            fixed,
            pl.BlockSpec((width, tile), lambda j, w: (0, jnp.minimum(j, steps - 1))),
            pl.BlockSpec((hidden,), lambda j, w: (0,)),
            cols,
        ],
        (
            shape_of((rows, hidden), BF),
            shape_of((rows, hidden), BF),
            shape_of((rows, width), BF),
            shape_of((1, hidden), F32),
            piece,
            piece,
            piece,
            piece,
        ),
        (cols, cols, fixed, pl.BlockSpec((1, tile), lambda j, w: (0, jnp.minimum(j, steps - 1)))) + (ANY,) * 4,
        [
            pltpu.VMEM((rows, tile), BF),
            pltpu.VMEM((1, hidden), F32),
            pltpu.VMEM((hidden, width), BF),
            pltpu.SemaphoreType.DMA((4,)),
        ],
        (steps + 1,),
        name="feed",
        vmem=60,
        prefetch=1,
    )


def weight_grad(chain, where, left, right, pieces, flip, size):
    outs = tuple(shape_of((size, piece[3]), BF) for piece in pieces)

    def body(where_ref, left_ref, right_ref, *out_refs):
        for (first, bit, start, count), out_ref in zip(pieces, out_refs, strict=True):
            half = first + (side_of(where_ref, bit) ^ flip)
            cols = left_ref[:, pl.ds(pl.multiple_of(half * size, size), size)]
            for at in range(0, count, 512):
                made = inner_rows(cols, right_ref[:, start + at : start + at + 512])
                out_ref[:, at : at + 512] = made.astype(BF)

    return chain(
        body,
        (where, left, right),
        [VM, VM],
        outs,
        (VM,) * len(outs),
        name="weight_grad",
        prefetch=1,
    )


def qkv_grad(chain, where, n1, grads, bits, flip):
    width = n1.shape[1]
    local = grads.shape[1] // 3
    size = width // 4

    def body(where_ref, n1_ref, g_ref, *out_refs):
        for lane in range(2):
            half = 2 * lane + (side_of(where_ref, bits[lane]) ^ flip)
            for i in range(3):
                block = 3 * half + i
                rows = pl.ds(pl.multiple_of((block & 3) * size, size), size)
                cols = pl.ds(pl.multiple_of((block >> 2) * local, local), local)
                made = inner_rows(n1_ref[:, rows], g_ref[:, cols])
                out_refs[lane][i * size : (i + 1) * size, :] = made.astype(BF)

    return chain(
        body,
        (where, n1, grads),
        [VM, VM],
        (shape_of((3 * size, local), BF),) * 2,
        (VM,) * 2,
        name="qkv_grad",
        prefetch=1,
    )


TILES = 4


def paired(own, other):
    return own[...].astype(F32) + other[...].astype(F32)


def back_up(chain, gp, w_up):
    rows, hidden = gp.shape
    width = w_up.shape[0]
    size = width // TILES

    def body(gp_ref, w_ref, *rest):
        out_ref, w_buf, sems = rest
        copies = [
            pltpu.make_async_copy(w_ref.at[pl.ds(i * size, size)], w_buf.at[i], sems.at[i]) for i in range(TILES)
        ]
        for copy in copies:
            copy.start()
        for i in range(TILES):
            copies[i].wait()
            out_ref[:, i * size : (i + 1) * size] = times_back(gp_ref[...], w_buf[i]).astype(BF)

    return chain(
        body,
        (gp, w_up),
        [VM, HBM],
        shape_of((rows, width), BF),
        VM,
        [pltpu.VMEM((TILES, size, hidden), BF), pltpu.SemaphoreType.DMA((TILES,))],
        name="back_up",
    )


def down(chain, act, w_down):
    rows, hidden = act.shape
    width = w_down.shape[1]
    size = width // TILES
    deep = hidden // TILES

    def body(act_ref, w_ref, *rest):
        out_ref, w_buf, sems = rest
        copies = [
            pltpu.make_async_copy(w_ref.at[pl.ds(i * deep, deep)], w_buf.at[pl.ds(i * deep, deep)], sems.at[i])
            for i in range(TILES)
        ]
        for copy in copies:
            copy.start()
        for copy in copies:
            copy.wait()
        for i in range(TILES):
            out_ref[:, i * size : (i + 1) * size] = nn(act_ref[...], w_buf[:, i * size : (i + 1) * size]).astype(BF)

    return chain(
        body,
        (act, w_down),
        [VM, HBM],
        shape_of((rows, width), BF),
        VM,
        [pltpu.VMEM((hidden, width), BF), pltpu.SemaphoreType.DMA((TILES,))],
        name="down",
    )


def resid_back_kernel(
    where_ref, x_ref, pa_ref, pb_ref, ob_ref, g_ref, ga_ref, gb_ref, go_ref, mixed_ref, wo_ref,
    gr_ref, gm_ref, sums_ref, keep_ref, send_ref, low, grads, sems, *, bit,
):
    rows, width = x_ref.shape
    padded, local = mixed_ref.shape
    resid = x_ref[...].astype(F32) + (pa_ref[...].astype(F32) + pb_ref[...].astype(F32)) + row_of(ob_ref)
    unit, inv = normal_unit(resid)
    grad = paired(ga_ref, gb_ref)
    total = go_ref[...].astype(F32) + norm_back(unit, inv, row_of(g_ref), grad)
    gr_ref[...] = total
    low[...] = jnp.concatenate([total, jnp.zeros((padded - rows, width), F32)], axis=0).astype(BF)
    sums_ref[...] = jnp.concatenate(
        [
            jnp.sum(total, axis=0, keepdims=True),
            jnp.sum(grad * unit, axis=0, keepdims=True),
            jnp.sum(grad, axis=0, keepdims=True),
            jnp.zeros((5, width), F32),
        ],
        axis=0,
    )
    for at in range(0, width, 256):
        grads[:, at : at + 256] = inner_rows(mixed_ref[...], low[:, at : at + 256]).astype(BF)
    half, side = local // 2, side_of(where_ref, bit)
    copies = (
        pltpu.make_async_copy(grads.at[pl.ds(pl.multiple_of((1 - side) * half, half), half)], send_ref, sems.at[0]),
        pltpu.make_async_copy(grads.at[pl.ds(pl.multiple_of(side * half, half), half)], keep_ref, sems.at[1]),
    )
    for copy in copies:
        copy.start()
    for at in range(0, local, 256):
        gm_ref[:, at : at + 256] = times_back(low[...], wo_ref[at : at + 256, :]).astype(BF)
    for copy in copies:
        copy.wait()


def resid_back(chain, where, bit, x, pa, pb, out_bias, gain, ga, gb, go, mixed, w_out):
    rows, width = x.shape
    padded, local = mixed.shape

    def body(*refs):
        resid_back_kernel(*refs, bit=bit)

    return chain(
        body,
        (where, x, pa, pb, out_bias, gain, ga, gb, go, mixed, w_out),
        [VM] * 10,
        (
            shape_of((rows, width), F32),
            shape_of((padded, local), BF),
            shape_of((8, width), F32),
            shape_of((local // 2, width), BF),
            shape_of((local // 2, width), BF),
        ),
        (VM, VM, VM, ANY, ANY),
        [pltpu.VMEM((padded, width), BF), pltpu.VMEM((local, width), BF), pltpu.SemaphoreType.DMA((2,))],
        name="resid_back",
        prefetch=1,
    )


def attend_back_kernel(q_ref, k_ref, v_ref, mixed_ref, gm_ref, lse_ref, out_ref, bias_ref, probs_s, slopes_s):
    padded, local = q_ref.shape
    mask = key_mask(padded)
    first = lane_halves()
    lane = lax.broadcasted_iota(jnp.int32, (1, 128), 1)

    def pair(p, carry):
        cols = pl.ds(pl.multiple_of(p * 128, 128), 128)
        keys, vals = k_ref[:, cols], v_ref[:, cols]
        zero = jnp.zeros_like(keys)
        own_k = (jnp.where(first, keys, zero), jnp.where(first, zero, keys))
        own_v = (jnp.where(first, vals, zero), jnp.where(first, zero, vals))
        for at, size in row_chunks(padded):
            query = q_ref[at : at + size, cols]
            grad = gm_ref[at : at + size, cols]
            both = grad.astype(F32) * mixed_ref[at : at + size, cols].astype(F32)
            logs = lse_ref[at : at + size, :]
            outs = []
            for h in range(2):
                own_lanes = first if h == 0 else jnp.logical_not(first)
                delta = jnp.sum(jnp.where(own_lanes, both, 0.0), axis=-1, keepdims=True)
                log = jnp.sum(jnp.where(lane == 2 * p + h, logs, 0.0), axis=-1, keepdims=True)
                probs = jnp.exp(times_back(query, own_k[h]) + mask - log)
                slope = (probs * (times_back(grad, own_v[h]) - delta)).astype(BF)
                probs_s[h, at : at + size, :] = probs.astype(BF)
                slopes_s[h, at : at + size, :] = slope
                outs.append(nn(slope, keys))
            out_ref[at : at + size, cols] = (jnp.where(first, outs[0], outs[1]) * HD ** (-0.5)).astype(BF)
        grad_t = gm_ref[:, cols].astype(F32).T.astype(BF)
        query_t = q_ref[:, cols].astype(F32).T.astype(BF)
        grad_k = [nn(query_t[HD * h : HD * h + HD], slopes_s[h]) for h in range(2)]
        grad_v = [nn(grad_t[HD * h : HD * h + HD], probs_s[h]) for h in range(2)]
        cols_k = pl.ds(pl.multiple_of(local + p * 128, 128), 128)
        cols_v = pl.ds(pl.multiple_of(2 * local + p * 128, 128), 128)
        out_ref[:, cols_k] = jnp.concatenate(grad_k, axis=0).T.astype(BF)
        out_ref[:, cols_v] = jnp.concatenate(grad_v, axis=0).T.astype(BF)
        return carry

    lax.fori_loop(0, local // 128, pair, 0)
    bias_ref[...] = jnp.sum(out_ref[...].astype(F32), axis=0, keepdims=True)


def attend_back(chain, q, k, v, mixed, gm, lse):
    padded, local = q.shape
    return chain(
        attend_back_kernel,
        (q, k, v, mixed, gm, lse),
        [VM] * 6,
        (shape_of((padded, 3 * local), BF), shape_of((1, 3 * local), F32)),
        (VM, VM),
        [pltpu.VMEM((2, padded, padded), BF), pltpu.VMEM((2, padded, padded), BF)],
        name="attend_back",
    )


def back_in(chain, grads, w3, rows):
    _, width, local = w3.shape
    size = width // TILES

    def body(g_ref, w_ref, *rest):
        out_ref, w_buf, sems = rest
        copies = [
            pltpu.make_async_copy(w_ref.at[:, pl.ds(i * size, size)], w_buf.at[i], sems.at[i]) for i in range(TILES)
        ]
        for copy in copies:
            copy.start()
        for i in range(TILES):
            copies[i].wait()
            total = times_back(g_ref[:, :local], w_buf[i, 0])
            for c in range(1, 3):
                total += times_back(g_ref[:, c * local : (c + 1) * local], w_buf[i, c])
            out_ref[:, i * size : (i + 1) * size] = total[:rows].astype(BF)

    return chain(
        body,
        (grads, w3),
        [VM, HBM],
        shape_of((rows, width), BF),
        VM,
        [pltpu.VMEM((TILES, 3, size, local), BF), pltpu.SemaphoreType.DMA((TILES,))],
        name="back_in",
    )


def images_back_kernel(x_ref, g_ref, gr_ref, ga_ref, gb_ref, bd_ref, bu_ref, s2_ref, bq_ref, out_ref, pack_ref):
    unit, inv = normal_unit(x_ref[...].astype(F32))
    grad = paired(ga_ref, gb_ref)
    out_ref[...] = (gr_ref[...] + norm_back(unit, inv, row_of(g_ref), grad)).astype(BF)
    width = x_ref.shape[1]
    hidden = bu_ref.shape[1]
    local = bq_ref.shape[1] // 3
    pack_ref[0:1, :] = jnp.sum(grad * unit, axis=0, keepdims=True)
    pack_ref[1:2, :] = jnp.sum(grad, axis=0, keepdims=True)
    pack_ref[2:5, :] = s2_ref[0:3, :]
    pack_ref[5:6, :] = bd_ref[...]
    for i in range(hidden // width):
        pack_ref[6 + i : 7 + i, :] = bu_ref[:, i * width : (i + 1) * width]
    after = 6 + hidden // width
    pack_ref[after : after + 1, :local] = bq_ref[:, :local]
    pack_ref[after : after + 1, local:] = bq_ref[:, 2 * local :]
    pack_ref[after + 1 :, :] = jnp.zeros((pack_ref.shape[0] - after - 1, width), F32)


def images_back(chain, x, gain, gr, ga, gb, bd, bu, s2, bq):
    return chain(
        images_back_kernel,
        (x, gain, gr, ga, gb, bd, bu, s2, bq),
        [VM] * 9,
        (shape_of(x.shape, BF), shape_of((16, x.shape[1]), F32)),
        (VM, VM),
        name="images_back",
    )


def block_out_kernel(x_ref, pa_ref, pb_ref, ob_ref, ma_ref, mb_ref, db_ref, out_ref):
    resid = x_ref[...].astype(F32) + (pa_ref[...].astype(F32) + pb_ref[...].astype(F32)) + row_of(ob_ref)
    out_ref[...] = (resid + paired(ma_ref, mb_ref) + row_of(db_ref)).astype(BF)


def block_out(chain, x, pa, pb, out_bias, ma, mb, down_bias):
    return chain(
        block_out_kernel,
        (x, pa, pb, out_bias, ma, mb, down_bias),
        [VM] * 7,
        shape_of(x.shape, BF), VM, name="block_out"
    )


def add_split_kernel(where_ref, k0_ref, k1_ref, r0_ref, r1_ref, send_ref, keep_ref):
    keep_ref[...] = (k0_ref[...].astype(F32) + r0_ref[...].astype(F32)).astype(BF)
    send_ref[...] = (k1_ref[...].astype(F32) + r1_ref[...].astype(F32)).astype(BF)


def add_split(chain, where, bit, keep, recv):
    rows, width = keep.shape
    half = rows // 2
    block = (half, width)
    own = pl.BlockSpec(block, lambda i, w: ((w[0] >> bit) & 1, 0))
    other = pl.BlockSpec(block, lambda i, w: (1 - ((w[0] >> bit) & 1), 0))
    out = pl.BlockSpec(block, lambda i, w: (0, 0))
    return chain(
        add_split_kernel,
        (where, keep, keep, recv, recv),
        [own, other, own, other],
        (shape_of((half, width), BF),) * 2,
        (out, out),
        grid=(1,),
        name="add_split",
        prefetch=1,
        vmem=16,
    )


def add_kernel(a_ref, b_ref, out_ref):
    out_ref[...] = (a_ref[...].astype(F32) + b_ref[...].astype(F32)).astype(out_ref.dtype)


def add(chain, a, b):
    return chain(add_kernel, (a, b), [VM, VM], shape_of(a.shape, a.dtype), VM, name="add", vmem=16)


def join(chain, where, bit, own, other):
    half, width = own.shape

    def body(where_ref, own_ref, other_ref, out_ref):
        side = side_of(where_ref, bit)
        out_ref[pl.ds(pl.multiple_of(side * half, 16), half), :] = own_ref[...]
        out_ref[pl.ds(pl.multiple_of((1 - side) * half, 16), half), :] = other_ref[...]

    return chain(
        body,
        (where, own, other),
        [VM, VM],
        shape_of((2 * half, width), BF),
        VM,
        name="join",
        prefetch=1,
        vmem=16,
    )


def finish(chain, where, bit, flip, piece, target, shape, start):
    half, width = piece.shape
    parts = 4
    block = half // parts

    def body(where_ref, piece_ref, *rest):
        out_ref, made, sems = rest[-4], rest[-2], rest[-1]
        row = start + (side_of(where_ref, bit) ^ flip) * half
        copies = []
        for i in range(parts):
            made[i * block : (i + 1) * block, :] = piece_ref[i * block : (i + 1) * block, :].astype(F32)
            copies.append(
                pltpu.make_async_copy(
                    made.at[pl.ds(i * block, block)],
                    out_ref.at[pl.ds(pl.multiple_of(row + i * block, 16), block)],
                    sems.at[i],
                )
            )
            copies[-1].start()
        for copy in copies:
            copy.wait()

    args, specs, aliases = (where, piece), [VM], {}
    if target is not None:
        args, specs, aliases = args + (target,), specs + [HBM], {2: 0}
    made, chain.last = chain(
        body,
        args,
        specs,
        (shape_of(shape, F32), shape_of((8, 128), F32)),
        (HBM, HBM),
        [pltpu.VMEM((half, width), F32), pltpu.SemaphoreType.DMA((parts,))],
        aliases=aliases,
        name="finish",
        prefetch=1,
        vmem=16,
    )
    return made


def unpack(chain, pack, hidden, local):
    width = pack.shape[1]
    steps = hidden // width

    def body(pack_ref, *outs):
        for i in range(6):
            outs[i][...] = pack_ref[i, :]
        for i in range(steps):
            outs[6][i * width : (i + 1) * width] = pack_ref[6 + i, :]
        for i in range(2):
            outs[7][i : i + 1, :] = pack_ref[6 + steps : 7 + steps, i * local : (i + 1) * local]

    line = shape_of((width,), F32)
    return chain(
        body,
        (pack,),
        [VM],
        (line,) * 6 + (shape_of((hidden,), F32), shape_of((2, local), F32)),
        (VM,) * 8,
        name="unpack",
    )


class Lane:
    def __init__(self, chain, where, order, swap, home, start):
        self.chain, self.where, self.order, self.swap = chain, where, order, swap
        self.home, self.start = home, start
        self.keep = self.send = None
        self.stage = 0

    def begin(self, keep, send):
        self.keep, self.send = keep, send

    def over(self, bit, piece):
        return lax.ppermute(piece, "dp", xor_pairs(1 << bit))

    def to_home(self, piece, flip):
        made = finish(
            self.chain, self.where, self.order[0], flip, piece, self.home["now"], self.home["shape"], self.start
        )
        self.home["now"] = made

    def step(self):
        stage, order, chain = self.stage, self.order, self.chain
        self.stage += 1
        if stage < 2:
            recv = self.over(order[stage], self.send)
            self.send, self.keep = add_split(chain, self.where, order[stage + 1], self.keep, recv)
        elif stage == 2:
            self.keep = add(chain, self.keep, self.over(order[2], self.send))
        elif stage == 3:
            self.keep = add(chain, self.keep, self.over(self.swap, self.keep))
        elif stage < 6:
            bit = order[6 - stage]
            self.keep = join(chain, self.where, bit, self.keep, self.over(bit, self.keep))
        elif stage == 6:
            self.send = self.over(order[0], self.keep)
            self.to_home(self.keep, 0)
        else:
            self.to_home(self.send, 1)


ORDERS = {
    "D0": (2, 1, 0),
    "D1": (0, 1, 2),
    "U0": (0, 1, 2),
    "U1": (1, 0, 2),
    "O0": (1, 2, 0),
    "Q0": (2, 1, 0),
    "Q1": (0, 1, 2),
}
SCHEDULE = """
back_up u_send resid_back u_keep attend_back q_send U0 down U1 D0 U0 back_in q_keep D1 Q0 O0 U0
block_out Q0 O0 Q1 images_back Q1 U1 O0 U0 Q1 O0 Q0 D0 Q1 U1 D0 D1 O0 pack0 Q0 Q1 D0 U0 pack1 Q1 Q0
U1 D1 D0 U1 U0 pack2 Q0 D1 Q0 U0 Q1 Q1 D0 D0 O0 D1 U1 pack3 D1 U1 U0 D0 O0 unpack D1 U1 Q0 O0 D1
"""


def shards_cube(
    images,
    image_mask,
    cotangent,
    ln1_gain,
    ln1_bias,
    w_qkv,
    qv_bias,
    w_out,
    out_bias,
    ln2_gain,
    ln2_bias,
    w_up,
    up_bias,
    w_down,
    down_bias,
):
    _, rows, width = images.shape
    local = w_qkv.shape[2]
    hidden = w_up.shape[1]
    x = images.reshape(rows, width)
    cot = cotangent.reshape(rows, width)
    where = lax.axis_index("dp").astype(jnp.int32).reshape(1)
    w3 = jnp.transpose(w_qkv, (1, 0, 2))
    chain = Chain()

    def swapped(piece):
        return lax.ppermute(piece, "tensor", [(0, 1), (1, 0)])

    homes = {
        "D": {"now": None, "shape": (hidden, width)},
        "U": {"now": None, "shape": (width, hidden)},
        "O": {"now": None, "shape": (local, width)},
        "Q": {"now": None, "shape": (3 * width, local)},
    }
    places = {
        "D0": ("D", 0),
        "D1": ("D", hidden // 2),
        "U0": ("U", 0),
        "U1": ("U", width // 2),
        "O0": ("O", 0),
        "Q0": ("Q", 0),
        "Q1": ("Q", 3 * width // 2),
    }
    lanes = {
        name: Lane(chain, where, ORDERS[name], 3, homes[home], start) for name, (home, start) in places.items()
    }

    part, q, k, v, mixed, n1, lse = attend(chain, x, ln1_gain, ln1_bias, qv_bias, w3, w_out)
    part_b = swapped(part)
    ga, go, bd = grad_act_of(chain, image_mask, cot, w_down)
    act, gp, n2, bu, k0, s0, k1, s1 = feed(
        chain, where, (ORDERS["D0"][0], ORDERS["D1"][0]), x, part, part_b, out_bias, ln2_gain, ln2_bias, go, w_up, up_bias, ga
    )
    lanes["D0"].begin(k0, s0)
    lanes["D1"].begin(k1, s1)
    up = [(0, ORDERS["U0"][0], 0, hidden), (2, ORDERS["U1"][0], 0, hidden)]
    qkv = (ORDERS["Q0"][0], ORDERS["Q1"][0])
    have = {}

    def compute(name):
        if name == "u_send":
            have["us"] = weight_grad(chain, where, n2, gp, up, 1, width // 4)
        elif name == "u_keep":
            kept = weight_grad(chain, where, n2, gp, up, 0, width // 4)
            for i in range(2):
                lanes["U%d" % i].begin(kept[i], have["us"][i])
        elif name == "back_up":
            have["gn2"] = back_up(chain, gp, w_up)
            have["gn2b"] = swapped(have["gn2"])
        elif name == "down":
            have["mlp"] = down(chain, act, w_down)
            have["mlpb"] = swapped(have["mlp"])
        elif name == "resid_back":
            have["gr"], have["gm"], have["s2"], keep, send = resid_back(
                chain, where, ORDERS["O0"][0], x, part, part_b, out_bias, ln2_gain, have["gn2"], have["gn2b"], go, mixed, w_out
            )
            lanes["O0"].begin(keep, send)
        elif name == "attend_back":
            have["grads"], have["bq"] = attend_back(chain, q, k, v, mixed, have["gm"], lse)
        elif name == "q_send":
            have["qs"] = qkv_grad(chain, where, n1, have["grads"], qkv, 1)
        elif name == "q_keep":
            kept = qkv_grad(chain, where, n1, have["grads"], qkv, 0)
            for i in range(2):
                lanes["Q%d" % i].begin(kept[i], have["qs"][i])
        elif name == "back_in":
            have["gn1"] = back_in(chain, have["grads"], w3, rows)
            have["gn1b"] = swapped(have["gn1"])
        elif name == "images_back":
            have["out"], have["pack"] = images_back(
                chain, x, ln1_gain, have["gr"], have["gn1"], have["gn1b"], bd, bu, have["s2"], have["bq"]
            )
        elif name == "block_out":
            have["block"] = block_out(chain, x, part, part_b, out_bias, have["mlp"], have["mlpb"], down_bias)
        elif name[:4] == "pack":
            have["pack"] = add(chain, have["pack"], lax.ppermute(have["pack"], "dp", xor_pairs(1 << int(name[4]))))
        elif name == "unpack":
            have["small"] = unpack(chain, have["pack"], hidden, local)

    for name in SCHEDULE.split():
        if name in lanes:
            lanes[name].step()
        else:
            compute(name)
    small = have["small"]
    return (
        have["block"].reshape(images.shape),
        have["out"].reshape(images.shape),
        small[0],
        small[1],
        jnp.transpose(homes["Q"]["now"].reshape(3, width, local), (1, 0, 2)),
        small[7],
        homes["O"]["now"],
        small[2],
        small[3],
        small[4],
        homes["U"]["now"],
        small[6],
        homes["D"]["now"],
        small[5],
    )


def shards(*args):
    images, w_up = args[0], args[11]
    cube = lax.axis_size("dp") == 16 and lax.axis_size("tensor") == 2
    if cube and images.shape[0] == 1 and w_up.shape[1] == 2 * w_up.shape[0]:
        return shards_cube(*args)
    return shards_any(*args)


def solution(mesh):
    in_specs = (
        P("dp", None, None),
        P("dp"),
        P("dp", None, None),
        P(),
        P(),
        P(None, None, "tensor"),
        P(None, "tensor"),
        P("tensor", None),
        P(),
        P(),
        P(),
        P(None, "tensor"),
        P("tensor"),
        P("tensor", None),
        P(),
    )
    out_specs = (
        P("dp", None, None),
        P("dp", None, None),
        P(),
        P(),
        P(None, None, "tensor"),
        P(None, "tensor"),
        P("tensor", None),
        P(),
        P(),
        P(),
        P(None, "tensor"),
        P("tensor"),
        P("tensor", None),
        P(),
    )
    return jax.shard_map(shards, mesh=mesh, in_specs=in_specs, out_specs=out_specs, check_vma=False)
```

```python
import jax
import jax.numpy as jnp
from jax import lax
from jax.experimental import pallas as pl
from jax.experimental.pallas import tpu as pltpu
from jax.sharding import PartitionSpec as P

HD = 64
VALID = 577
EPS = 1e-06
BF = jnp.bfloat16
F32 = jnp.float32


def stats(values):
    mean = jnp.mean(values, axis=-1, keepdims=True)
    centred = values - mean
    spread = jnp.mean(centred * centred, axis=-1, keepdims=True)
    inv = lax.rsqrt(spread + EPS)
    return centred * inv, inv


def norm_back(unit, inv, gain, grad):
    scaled = grad * gain
    mean_a = jnp.mean(scaled, axis=-1, keepdims=True)
    mean_b = jnp.mean(scaled * unit, axis=-1, keepdims=True)
    return inv * (scaled - mean_a - unit * mean_b)


def inner_rows(left, right):
    return lax.dot_general(
        left, right, (((0,), (0,)), ((), ())), preferred_element_type=F32
    )


def times_back(left, weight):
    return lax.dot_general(
        left, weight, (((1,), (1,)), ((), ())), preferred_element_type=F32
    )


def score_block(query, keyset):
    raw = jnp.einsum("qhd,khd->hqk", query, keyset, preferred_element_type=F32)
    live = jnp.arange(raw.shape[-1]) < VALID
    return jnp.where(live, raw * HD ** (-0.5), -1e30)


def attend_forward(query, keyset, valueset):
    scores = score_block(query, keyset)
    peak = jnp.max(scores, axis=-1, keepdims=True)
    expo = jnp.exp(scores - peak)
    total = jnp.sum(expo, axis=-1, keepdims=True)
    probs = (expo / total).astype(BF)
    mixed = jnp.einsum("hqk,khd->qhd", probs, valueset, preferred_element_type=F32)
    return mixed.astype(BF), peak[..., 0] + jnp.log(total[..., 0])


def attend_backward(query, keyset, valueset, grad_mixed, logsum):
    scores = score_block(query, keyset)
    probs = jnp.exp(scores - logsum[..., None])
    grad_probs = jnp.einsum("qhd,khd->hqk", grad_mixed, valueset, preferred_element_type=F32)
    delta = jnp.sum(probs * grad_probs, axis=-1, keepdims=True)
    grad_scores = (probs * (grad_probs - delta) * HD ** (-0.5)).astype(BF)
    low_probs = probs.astype(BF)
    grad_value = jnp.einsum("hqk,qhd->khd", low_probs, grad_mixed, preferred_element_type=F32)
    grad_query = jnp.einsum("hqk,khd->qhd", grad_scores, keyset, preferred_element_type=F32)
    grad_key = jnp.einsum("hqk,qhd->khd", grad_scores, query, preferred_element_type=F32)
    return jnp.stack([grad_query, grad_key, grad_value], axis=1).astype(BF)


def swap_sum(part):
    if lax.axis_size("tensor") == 2:
        other = lax.ppermute(part, "tensor", [(0, 1), (1, 0)])
        return part.astype(F32) + other.astype(F32)
    return lax.psum(part.astype(F32), "tensor")


def xor_pairs(bit):
    return [(i, i ^ bit) for i in range(lax.axis_size("dp"))]


def bits_of():
    count = lax.axis_size("dp")
    bits = []
    while count > 1:
        if count % 2:
            raise ValueError("dp")
        bits.append(1 << len(bits))
        count //= 2
    return bits


def sum_small(vector):
    for bit in bits_of():
        vector = vector + lax.ppermute(vector, "dp", xor_pairs(bit))
    return vector


def cut_thirds(rows, turn):
    unit = 128
    whole = rows // unit
    base = whole // 3
    counts = [base + (1 if (i - turn) % 3 < whole % 3 else 0) for i in range(3)]
    return [c * unit for c in counts]


def sum_over_dp(matrix, turn):
    bits = bits_of()
    index = lax.axis_index("dp")
    halving = bits[: min(3, len(bits) - 1)]
    swaps = bits[len(halving) :]
    pieces, orders, start = [], [], 0
    for lane, rows in enumerate(cut_thirds(matrix.shape[0], turn)):
        if rows == 0:
            continue
        pieces.append(lax.slice_in_dim(matrix, start, start + rows, axis=0))
        turned = lane % len(halving)
        orders.append(halving[turned:] + halving[:turned])
        start += rows
    for step in range(len(halving)):
        for lane in range(len(pieces)):
            piece, bit = pieces[lane], orders[lane][step]
            half = piece.shape[0] // 2
            side = (index // bit) & 1
            kept = lax.dynamic_slice_in_dim(piece, side * half, half, 0)
            sent = lax.dynamic_slice_in_dim(piece, (1 - side) * half, half, 0)
            pieces[lane] = kept + lax.ppermute(sent, "dp", xor_pairs(bit))
    for bit in swaps:
        for lane in range(len(pieces)):
            pieces[lane] = pieces[lane] + lax.ppermute(pieces[lane], "dp", xor_pairs(bit))
    for step in reversed(range(len(halving))):
        for lane in range(len(pieces)):
            piece, bit = pieces[lane], orders[lane][step]
            other = lax.ppermute(piece, "dp", xor_pairs(bit))
            side = (index // bit) & 1
            pieces[lane] = jnp.where(
                side == 0,
                jnp.concatenate([piece, other], axis=0),
                jnp.concatenate([other, piece], axis=0),
            )
    return jnp.concatenate(pieces, axis=0).astype(F32)


def shards_any(
    images,
    image_mask,
    cotangent,
    ln1_gain,
    ln1_bias,
    w_qkv,
    qv_bias,
    w_out,
    out_bias,
    ln2_gain,
    ln2_bias,
    w_up,
    up_bias,
    w_down,
    down_bias,
):
    count, seq, width = images.shape
    rows = count * seq
    local = w_qkv.shape[2]
    heads = local // HD
    gain1 = ln1_gain.astype(F32)
    gain2 = ln2_gain.astype(F32)
    inputs = images.reshape(rows, width).astype(F32)
    keep = image_mask.astype(BF)[:, None, None]
    grad_out = (cotangent * keep).reshape(rows, width)
    w_qkv_flat = w_qkv.reshape(width, 3 * local)
    bias_row = jnp.concatenate([qv_bias[0], jnp.zeros_like(qv_bias[0]), qv_bias[1]]).astype(F32)

    unit1, inv1 = stats(inputs)
    normed1 = (unit1 * gain1 + ln1_bias.astype(F32)).astype(BF)
    qkv = (jnp.dot(normed1, w_qkv_flat, preferred_element_type=F32) + bias_row).astype(BF)
    split = qkv.reshape(count, seq, 3, heads, HD)
    attended = [attend_forward(split[i, :, 0], split[i, :, 1], split[i, :, 2]) for i in range(count)]
    mixed = jnp.concatenate([a[0] for a in attended], axis=0).reshape(rows, local)
    attn = swap_sum(jnp.dot(mixed, w_out, preferred_element_type=F32).astype(BF))
    grad_act = times_back(grad_out, w_down)
    resid = inputs + attn + out_bias.astype(F32)
    unit2, inv2 = stats(resid)
    normed2 = (unit2 * gain2 + ln2_bias.astype(F32)).astype(BF)
    pre = jnp.dot(normed2, w_up, preferred_element_type=F32) + up_bias.astype(F32)
    cdf = 0.5 * (1.0 + lax.erf(pre * (0.5**0.5)))
    act = (pre * cdf).astype(BF)
    slope = cdf + pre * jnp.exp(-0.5 * pre * pre) * ((0.5 / jnp.pi) ** 0.5)
    grad_pre = (grad_act * slope).astype(BF)
    grad_wdown = inner_rows(act, grad_out).astype(BF)
    summed_wdown = sum_over_dp(grad_wdown, 0)
    grad_wup = inner_rows(normed2, grad_pre).astype(BF)
    summed_wup = sum_over_dp(grad_wup, 1)
    grad_normed2 = swap_sum(times_back(grad_pre, w_up).astype(BF))
    mlp = swap_sum(jnp.dot(act, w_down, preferred_element_type=F32).astype(BF))
    block_output = (resid + mlp + down_bias.astype(F32)).astype(BF).reshape(images.shape)
    grad_resid = grad_out.astype(F32) + norm_back(unit2, inv2, gain2, grad_normed2)
    resid_low = grad_resid.astype(BF)
    grad_wout = inner_rows(mixed, resid_low).astype(BF)
    summed_wout = sum_over_dp(grad_wout, 2)
    grad_mixed = times_back(resid_low, w_out).astype(BF).reshape(count, seq, heads, HD)
    grad_qkv = jnp.concatenate(
        [
            attend_backward(split[i, :, 0], split[i, :, 1], split[i, :, 2], grad_mixed[i], attended[i][1])
            for i in range(count)
        ],
        axis=0,
    ).reshape(rows, 3 * local)
    grad_wqkv = inner_rows(normed1, grad_qkv).astype(BF)
    summed_wqkv = sum_over_dp(grad_wqkv, 0).reshape(width, 3, local)
    bias_sums = jnp.sum(grad_qkv.astype(F32), axis=0)
    grad_normed1 = swap_sum(times_back(grad_qkv, w_qkv_flat).astype(BF))
    images_grad = (
        (grad_resid + norm_back(unit1, inv1, gain1, grad_normed1)).astype(BF).reshape(images.shape)
    )

    small = [
        jnp.sum(grad_normed1 * unit1, axis=0),
        jnp.sum(grad_normed1, axis=0),
        jnp.sum(grad_resid, axis=0),
        jnp.sum(grad_normed2 * unit2, axis=0),
        jnp.sum(grad_normed2, axis=0),
        jnp.sum(grad_out.astype(F32), axis=0),
        jnp.sum(grad_pre.astype(F32), axis=0),
        bias_sums[:local],
        bias_sums[2 * local :],
    ]
    flat = jnp.concatenate(small)
    length = flat.shape[0]
    padded = -(-length // 1024) * 1024
    flat = sum_small(jnp.pad(flat, (0, padded - length)).reshape(padded // 128, 128)).reshape(-1)
    out, at = [], 0
    for part in small:
        out.append(flat[at : at + part.shape[0]])
        at += part.shape[0]
    return (
        block_output,
        images_grad,
        out[0],
        out[1],
        summed_wqkv,
        jnp.stack([out[7], out[8]]),
        summed_wout,
        out[2],
        out[3],
        out[4],
        summed_wup,
        out[6],
        summed_wdown,
        out[5],
    )


CHUNKS = 2
ANY = pl.BlockSpec(memory_space=pl.ANY)
HBM = pl.BlockSpec(memory_space=pltpu.HBM)
VM = pl.BlockSpec(memory_space=pltpu.VMEM)
MIB = 1024 * 1024


def shape_of(shape, dtype):
    return jax.ShapeDtypeStruct(shape, dtype)


def nn(left, right):
    return jnp.dot(left, right, preferred_element_type=F32)


def normal_unit(values):
    mean = jnp.mean(values, axis=-1, keepdims=True)
    centred = values - mean
    spread = jnp.mean(centred * centred, axis=-1, keepdims=True)
    inv = lax.rsqrt(spread + EPS)
    return centred * inv, inv


def row_of(ref):
    return ref[...].astype(F32).reshape(1, ref.shape[0])


def side_of(where_ref, bits):
    bit = bits[0] if bits[0] == bits[1] else jnp.where(where_ref[1] == 0, bits[0], bits[1])
    return (where_ref[0] >> bit) & 1


class Chain:
    def __init__(self):
        self.last = None

    def __call__(
        self, body, args, in_specs, outs, out_specs, scratch=(), grid=(), vmem=40, aliases=None, name=None, prefetch=0, cost=0.001
    ):
        args, in_specs, run = list(args), list(in_specs), body
        if self.last is not None:
            spot = len(args)

            def run(*refs):
                body(*refs[:spot], *refs[spot + 1 :])

            args.append(self.last)
            in_specs.append(ANY)
        spec = pltpu.PrefetchScalarGridSpec(
            num_scalar_prefetch=prefetch,
            grid=grid,
            in_specs=in_specs,
            out_specs=out_specs,
            scratch_shapes=list(scratch),
        )
        made = pl.pallas_call(
            run,
            out_shape=outs,
            grid_spec=spec,
            input_output_aliases=aliases or {},
            compiler_params=pltpu.CompilerParams(vmem_limit_bytes=vmem * MIB),
            cost_estimate=pl.CostEstimate(flops=0, bytes_accessed=int(cost * 3e6), transcendentals=0),
            name=name,
        )(*args)
        self.last = made[0] if isinstance(made, (tuple, list)) else made
        return made


def row_chunks(rows):
    units, parts = rows // 16, CHUNKS
    cuts = [16 * (units * i // parts) for i in range(parts)] + [rows]
    return [(cuts[i], cuts[i + 1] - cuts[i]) for i in range(parts)]


def lane_halves():
    return lax.broadcasted_iota(jnp.int32, (1, 2 * HD), 1) < HD


def key_mask(length):
    return jnp.where(lax.broadcasted_iota(jnp.int32, (1, length), 1) < VALID, 0.0, -1e30)


def copier(sems):
    count = [0]

    def copy(source, target):
        made = pltpu.make_async_copy(source, target, sems.at[count[0]])
        count[0] += 1
        made.start()
        return made

    return copy


def attend_kernel(
    mask_ref, g_ref, s_ref, b_ref, x_ref, w_ref, wo_ref, cot_ref, wd_ref,
    part_ref, q_ref, k_ref, v_ref, mixed_ref, n1_ref, lse_ref, ga_ref, go_ref, bd_ref,
    x_b, w_b, wo_b, cot_b, wd_b, part_b, q_b, k_b, v_b, mixed_b, n1_b, lse_b, ga_b, go_b, sems,
):
    rows, width = x_ref.shape
    padded, local = q_ref.shape
    pairs = local // 128
    deep = wd_ref.shape[0] // pairs
    copy = copier(sems)
    get_x = copy(x_ref, x_b)
    get_w = [copy(w_ref.at[c], w_b.at[c]) for c in range(3)]
    get_cot = copy(cot_ref, cot_b)
    get_wd = [copy(wd_ref.at[pl.ds(i * deep, deep)], wd_b.at[i]) for i in range(pairs)]
    get_wo = copy(wo_ref, wo_b)
    puts = []
    get_x.wait()
    unit, _ = normal_unit(x_b[...].astype(F32))
    normed = unit * row_of(g_ref) + row_of(s_ref)
    n1_b[...] = jnp.concatenate([normed, jnp.zeros((padded - rows, width), F32)], axis=0).astype(BF)
    puts.append(copy(n1_b, n1_ref))
    lse_b[...] = jnp.zeros(lse_b.shape, F32)
    live = lax.broadcasted_iota(jnp.int32, (padded, 1), 0) < rows
    for c, (buf, ref, scale) in enumerate(((q_b, q_ref, HD ** (-0.5)), (k_b, k_ref, 1.0), (v_b, v_ref, 1.0))):
        get_w[c].wait()
        for at in range(0, local, 256):
            made = nn(n1_b[...], w_b[c, :, at : at + 256])
            if c != 1:
                made = made + b_ref[c // 2 : c // 2 + 1, at : at + 256].astype(F32)
            made = jnp.where(live, made, 0.0).astype(BF)
            buf[:, at : at + 256] = made * jnp.asarray(scale, BF)
        puts.append(copy(buf, ref))
    get_cot.wait()
    masked = cot_b[...].astype(F32) * mask_ref[0].astype(F32)
    go_b[...] = masked.astype(BF)
    puts.append(copy(go_b, go_ref))
    bd_ref[...] = jnp.sum(masked, axis=0, keepdims=True)
    for get in get_wd:
        get.wait()
    mask = key_mask(padded)
    first = lane_halves()
    lane = lax.broadcasted_iota(jnp.int32, (1, 128), 1)

    def pair(p, carry):
        cols = pl.ds(pl.multiple_of(p * 128, 128), 128)
        keys, vals = k_b[:, cols], v_b[:, cols]
        query = q_b[:, cols]
        zero, ones = jnp.zeros_like(keys), jnp.ones_like(vals)
        own_k = (jnp.where(first, keys, zero), jnp.where(first, zero, keys))
        own_v = (jnp.where(first, vals, ones), jnp.where(first, ones, vals))
        ga_b[:, pl.ds(pl.multiple_of(p * deep, deep), deep)] = times_back(go_b[...], wd_b[p]).astype(BF)
        outs = []
        logs = lse_b[...]
        for h in range(2):
            scores = times_back(query, own_k[h]) + mask
            peak = jnp.max(scores, axis=-1, keepdims=True)
            made = nn(jnp.exp(scores - peak).astype(BF), own_v[h])
            total = made[:, HD : HD + 1] if h == 0 else made[:, 0:1]
            outs.append(made * (1.0 / total))
            logs = jnp.where(lane == 2 * p + h, peak + jnp.log(total), logs)
        lse_b[...] = logs
        mixed_b[:, cols] = jnp.where(first, outs[0], outs[1]).astype(BF)
        return carry

    lax.fori_loop(0, pairs, pair, 0)
    puts += [copy(ga_b, ga_ref), copy(mixed_b, mixed_ref), copy(lse_b, lse_ref)]
    get_wo.wait()
    for at in range(0, width, 256):
        made = nn(mixed_b[...], wo_b[:, at : at + 256])
        part_b[:, at : at + 256] = made[:rows].astype(BF)
    puts.append(copy(part_b, part_ref))
    for put in puts:
        put.wait()


def attend(chain, mask, gain, shift, bias, x, w3, w_out, cot, w_down):
    rows, width = x.shape
    local = w3.shape[2]
    hidden = w_down.shape[0]
    padded = -(-rows // 16) * 16
    pairs = local // 128
    slab = ((rows, width), BF)
    wide = ((padded, local), BF)
    outs = (slab, wide, wide, wide, wide, ((padded, width), BF), ((padded, 128), F32), ((rows, hidden), BF), slab)
    held = (slab, ((3, width, local), BF), ((local, width), BF), slab, ((pairs, hidden // pairs, width), BF)) + outs
    return chain(
        attend_kernel,
        (mask, gain, shift, bias, x, w3, w_out, cot, w_down),
        [VM] * 3 + [HBM] * 5,
        tuple(shape_of(*out) for out in outs) + (shape_of((1, width), F32),),
        (HBM,) * len(outs) + (VM,),
        [pltpu.VMEM(*hold) for hold in held] + [pltpu.SemaphoreType.DMA((7 + pairs + len(outs),))],
        name="attend",
        vmem=60,
        prefetch=1,
    )


def gelu_pair(pre):
    bell = jnp.exp(-0.5 * pre * pre)
    near = 1.0 / (1.0 + (0.3275911 * 0.5**0.5) * jnp.abs(pre))
    poly = near * (
        0.254829592 + near * (-0.284496736 + near * (1.421413741 + near * (-1.453152027 + near * 1.061405429)))
    )
    tail = 0.5 * poly * bell
    cdf = jnp.where(pre < 0, tail, 1.0 - tail)
    return cdf, cdf + pre * bell * ((0.5 / jnp.pi) ** 0.5)


def feed_kernel(
    where_ref, ob_ref, g_ref, s_ref, ub_ref, x_ref, pa_ref, pb_ref, go_ref, wu_ref, ga_ref,
    act_ref, gn_ref, ds0_ref, ds1_ref, dk0_ref, dk1_ref, us0_ref, us1_ref, uk0_ref, uk1_ref, bu_ref,
    x_b, pa_b, pb_b, go_b, wu_b, ga_b, act_b, n2_b, down_b, up_b, gn_b, total, bias, sems, *, bits,
):
    rows, width = x_ref.shape
    hidden = wu_ref.shape[1]
    size = hidden // 4
    tall = width // 4
    sides = [side_of(where_ref, bit) for bit in bits]
    starts = [pl.multiple_of((2 * lane + (1 - sides[lane])) * size, size) for lane in range(2)]
    starts += [pl.multiple_of((2 * lane + sides[lane]) * size, size) for lane in range(2)]
    tops = [pl.multiple_of((2 * lane + (1 - sides[2 + lane])) * tall, tall) for lane in range(2)]
    tops += [pl.multiple_of((2 * lane + sides[2 + lane]) * tall, tall) for lane in range(2)]
    copy = copier(sems)
    gets = [copy(x_ref, x_b), copy(pa_ref, pa_b), copy(pb_ref, pb_b)]
    get_w, get_ga = [], []
    for c in range(4):
        get_w.append(copy(wu_ref.at[:, pl.ds(starts[c], size)], wu_b.at[c]))
        get_ga.append(copy(ga_ref.at[:, pl.ds(starts[c], size)], ga_b.at[c]))
        if c == 0:
            get_go = copy(go_ref, go_b)
    puts = []
    bias[...] = row_of(ub_ref)
    for get in gets:
        get.wait()
    resid = x_b[...].astype(F32) + (pa_b[...].astype(F32) + pb_b[...].astype(F32)) + row_of(ob_ref)
    unit, _ = normal_unit(resid)
    n2_b[...] = (unit * row_of(g_ref) + row_of(s_ref)).astype(BF)

    def front(c):
        get_w[c].wait()
        get_ga[c].wait()
        for at in range(0, size, 256):
            cols = pl.ds(pl.multiple_of(starts[c] + at, 256), 256)
            pre = nn(n2_b[...], wu_b[c, :, at : at + 256]) + bias[:, cols]
            cdf, slope = gelu_pair(pre)
            act_b[c, :, at : at + 256] = (pre * cdf).astype(BF)
            grad_pre = (ga_b[c, :, at : at + 256].astype(F32) * slope).astype(BF)
            ga_b[c, :, at : at + 256] = grad_pre
            bu_ref[:, cols] = jnp.sum(grad_pre.astype(F32), axis=0, keepdims=True)
        puts.append(copy(act_b.at[c], act_ref.at[:, pl.ds(starts[c], size)]))

    def back(c):
        if c == 0:
            get_go.wait()
        for at in range(0, width, 512):
            made = inner_rows(act_b[c], go_b[:, at : at + 512])
            down_b[c, :, at : at + 512] = made.astype(BF)
        puts.append(copy(down_b.at[c], (ds0_ref, ds1_ref, dk0_ref, dk1_ref)[c]))
        for piece in range(4):
            made = inner_rows(n2_b[:, pl.ds(tops[piece], tall)], ga_b[c])
            up_b[piece, :, pl.ds(starts[c], size)] = made.astype(BF)
        for at in range(0, width, 512):
            made = times_back(ga_b[c], wu_b[c, at : at + 512, :])
            if c:
                made = made + total[:, at : at + 512]
            if c < 3:
                total[:, at : at + 512] = made
            else:
                gn_b[:, at : at + 512] = made.astype(BF)

    for c in range(5):
        if c < 4:
            front(c)
        if c:
            back(c - 1)
    puts.append(copy(gn_b, gn_ref))
    for piece, ref in enumerate((us0_ref, us1_ref, uk0_ref, uk1_ref)):
        puts.append(copy(up_b.at[piece], ref))
    for put in puts:
        put.wait()


def feed(chain, where, bits, out_bias, gain, shift, up_bias, x, pa, pb, go, w_up, ga):
    rows, width = x.shape
    hidden = w_up.shape[1]

    def body(*refs):
        feed_kernel(*refs, bits=bits)

    slab = ((rows, width), BF)
    deep = ((4, rows, hidden // 4), BF)
    outs = (((rows, hidden), BF), slab) + (((hidden // 4, width), BF),) * 4 + (((width // 4, hidden), BF),) * 4
    held = (slab,) * 4 + (((4, width, hidden // 4), BF), deep, deep, slab, ((4, hidden // 4, width), BF))
    held += (((4, width // 4, hidden), BF), slab, ((rows, width), F32), ((1, hidden), F32))
    return chain(
        body,
        (where, out_bias, gain, shift, up_bias, x, pa, pb, go, w_up, ga),
        [VM] * 4 + [HBM] * 6,
        tuple(shape_of(*out) for out in outs) + (shape_of((1, hidden), F32),),
        (HBM,) * len(outs) + (VM,),
        [pltpu.VMEM(*hold) for hold in held] + [pltpu.SemaphoreType.DMA((12 + 4 + len(outs),))],
        name="feed",
        vmem=60,
        prefetch=1,
    )


def qkv_grad(chain, where, n1, grads, out_grad, bits, flip):
    width = n1.shape[1]
    local = grads.shape[1] // 3
    size = width // 4

    def body(where_ref, n1_ref, g_ref, o_ref, first_ref, second_ref):
        def product(ref, start):
            for i in range(4):
                made = inner_rows(n1_ref[:, i * size : (i + 1) * size], g_ref[:, pl.ds(start, local)])
                ref[i * size : (i + 1) * size, :] = made.astype(BF)

        product(first_ref, pl.multiple_of((side_of(where_ref, bits[0]) ^ flip) * local, local))
        which = side_of(where_ref, bits[1]) ^ flip

        @pl.when(which == 0)
        def _():
            product(second_ref, 2 * local)

        @pl.when(which == 1)
        def _():
            second_ref[...] = o_ref[...]

    return chain(
        body,
        (where, n1, grads, out_grad),
        [VM, VM, VM],
        (shape_of((width, local), BF),) * 2,
        (VM,) * 2,
        name="qkv_grad",
        prefetch=1,
    )


TILES = 4


def paired(own, other):
    return own[...].astype(F32) + other[...].astype(F32)


def down(chain, act, w_down):
    rows, hidden = act.shape
    width = w_down.shape[1]
    size = width // TILES
    deep = hidden // TILES

    def body(act_ref, w_ref, *rest):
        out_ref, w_buf, sems = rest
        copies = [
            pltpu.make_async_copy(w_ref.at[pl.ds(i * deep, deep)], w_buf.at[pl.ds(i * deep, deep)], sems.at[i])
            for i in range(TILES)
        ]
        for copy in copies:
            copy.start()
        for copy in copies:
            copy.wait()
        for i in range(TILES):
            out_ref[:, i * size : (i + 1) * size] = nn(act_ref[...], w_buf[:, i * size : (i + 1) * size]).astype(BF)

    return chain(
        body,
        (act, w_down),
        [VM, HBM],
        shape_of((rows, width), BF),
        VM,
        [pltpu.VMEM((hidden, width), BF), pltpu.SemaphoreType.DMA((TILES,))],
        name="down",
    )


def resid_back_kernel(
    x_ref, pa_ref, pb_ref, ob_ref, g_ref, ga_ref, gb_ref, go_ref, mixed_ref, wo_ref, gr_ref, gm_ref, sums_ref, og_ref, low
):
    rows, width = x_ref.shape
    padded, local = mixed_ref.shape
    resid = x_ref[...].astype(F32) + (pa_ref[...].astype(F32) + pb_ref[...].astype(F32)) + row_of(ob_ref)
    unit, inv = normal_unit(resid)
    grad = paired(ga_ref, gb_ref)
    total = go_ref[...].astype(F32) + norm_back(unit, inv, row_of(g_ref), grad)
    gr_ref[...] = total
    low[...] = jnp.concatenate([total, jnp.zeros((padded - rows, width), F32)], axis=0).astype(BF)
    sums_ref[...] = jnp.concatenate(
        [
            jnp.sum(total, axis=0, keepdims=True),
            jnp.sum(grad * unit, axis=0, keepdims=True),
            jnp.sum(grad, axis=0, keepdims=True),
            jnp.zeros((5, width), F32),
        ],
        axis=0,
    )
    for i in range(2):
        for at in range(0, width // 2, 256):
            start = i * width // 2 + at
            made = inner_rows(mixed_ref[...], low[:, start : start + 256])
            og_ref[i * local : (i + 1) * local, at : at + 256] = made.astype(BF)
    for at in range(0, local, 256):
        gm_ref[:, at : at + 256] = times_back(low[...], wo_ref[at : at + 256, :]).astype(BF)


def resid_back(chain, x, pa, pb, out_bias, gain, ga, gb, go, mixed, w_out):
    rows, width = x.shape
    padded, local = mixed.shape
    return chain(
        resid_back_kernel,
        (x, pa, pb, out_bias, gain, ga, gb, go, mixed, w_out),
        [VM] * 10,
        (
            shape_of((rows, width), F32),
            shape_of((padded, local), BF),
            shape_of((8, width), F32),
            shape_of((2 * local, width // 2), BF),
        ),
        (VM,) * 4,
        [pltpu.VMEM((padded, width), BF)],
        name="resid_back",
    )


def attend_back_kernel(q_ref, k_ref, v_ref, mixed_ref, gm_ref, lse_ref, out_ref, bias_ref, probs_s, slopes_s):
    padded, local = q_ref.shape
    mask = key_mask(padded)
    first = lane_halves()
    lane = lax.broadcasted_iota(jnp.int32, (1, 128), 1)

    def pair(p, carry):
        cols = pl.ds(pl.multiple_of(p * 128, 128), 128)
        keys, vals = k_ref[:, cols], v_ref[:, cols]
        zero = jnp.zeros_like(keys)
        own_k = (jnp.where(first, keys, zero), jnp.where(first, zero, keys))
        own_v = (jnp.where(first, vals, zero), jnp.where(first, zero, vals))
        for at, size in row_chunks(padded):
            query = q_ref[at : at + size, cols]
            grad = gm_ref[at : at + size, cols]
            both = grad.astype(F32) * mixed_ref[at : at + size, cols].astype(F32)
            logs = lse_ref[at : at + size, :]
            outs = []
            for h in range(2):
                own_lanes = first if h == 0 else jnp.logical_not(first)
                delta = jnp.sum(jnp.where(own_lanes, both, 0.0), axis=-1, keepdims=True)
                log = jnp.sum(jnp.where(lane == 2 * p + h, logs, 0.0), axis=-1, keepdims=True)
                probs = jnp.exp(times_back(query, own_k[h]) + mask - log)
                slope = (probs * (times_back(grad, own_v[h]) - delta)).astype(BF)
                probs_s[h, at : at + size, :] = probs.astype(BF)
                slopes_s[h, at : at + size, :] = slope
                outs.append(nn(slope, keys))
            out_ref[at : at + size, cols] = (jnp.where(first, outs[0], outs[1]) * HD ** (-0.5)).astype(BF)
        grad_t = gm_ref[:, cols].astype(F32).T.astype(BF)
        query_t = q_ref[:, cols].astype(F32).T.astype(BF)
        grad_k = [nn(query_t[HD * h : HD * h + HD], slopes_s[h]) for h in range(2)]
        grad_v = [nn(grad_t[HD * h : HD * h + HD], probs_s[h]) for h in range(2)]
        cols_k = pl.ds(pl.multiple_of(local + p * 128, 128), 128)
        cols_v = pl.ds(pl.multiple_of(2 * local + p * 128, 128), 128)
        out_ref[:, cols_k] = jnp.concatenate(grad_k, axis=0).T.astype(BF)
        out_ref[:, cols_v] = jnp.concatenate(grad_v, axis=0).T.astype(BF)
        return carry

    lax.fori_loop(0, local // 128, pair, 0)
    bias_ref[...] = jnp.sum(out_ref[...].astype(F32), axis=0, keepdims=True)


def attend_back(chain, q, k, v, mixed, gm, lse):
    padded, local = q.shape
    return chain(
        attend_back_kernel,
        (q, k, v, mixed, gm, lse),
        [VM] * 6,
        (shape_of((padded, 3 * local), BF), shape_of((1, 3 * local), F32)),
        (VM, VM),
        [pltpu.VMEM((2, padded, padded), BF), pltpu.VMEM((2, padded, padded), BF)],
        name="attend_back",
    )


def back_in(chain, grads, w3, rows):
    _, width, local = w3.shape
    size = width // TILES

    def body(g_ref, w_ref, *rest):
        out_ref, w_buf, sems = rest
        copies = [
            pltpu.make_async_copy(w_ref.at[:, pl.ds(i * size, size)], w_buf.at[i], sems.at[i]) for i in range(TILES)
        ]
        for copy in copies:
            copy.start()
        for i in range(TILES):
            copies[i].wait()
            total = times_back(g_ref[:, :local], w_buf[i, 0])
            for c in range(1, 3):
                total += times_back(g_ref[:, c * local : (c + 1) * local], w_buf[i, c])
            out_ref[:, i * size : (i + 1) * size] = total[:rows].astype(BF)

    return chain(
        body,
        (grads, w3),
        [VM, HBM],
        shape_of((rows, width), BF),
        VM,
        [pltpu.VMEM((TILES, 3, size, local), BF), pltpu.SemaphoreType.DMA((TILES,))],
        name="back_in",
    )


def images_back_kernel(x_ref, g_ref, gr_ref, ga_ref, gb_ref, bd_ref, bu_ref, s2_ref, bq_ref, out_ref, pack_ref):
    unit, inv = normal_unit(x_ref[...].astype(F32))
    grad = paired(ga_ref, gb_ref)
    out_ref[...] = (gr_ref[...] + norm_back(unit, inv, row_of(g_ref), grad)).astype(BF)
    width = x_ref.shape[1]
    hidden = bu_ref.shape[1]
    local = bq_ref.shape[1] // 3
    pack_ref[0:1, :] = jnp.sum(grad * unit, axis=0, keepdims=True)
    pack_ref[1:2, :] = jnp.sum(grad, axis=0, keepdims=True)
    pack_ref[2:5, :] = s2_ref[0:3, :]
    pack_ref[5:6, :] = bd_ref[...]
    for i in range(hidden // width):
        pack_ref[6 + i : 7 + i, :] = bu_ref[:, i * width : (i + 1) * width]
    after = 6 + hidden // width
    pack_ref[after : after + 1, :local] = bq_ref[:, :local]
    pack_ref[after : after + 1, local:] = bq_ref[:, 2 * local :]
    pack_ref[after + 1 :, :] = jnp.zeros((pack_ref.shape[0] - after - 1, width), F32)


def images_back(chain, x, gain, gr, ga, gb, bd, bu, s2, bq):
    return chain(
        images_back_kernel,
        (x, gain, gr, ga, gb, bd, bu, s2, bq),
        [VM] * 9,
        (shape_of(x.shape, BF), shape_of((16, x.shape[1]), F32)),
        (VM, VM),
        name="images_back",
    )


def block_out_kernel(x_ref, pa_ref, pb_ref, ob_ref, ma_ref, mb_ref, db_ref, out_ref):
    resid = x_ref[...].astype(F32) + (pa_ref[...].astype(F32) + pb_ref[...].astype(F32)) + row_of(ob_ref)
    out_ref[...] = (resid + paired(ma_ref, mb_ref) + row_of(db_ref)).astype(BF)


def block_out(chain, x, pa, pb, out_bias, ma, mb, down_bias):
    return chain(
        block_out_kernel,
        (x, pa, pb, out_bias, ma, mb, down_bias),
        [VM] * 7,
        shape_of(x.shape, BF), VM, name="block_out"
    )


def add_split_kernel(where_ref, k0_ref, k1_ref, r0_ref, r1_ref, send_ref, keep_ref):
    keep_ref[...] = (k0_ref[...].astype(F32) + r0_ref[...].astype(F32)).astype(BF)
    send_ref[...] = (k1_ref[...].astype(F32) + r1_ref[...].astype(F32)).astype(BF)


def add_split(chain, where, bit, keep, recv):
    rows, width = keep.shape
    half = rows // 2
    block = (half, width)
    own = pl.BlockSpec(block, lambda i, w: (side_of(w, bit), 0))
    other = pl.BlockSpec(block, lambda i, w: (1 - side_of(w, bit), 0))
    out = pl.BlockSpec(block, lambda i, w: (0, 0))
    return chain(
        add_split_kernel,
        (where, keep, keep, recv, recv),
        [own, other, own, other],
        (shape_of((half, width), BF),) * 2,
        (out, out),
        grid=(1,),
        name="add_split",
        prefetch=1,
        vmem=16,
    )


def add_kernel(a_ref, b_ref, out_ref):
    out_ref[...] = (a_ref[...].astype(F32) + b_ref[...].astype(F32)).astype(out_ref.dtype)


def add(chain, a, b):
    return chain(add_kernel, (a, b), [VM, VM], shape_of(a.shape, a.dtype), VM, name="add", vmem=16)


def join(chain, where, bit, own, other):
    half, width = own.shape

    def body(where_ref, own_ref, other_ref, out_ref):
        side = side_of(where_ref, bit)
        out_ref[pl.ds(pl.multiple_of(side * half, 16), half), :] = own_ref[...]
        out_ref[pl.ds(pl.multiple_of((1 - side) * half, 16), half), :] = other_ref[...]

    return chain(
        body,
        (where, own, other),
        [VM, VM],
        shape_of((2 * half, width), BF),
        VM,
        name="join",
        prefetch=1,
        vmem=16,
    )


class Home:
    def __init__(self, shape):
        self.shape, self.now = shape, None


def finish(chain, where, bits, flip, piece, homes):
    half, width = piece.shape
    parts = 4
    block = half // parts
    targets = list(dict.fromkeys(home for home, _ in homes))
    old = [home for home in targets if home.now is not None]

    def body(where_ref, piece_ref, *rest):
        outs = rest[len(old) : len(old) + len(targets)]
        made, sems = rest[-2:]
        which = side_of(where_ref, bits) ^ flip

        def write(number):
            home, row = homes[number]
            out_ref = outs[targets.index(home)]
            copies = []
            for i in range(parts):
                made[i * block : (i + 1) * block, :] = piece_ref[i * block : (i + 1) * block, :].astype(F32)
                if home.shape[1] == width:
                    place = out_ref.at[pl.ds(row + i * block, block)]
                else:
                    high = home.shape[0]
                    place = out_ref.at[pl.ds(i * block % high, block), pl.ds(i * block // high * width, width)]
                copies.append(pltpu.make_async_copy(made.at[pl.ds(i * block, block)], place, sems.at[i]))
                copies[-1].start()
            for copy in copies:
                copy.wait()

        for number in range(2):

            @pl.when(which == number)
            def _(number=number):
                write(number)

    made = chain(
        body,
        (where, piece, *(home.now for home in old)),
        [VM] + [HBM] * len(old),
        tuple(shape_of(home.shape, F32) for home in targets) + (shape_of((8, 128), F32),),
        (HBM,) * (len(targets) + 1),
        [pltpu.VMEM((half, width), F32), pltpu.SemaphoreType.DMA((parts,))],
        aliases={2 + i: targets.index(home) for i, home in enumerate(old)},
        name="finish",
        prefetch=1,
        vmem=16,
    )
    for home, now in zip(targets, made[:-1], strict=True):
        home.now = now
    chain.last = made[-1]


def unpack(chain, pack, hidden, local):
    width = pack.shape[1]
    steps = hidden // width

    def body(pack_ref, *outs):
        for i in range(6):
            outs[i][...] = pack_ref[i, :]
        for i in range(steps):
            outs[6][i * width : (i + 1) * width] = pack_ref[6 + i, :]
        for i in range(2):
            outs[7][i : i + 1, :] = pack_ref[6 + steps : 7 + steps, i * local : (i + 1) * local]

    line = shape_of((width,), F32)
    return chain(
        body,
        (pack,),
        [VM],
        (line,) * 6 + (shape_of((hidden,), F32), shape_of((2, local), F32)),
        (VM,) * 8,
        name="unpack",
    )


class Lane:
    def __init__(self, chain, where, order, homes):
        self.chain, self.where, self.homes = chain, where, homes
        self.bits = list(zip(*order, strict=True))
        self.keep = self.send = None
        self.stage = 0

    def begin(self, keep, send):
        self.keep, self.send = keep, send

    def over(self, bits, piece):
        pairs = [
            (2 * i + core, 2 * (i ^ (1 << bits[core])) + core) for i in range(lax.axis_size("dp")) for core in range(2)
        ]
        return lax.ppermute(piece, ("dp", "tensor"), pairs)

    def step(self):
        stage, bits, chain = self.stage, self.bits, self.chain
        self.stage += 1
        if stage < 2:
            recv = self.over(bits[stage], self.send)
            self.send, self.keep = add_split(chain, self.where, bits[stage + 1], self.keep, recv)
        elif stage == 2:
            self.keep = add(chain, self.keep, self.over(bits[2], self.send))
        elif stage == 3:
            self.keep = add(chain, self.keep, self.over((3, 3), self.keep))
        elif stage < 6:
            bit = bits[6 - stage]
            self.keep = join(chain, self.where, bit, self.keep, self.over(bit, self.keep))
        elif stage == 6:
            self.send = self.over(bits[0], self.keep)
            finish(chain, self.where, bits[0], 0, self.keep, self.homes)
        else:
            finish(chain, self.where, bits[0], 1, self.send, self.homes)


ORDERS = {
    "D0": ((0, 1, 2), (1, 0, 2)),
    "D1": ((2, 0, 1), (2, 0, 1)),
    "U0": ((1, 2, 0), (0, 1, 2)),
    "U1": ((2, 1, 0), (1, 0, 2)),
    "Q0": ((1, 0, 2), (0, 1, 2)),
    "Q1": ((0, 1, 2), (2, 1, 0)),
}
SCHEDULE = (
    "down", "resid_back", "D0", "attend_back", "q_send", "D1", "q_keep", "back_in", "U0", "D0",
    "block_out", "U1", "Q1", "D0", "Q0", "images_back", "Q1", "D0", "U0", "D1", "Q1", "pack0", "D0",
    "D1", "Q1", "U1", "U0", "D1", "U1", "Q1", "Q0", "D0", "U0", "D1", "pack1", "Q0", "D0", "U1", "U0",
    "Q0", "Q1", "U1", "Q0", "D1", "D1", "U0", "D0", "Q0", "Q1", "pack2", "U1", "U0", "Q0", "U1", "D1",
    "pack3", "unpack", "Q1", "U0", "Q0", "U1",
)


def shards_cube(
    images,
    image_mask,
    cotangent,
    ln1_gain,
    ln1_bias,
    w_qkv,
    qv_bias,
    w_out,
    out_bias,
    ln2_gain,
    ln2_bias,
    w_up,
    up_bias,
    w_down,
    down_bias,
):
    _, rows, width = images.shape
    local = w_qkv.shape[2]
    hidden = w_up.shape[1]
    x = images.reshape(rows, width)
    cot = cotangent.reshape(rows, width)
    where = jnp.stack([lax.axis_index("dp"), lax.axis_index("tensor")]).astype(jnp.int32)
    w3 = jnp.transpose(w_qkv, (1, 0, 2))
    chain = Chain()

    def swapped(piece):
        return lax.ppermute(piece, "tensor", [(0, 1), (1, 0)])

    downs, ups, outs = Home((hidden, width)), Home((width, hidden)), Home((local, width))
    projections = Home((3 * width, local))
    places = {
        "D0": ((downs, 0), (downs, hidden // 4)),
        "D1": ((downs, hidden // 2), (downs, 3 * hidden // 4)),
        "U0": ((ups, 0), (ups, width // 4)),
        "U1": ((ups, width // 2), (ups, 3 * width // 4)),
        "Q0": ((projections, 0), (projections, width)),
        "Q1": ((projections, 2 * width), (outs, 0)),
    }
    lanes = {name: Lane(chain, where, ORDERS[name], homes) for name, homes in places.items()}
    first = {name: lane.bits[0] for name, lane in lanes.items()}

    part, q, k, v, mixed, n1, lse, ga, go, bd = attend(
        chain, image_mask, ln1_gain, ln1_bias, qv_bias, x, w3, w_out, cot, w_down
    )
    part_b = swapped(part)
    bits = [first[name] for name in ("D0", "D1", "U0", "U1")]
    act, gn2, ds0, ds1, dk0, dk1, us0, us1, uk0, uk1, bu = feed(
        chain, where, bits, out_bias, ln2_gain, ln2_bias, up_bias, x, part, part_b, go, w_up, ga
    )
    for name, keep, send in (("D0", dk0, ds0), ("D1", dk1, ds1), ("U0", uk0, us0), ("U1", uk1, us1)):
        lanes[name].begin(keep, send)
    gn2_b = swapped(gn2)
    qkv = (first["Q0"], first["Q1"])
    have = {}

    def compute(name):
        if name == "down":
            have["mlp"] = down(chain, act, w_down)
            have["mlpb"] = swapped(have["mlp"])
        elif name == "resid_back":
            have["gr"], have["gm"], have["s2"], have["og"] = resid_back(
                chain, x, part, part_b, out_bias, ln2_gain, gn2, gn2_b, go, mixed, w_out
            )
        elif name == "attend_back":
            have["grads"], have["bq"] = attend_back(chain, q, k, v, mixed, have["gm"], lse)
        elif name == "q_send":
            have["qs"] = qkv_grad(chain, where, n1, have["grads"], have["og"], qkv, 1)
        elif name == "q_keep":
            kept = qkv_grad(chain, where, n1, have["grads"], have["og"], qkv, 0)
            for i in range(2):
                lanes["Q%d" % i].begin(kept[i], have["qs"][i])
        elif name == "back_in":
            have["gn1"] = back_in(chain, have["grads"], w3, rows)
            have["gn1b"] = swapped(have["gn1"])
        elif name == "images_back":
            have["out"], have["pack"] = images_back(
                chain, x, ln1_gain, have["gr"], have["gn1"], have["gn1b"], bd, bu, have["s2"], have["bq"]
            )
        elif name == "block_out":
            have["block"] = block_out(chain, x, part, part_b, out_bias, have["mlp"], have["mlpb"], down_bias)
        elif name[:4] == "pack":
            have["pack"] = add(chain, have["pack"], lax.ppermute(have["pack"], "dp", xor_pairs(1 << int(name[4]))))
        elif name == "unpack":
            have["small"] = unpack(chain, have["pack"], hidden, local)

    for name in SCHEDULE:
        if name in lanes:
            lanes[name].step()
        else:
            compute(name)
    small = have["small"]
    return (
        have["block"].reshape(images.shape),
        have["out"].reshape(images.shape),
        small[0],
        small[1],
        jnp.transpose(projections.now.reshape(3, width, local), (1, 0, 2)),
        small[7],
        outs.now,
        small[2],
        small[3],
        small[4],
        ups.now,
        small[6],
        downs.now,
        small[5],
    )


def shards(*args):
    images, w_up = args[0], args[11]
    cube = lax.axis_size("dp") == 16 and lax.axis_size("tensor") == 2
    if cube and images.shape[0] == 1 and w_up.shape[1] == 2 * w_up.shape[0]:
        return shards_cube(*args)
    return shards_any(*args)


def solution(mesh):
    in_specs = (
        P("dp", None, None),
        P("dp"),
        P("dp", None, None),
        P(),
        P(),
        P(None, None, "tensor"),
        P(None, "tensor"),
        P("tensor", None),
        P(),
        P(),
        P(),
        P(None, "tensor"),
        P("tensor"),
        P("tensor", None),
        P(),
    )
    out_specs = (
        P("dp", None, None),
        P("dp", None, None),
        P(),
        P(),
        P(None, None, "tensor"),
        P(None, "tensor"),
        P("tensor", None),
        P(),
        P(),
        P(),
        P(None, "tensor"),
        P("tensor"),
        P("tensor", None),
        P(),
    )
    return jax.shard_map(shards, mesh=mesh, in_specs=in_specs, out_specs=out_specs, check_vma=False)
```

```python
import jax
import jax.numpy as jnp
from jax import lax
from jax.experimental import pallas as pl
from jax.experimental.pallas import tpu as pltpu
from jax.sharding import PartitionSpec as P

HD = 64
VALID = 577
EPS = 1e-06
BF = jnp.bfloat16
F32 = jnp.float32


def stats(values):
    mean = jnp.mean(values, axis=-1, keepdims=True)
    centred = values - mean
    spread = jnp.mean(centred * centred, axis=-1, keepdims=True)
    inv = lax.rsqrt(spread + EPS)
    return centred * inv, inv


def norm_back(unit, inv, gain, grad):
    scaled = grad * gain
    mean_a = jnp.mean(scaled, axis=-1, keepdims=True)
    mean_b = jnp.mean(scaled * unit, axis=-1, keepdims=True)
    return inv * (scaled - mean_a - unit * mean_b)


def inner_rows(left, right):
    return lax.dot_general(
        left, right, (((0,), (0,)), ((), ())), preferred_element_type=F32
    )


def times_back(left, weight):
    return lax.dot_general(
        left, weight, (((1,), (1,)), ((), ())), preferred_element_type=F32
    )


def score_block(query, keyset):
    raw = jnp.einsum("qhd,khd->hqk", query, keyset, preferred_element_type=F32)
    live = jnp.arange(raw.shape[-1]) < VALID
    return jnp.where(live, raw * HD ** (-0.5), -1e30)


def attend_forward(query, keyset, valueset):
    scores = score_block(query, keyset)
    peak = jnp.max(scores, axis=-1, keepdims=True)
    expo = jnp.exp(scores - peak)
    total = jnp.sum(expo, axis=-1, keepdims=True)
    probs = (expo / total).astype(BF)
    mixed = jnp.einsum("hqk,khd->qhd", probs, valueset, preferred_element_type=F32)
    return mixed.astype(BF), peak[..., 0] + jnp.log(total[..., 0])


def attend_backward(query, keyset, valueset, grad_mixed, logsum):
    scores = score_block(query, keyset)
    probs = jnp.exp(scores - logsum[..., None])
    grad_probs = jnp.einsum("qhd,khd->hqk", grad_mixed, valueset, preferred_element_type=F32)
    delta = jnp.sum(probs * grad_probs, axis=-1, keepdims=True)
    grad_scores = (probs * (grad_probs - delta) * HD ** (-0.5)).astype(BF)
    low_probs = probs.astype(BF)
    grad_value = jnp.einsum("hqk,qhd->khd", low_probs, grad_mixed, preferred_element_type=F32)
    grad_query = jnp.einsum("hqk,khd->qhd", grad_scores, keyset, preferred_element_type=F32)
    grad_key = jnp.einsum("hqk,qhd->khd", grad_scores, query, preferred_element_type=F32)
    return jnp.stack([grad_query, grad_key, grad_value], axis=1).astype(BF)


def swap_sum(part):
    if lax.axis_size("tensor") == 2:
        other = lax.ppermute(part, "tensor", [(0, 1), (1, 0)])
        return part.astype(F32) + other.astype(F32)
    return lax.psum(part.astype(F32), "tensor")


def xor_pairs(bit):
    return [(i, i ^ bit) for i in range(lax.axis_size("dp"))]


def bits_of():
    count = lax.axis_size("dp")
    bits = []
    while count > 1:
        if count % 2:
            raise ValueError("dp")
        bits.append(1 << len(bits))
        count //= 2
    return bits


def sum_small(vector):
    for bit in bits_of():
        vector = vector + lax.ppermute(vector, "dp", xor_pairs(bit))
    return vector


def cut_thirds(rows, turn):
    unit = 128
    whole = rows // unit
    base = whole // 3
    counts = [base + (1 if (i - turn) % 3 < whole % 3 else 0) for i in range(3)]
    return [c * unit for c in counts]


def sum_over_dp(matrix, turn):
    bits = bits_of()
    index = lax.axis_index("dp")
    halving = bits[: min(3, len(bits) - 1)]
    swaps = bits[len(halving) :]
    pieces, orders, start = [], [], 0
    for lane, rows in enumerate(cut_thirds(matrix.shape[0], turn)):
        if rows == 0:
            continue
        pieces.append(lax.slice_in_dim(matrix, start, start + rows, axis=0))
        turned = lane % len(halving)
        orders.append(halving[turned:] + halving[:turned])
        start += rows
    for step in range(len(halving)):
        for lane in range(len(pieces)):
            piece, bit = pieces[lane], orders[lane][step]
            half = piece.shape[0] // 2
            side = (index // bit) & 1
            kept = lax.dynamic_slice_in_dim(piece, side * half, half, 0)
            sent = lax.dynamic_slice_in_dim(piece, (1 - side) * half, half, 0)
            pieces[lane] = kept + lax.ppermute(sent, "dp", xor_pairs(bit))
    for bit in swaps:
        for lane in range(len(pieces)):
            pieces[lane] = pieces[lane] + lax.ppermute(pieces[lane], "dp", xor_pairs(bit))
    for step in reversed(range(len(halving))):
        for lane in range(len(pieces)):
            piece, bit = pieces[lane], orders[lane][step]
            other = lax.ppermute(piece, "dp", xor_pairs(bit))
            side = (index // bit) & 1
            pieces[lane] = jnp.where(
                side == 0,
                jnp.concatenate([piece, other], axis=0),
                jnp.concatenate([other, piece], axis=0),
            )
    return jnp.concatenate(pieces, axis=0).astype(F32)


def shards_any(
    images,
    image_mask,
    cotangent,
    ln1_gain,
    ln1_bias,
    w_qkv,
    qv_bias,
    w_out,
    out_bias,
    ln2_gain,
    ln2_bias,
    w_up,
    up_bias,
    w_down,
    down_bias,
):
    count, seq, width = images.shape
    rows = count * seq
    local = w_qkv.shape[2]
    heads = local // HD
    gain1 = ln1_gain.astype(F32)
    gain2 = ln2_gain.astype(F32)
    inputs = images.reshape(rows, width).astype(F32)
    keep = image_mask.astype(BF)[:, None, None]
    grad_out = (cotangent * keep).reshape(rows, width)
    w_qkv_flat = w_qkv.reshape(width, 3 * local)
    bias_row = jnp.concatenate([qv_bias[0], jnp.zeros_like(qv_bias[0]), qv_bias[1]]).astype(F32)

    unit1, inv1 = stats(inputs)
    normed1 = (unit1 * gain1 + ln1_bias.astype(F32)).astype(BF)
    qkv = (jnp.dot(normed1, w_qkv_flat, preferred_element_type=F32) + bias_row).astype(BF)
    split = qkv.reshape(count, seq, 3, heads, HD)
    attended = [attend_forward(split[i, :, 0], split[i, :, 1], split[i, :, 2]) for i in range(count)]
    mixed = jnp.concatenate([a[0] for a in attended], axis=0).reshape(rows, local)
    attn = swap_sum(jnp.dot(mixed, w_out, preferred_element_type=F32).astype(BF))
    grad_act = times_back(grad_out, w_down)
    resid = inputs + attn + out_bias.astype(F32)
    unit2, inv2 = stats(resid)
    normed2 = (unit2 * gain2 + ln2_bias.astype(F32)).astype(BF)
    pre = jnp.dot(normed2, w_up, preferred_element_type=F32) + up_bias.astype(F32)
    cdf = 0.5 * (1.0 + lax.erf(pre * (0.5**0.5)))
    act = (pre * cdf).astype(BF)
    slope = cdf + pre * jnp.exp(-0.5 * pre * pre) * ((0.5 / jnp.pi) ** 0.5)
    grad_pre = (grad_act * slope).astype(BF)
    grad_wdown = inner_rows(act, grad_out).astype(BF)
    summed_wdown = sum_over_dp(grad_wdown, 0)
    grad_wup = inner_rows(normed2, grad_pre).astype(BF)
    summed_wup = sum_over_dp(grad_wup, 1)
    grad_normed2 = swap_sum(times_back(grad_pre, w_up).astype(BF))
    mlp = swap_sum(jnp.dot(act, w_down, preferred_element_type=F32).astype(BF))
    block_output = (resid + mlp + down_bias.astype(F32)).astype(BF).reshape(images.shape)
    grad_resid = grad_out.astype(F32) + norm_back(unit2, inv2, gain2, grad_normed2)
    resid_low = grad_resid.astype(BF)
    grad_wout = inner_rows(mixed, resid_low).astype(BF)
    summed_wout = sum_over_dp(grad_wout, 2)
    grad_mixed = times_back(resid_low, w_out).astype(BF).reshape(count, seq, heads, HD)
    grad_qkv = jnp.concatenate(
        [
            attend_backward(split[i, :, 0], split[i, :, 1], split[i, :, 2], grad_mixed[i], attended[i][1])
            for i in range(count)
        ],
        axis=0,
    ).reshape(rows, 3 * local)
    grad_wqkv = inner_rows(normed1, grad_qkv).astype(BF)
    summed_wqkv = sum_over_dp(grad_wqkv, 0).reshape(width, 3, local)
    bias_sums = jnp.sum(grad_qkv.astype(F32), axis=0)
    grad_normed1 = swap_sum(times_back(grad_qkv, w_qkv_flat).astype(BF))
    images_grad = (
        (grad_resid + norm_back(unit1, inv1, gain1, grad_normed1)).astype(BF).reshape(images.shape)
    )

    small = [
        jnp.sum(grad_normed1 * unit1, axis=0),
        jnp.sum(grad_normed1, axis=0),
        jnp.sum(grad_resid, axis=0),
        jnp.sum(grad_normed2 * unit2, axis=0),
        jnp.sum(grad_normed2, axis=0),
        jnp.sum(grad_out.astype(F32), axis=0),
        jnp.sum(grad_pre.astype(F32), axis=0),
        bias_sums[:local],
        bias_sums[2 * local :],
    ]
    flat = jnp.concatenate(small)
    length = flat.shape[0]
    padded = -(-length // 1024) * 1024
    flat = sum_small(jnp.pad(flat, (0, padded - length)).reshape(padded // 128, 128)).reshape(-1)
    out, at = [], 0
    for part in small:
        out.append(flat[at : at + part.shape[0]])
        at += part.shape[0]
    return (
        block_output,
        images_grad,
        out[0],
        out[1],
        summed_wqkv,
        jnp.stack([out[7], out[8]]),
        summed_wout,
        out[2],
        out[3],
        out[4],
        summed_wup,
        out[6],
        summed_wdown,
        out[5],
    )


CHUNKS = 2
ANY = pl.BlockSpec(memory_space=pl.ANY)
HBM = pl.BlockSpec(memory_space=pltpu.HBM)
VM = pl.BlockSpec(memory_space=pltpu.VMEM)
MIB = 1024 * 1024


def shape_of(shape, dtype):
    return jax.ShapeDtypeStruct(shape, dtype)


def nn(left, right):
    return jnp.dot(left, right, preferred_element_type=F32)


def normal_unit(values):
    mean = jnp.mean(values, axis=-1, keepdims=True)
    centred = values - mean
    spread = jnp.mean(centred * centred, axis=-1, keepdims=True)
    inv = lax.rsqrt(spread + EPS)
    return centred * inv, inv


def row_of(ref):
    return ref[...].astype(F32).reshape(1, ref.shape[0])


def side_of(where_ref, bits):
    bit = bits[0] if bits[0] == bits[1] else jnp.where(where_ref[1] == 0, bits[0], bits[1])
    return (where_ref[0] >> bit) & 1


class Chain:
    def __init__(self):
        self.last = None

    def __call__(
        self, body, args, in_specs, outs, out_specs, scratch=(), grid=(), vmem=40, aliases=None, name=None, prefetch=0, cost=0.001
    ):
        args, in_specs, run = list(args), list(in_specs), body
        if self.last is not None:
            spot = len(args)

            def run(*refs):
                body(*refs[:spot], *refs[spot + 1 :])

            args.append(self.last)
            in_specs.append(ANY)
        spec = pltpu.PrefetchScalarGridSpec(
            num_scalar_prefetch=prefetch,
            grid=grid,
            in_specs=in_specs,
            out_specs=out_specs,
            scratch_shapes=list(scratch),
        )
        made = pl.pallas_call(
            run,
            out_shape=outs,
            grid_spec=spec,
            input_output_aliases=aliases or {},
            compiler_params=pltpu.CompilerParams(vmem_limit_bytes=vmem * MIB),
            cost_estimate=pl.CostEstimate(flops=0, bytes_accessed=int(cost * 3e6), transcendentals=0),
            name=name,
        )(*args)
        self.last = made[0] if isinstance(made, (tuple, list)) else made
        return made


def row_chunks(rows):
    units, parts = rows // 16, CHUNKS
    cuts = [16 * (units * i // parts) for i in range(parts)] + [rows]
    return [(cuts[i], cuts[i + 1] - cuts[i]) for i in range(parts)]


def lane_halves():
    return lax.broadcasted_iota(jnp.int32, (1, 2 * HD), 1) < HD


def key_mask(length):
    return jnp.where(lax.broadcasted_iota(jnp.int32, (1, length), 1) < VALID, 0.0, -1e30)


def copier(sems):
    count = [0]

    def copy(source, target):
        made = pltpu.make_async_copy(source, target, sems.at[count[0]])
        count[0] += 1
        made.start()
        return made

    return copy


def attend_kernel(
    mask_ref, g_ref, s_ref, b_ref, x_ref, w_ref, wo_ref, cot_ref, wd_ref,
    part_ref, q_ref, k_ref, v_ref, mixed_ref, n1_ref, lse_ref, ga_ref, go_ref, bd_ref,
    x_b, w_b, wo_b, cot_b, wd_b, part_b, q_b, k_b, v_b, mixed_b, n1_b, lse_b, ga_b, go_b, sems,
):
    rows, width = x_ref.shape
    padded, local = q_ref.shape
    pairs = local // 128
    deep = wd_ref.shape[0] // pairs
    copy = copier(sems)
    get_x = copy(x_ref, x_b)
    get_w = [copy(w_ref.at[c], w_b.at[c]) for c in range(3)]
    get_cot = copy(cot_ref, cot_b)
    get_wd = [copy(wd_ref.at[pl.ds(i * deep, deep)], wd_b.at[i]) for i in range(pairs)]
    get_wo = copy(wo_ref, wo_b)
    puts = []
    get_x.wait()
    unit, _ = normal_unit(x_b[...].astype(F32))
    normed = unit * row_of(g_ref) + row_of(s_ref)
    n1_b[...] = jnp.concatenate([normed, jnp.zeros((padded - rows, width), F32)], axis=0).astype(BF)
    puts.append(copy(n1_b, n1_ref))
    lse_b[...] = jnp.zeros(lse_b.shape, F32)
    live = lax.broadcasted_iota(jnp.int32, (padded, 1), 0) < rows
    for c, (buf, ref, scale) in enumerate(((q_b, q_ref, HD ** (-0.5)), (k_b, k_ref, 1.0), (v_b, v_ref, 1.0))):
        get_w[c].wait()
        for at in range(0, local, 256):
            made = nn(n1_b[...], w_b[c, :, at : at + 256])
            if c != 1:
                made = made + b_ref[c // 2 : c // 2 + 1, at : at + 256].astype(F32)
            made = jnp.where(live, made, 0.0).astype(BF)
            buf[:, at : at + 256] = made * jnp.asarray(scale, BF)
        puts.append(copy(buf, ref))
    get_cot.wait()
    masked = cot_b[...].astype(F32) * mask_ref[0].astype(F32)
    go_b[...] = masked.astype(BF)
    puts.append(copy(go_b, go_ref))
    bd_ref[...] = jnp.sum(masked, axis=0, keepdims=True)
    for get in get_wd:
        get.wait()
    mask = key_mask(padded)
    first = lane_halves()
    lane = lax.broadcasted_iota(jnp.int32, (1, 128), 1)

    def pair(p, carry):
        cols = pl.ds(pl.multiple_of(p * 128, 128), 128)
        keys, vals = k_b[:, cols], v_b[:, cols]
        query = q_b[:, cols]
        zero, ones = jnp.zeros_like(keys), jnp.ones_like(vals)
        own_k = (jnp.where(first, keys, zero), jnp.where(first, zero, keys))
        own_v = (jnp.where(first, vals, ones), jnp.where(first, ones, vals))
        ga_b[:, pl.ds(pl.multiple_of(p * deep, deep), deep)] = times_back(go_b[...], wd_b[p]).astype(BF)
        outs = []
        logs = lse_b[...]
        for h in range(2):
            scores = times_back(query, own_k[h]) + mask
            peak = jnp.max(scores, axis=-1, keepdims=True)
            made = nn(jnp.exp(scores - peak).astype(BF), own_v[h])
            total = made[:, HD : HD + 1] if h == 0 else made[:, 0:1]
            outs.append(made * (1.0 / total))
            logs = jnp.where(lane == 2 * p + h, peak + jnp.log(total), logs)
        lse_b[...] = logs
        mixed_b[:, cols] = jnp.where(first, outs[0], outs[1]).astype(BF)
        return carry

    lax.fori_loop(0, pairs, pair, 0)
    puts += [copy(ga_b, ga_ref), copy(mixed_b, mixed_ref), copy(lse_b, lse_ref)]
    get_wo.wait()
    for at in range(0, width, 256):
        made = nn(mixed_b[...], wo_b[:, at : at + 256])
        part_b[:, at : at + 256] = made[:rows].astype(BF)
    puts.append(copy(part_b, part_ref))
    for put in puts:
        put.wait()


def attend(chain, mask, gain, shift, bias, x, w3, w_out, cot, w_down):
    rows, width = x.shape
    local = w3.shape[2]
    hidden = w_down.shape[0]
    padded = -(-rows // 16) * 16
    pairs = local // 128
    slab = ((rows, width), BF)
    wide = ((padded, local), BF)
    outs = (slab, wide, wide, wide, wide, ((padded, width), BF), ((padded, 128), F32), ((rows, hidden), BF), slab)
    held = (slab, ((3, width, local), BF), ((local, width), BF), slab, ((pairs, hidden // pairs, width), BF)) + outs
    return chain(
        attend_kernel,
        (mask, gain, shift, bias, x, w3, w_out, cot, w_down),
        [VM] * 3 + [HBM] * 5,
        tuple(shape_of(*out) for out in outs) + (shape_of((1, width), F32),),
        (HBM,) * len(outs) + (VM,),
        [pltpu.VMEM(*hold) for hold in held] + [pltpu.SemaphoreType.DMA((7 + pairs + len(outs),))],
        name="attend",
        vmem=60,
        prefetch=1,
    )


def gelu_pair(pre):
    bell = jnp.exp(-0.5 * pre * pre)
    near = 1.0 / (1.0 + (0.3275911 * 0.5**0.5) * jnp.abs(pre))
    poly = near * (
        0.254829592 + near * (-0.284496736 + near * (1.421413741 + near * (-1.453152027 + near * 1.061405429)))
    )
    tail = 0.5 * poly * bell
    cdf = jnp.where(pre < 0, tail, 1.0 - tail)
    return cdf, cdf + pre * bell * ((0.5 / jnp.pi) ** 0.5)


def feed_kernel(
    where_ref, ob_ref, g_ref, s_ref, ub_ref, x_ref, pa_ref, pb_ref, go_ref, wu_ref, ga_ref,
    act_ref, gn_ref, ds0_ref, ds1_ref, dk0_ref, dk1_ref, us0_ref, us1_ref, uk0_ref, uk1_ref, bu_ref,
    x_b, pa_b, pb_b, go_b, wu_b, ga_b, act_b, n2_b, down_b, up_b, gn_b, total, bias, sems, *, bits,
):
    rows, width = x_ref.shape
    hidden = wu_ref.shape[1]
    size = hidden // 4
    tall = width // 4
    sides = [side_of(where_ref, bit) for bit in bits]
    starts = [pl.multiple_of((2 * lane + (1 - sides[lane])) * size, size) for lane in range(2)]
    starts += [pl.multiple_of((2 * lane + sides[lane]) * size, size) for lane in range(2)]
    tops = [pl.multiple_of((2 * lane + (1 - sides[2 + lane])) * tall, tall) for lane in range(2)]
    tops += [pl.multiple_of((2 * lane + sides[2 + lane]) * tall, tall) for lane in range(2)]
    copy = copier(sems)
    gets = [copy(x_ref, x_b), copy(pa_ref, pa_b), copy(pb_ref, pb_b)]
    get_w, get_ga = [], []
    for c in range(4):
        get_w.append(copy(wu_ref.at[:, pl.ds(starts[c], size)], wu_b.at[c]))
        get_ga.append(copy(ga_ref.at[:, pl.ds(starts[c], size)], ga_b.at[c]))
        if c == 0:
            get_go = copy(go_ref, go_b)
    puts = []
    bias[...] = row_of(ub_ref)
    for get in gets:
        get.wait()
    resid = x_b[...].astype(F32) + (pa_b[...].astype(F32) + pb_b[...].astype(F32)) + row_of(ob_ref)
    unit, _ = normal_unit(resid)
    n2_b[...] = (unit * row_of(g_ref) + row_of(s_ref)).astype(BF)

    def front(c):
        get_w[c].wait()
        get_ga[c].wait()
        for at in range(0, size, 256):
            cols = pl.ds(pl.multiple_of(starts[c] + at, 256), 256)
            pre = nn(n2_b[...], wu_b[c, :, at : at + 256]) + bias[:, cols]
            cdf, slope = gelu_pair(pre)
            act_b[c, :, at : at + 256] = (pre * cdf).astype(BF)
            grad_pre = (ga_b[c, :, at : at + 256].astype(F32) * slope).astype(BF)
            ga_b[c, :, at : at + 256] = grad_pre
            bu_ref[:, cols] = jnp.sum(grad_pre.astype(F32), axis=0, keepdims=True)
        puts.append(copy(act_b.at[c], act_ref.at[:, pl.ds(starts[c], size)]))

    def back(c):
        if c == 0:
            get_go.wait()
        for at in range(0, width, 512):
            made = inner_rows(act_b[c], go_b[:, at : at + 512])
            down_b[c, :, at : at + 512] = made.astype(BF)
        puts.append(copy(down_b.at[c], (ds0_ref, ds1_ref, dk0_ref, dk1_ref)[c]))
        for piece in range(4):
            made = inner_rows(n2_b[:, pl.ds(tops[piece], tall)], ga_b[c])
            up_b[piece, :, pl.ds(starts[c], size)] = made.astype(BF)
        for at in range(0, width, 512):
            made = times_back(ga_b[c], wu_b[c, at : at + 512, :])
            if c:
                made = made + total[:, at : at + 512]
            if c < 3:
                total[:, at : at + 512] = made
            else:
                gn_b[:, at : at + 512] = made.astype(BF)

    for c in range(5):
        if c < 4:
            front(c)
        if c:
            back(c - 1)
    puts.append(copy(gn_b, gn_ref))
    for piece, ref in enumerate((us0_ref, us1_ref, uk0_ref, uk1_ref)):
        puts.append(copy(up_b.at[piece], ref))
    for put in puts:
        put.wait()


def feed(chain, where, bits, out_bias, gain, shift, up_bias, x, pa, pb, go, w_up, ga):
    rows, width = x.shape
    hidden = w_up.shape[1]

    def body(*refs):
        feed_kernel(*refs, bits=bits)

    slab = ((rows, width), BF)
    deep = ((4, rows, hidden // 4), BF)
    outs = (((rows, hidden), BF), slab) + (((hidden // 4, width), BF),) * 4 + (((width // 4, hidden), BF),) * 4
    held = (slab,) * 4 + (((4, width, hidden // 4), BF), deep, deep, slab, ((4, hidden // 4, width), BF))
    held += (((4, width // 4, hidden), BF), slab, ((rows, width), F32), ((1, hidden), F32))
    return chain(
        body,
        (where, out_bias, gain, shift, up_bias, x, pa, pb, go, w_up, ga),
        [VM] * 4 + [HBM] * 6,
        tuple(shape_of(*out) for out in outs) + (shape_of((1, hidden), F32),),
        (HBM,) * len(outs) + (VM,),
        [pltpu.VMEM(*hold) for hold in held] + [pltpu.SemaphoreType.DMA((12 + 4 + len(outs),))],
        name="feed",
        vmem=60,
        prefetch=1,
    )


def qkv_grad(chain, where, n1, grads, out_grad, bits, flip):
    width = n1.shape[1]
    local = grads.shape[1] // 3
    size = width // 4

    def body(where_ref, n1_ref, g_ref, o_ref, first_ref, second_ref):
        def product(ref, start):
            for i in range(4):
                made = inner_rows(n1_ref[:, i * size : (i + 1) * size], g_ref[:, pl.ds(start, local)])
                ref[i * size : (i + 1) * size, :] = made.astype(BF)

        product(first_ref, pl.multiple_of((side_of(where_ref, bits[0]) ^ flip) * local, local))
        which = side_of(where_ref, bits[1]) ^ flip

        @pl.when(which == 0)
        def _():
            product(second_ref, 2 * local)

        @pl.when(which == 1)
        def _():
            second_ref[...] = o_ref[...]

    return chain(
        body,
        (where, n1, grads, out_grad),
        [VM, VM, VM],
        (shape_of((width, local), BF),) * 2,
        (VM,) * 2,
        name="qkv_grad",
        prefetch=1,
    )


TILES = 4


def paired(own, other):
    return own[...].astype(F32) + other[...].astype(F32)


def down(chain, act, w_down):
    rows, hidden = act.shape
    width = w_down.shape[1]
    size = width // TILES
    deep = hidden // TILES

    def body(act_ref, w_ref, *rest):
        out_ref, w_buf, sems = rest
        copies = [
            pltpu.make_async_copy(w_ref.at[pl.ds(i * deep, deep)], w_buf.at[pl.ds(i * deep, deep)], sems.at[i])
            for i in range(TILES)
        ]
        for copy in copies:
            copy.start()
        for copy in copies:
            copy.wait()
        for i in range(TILES):
            out_ref[:, i * size : (i + 1) * size] = nn(act_ref[...], w_buf[:, i * size : (i + 1) * size]).astype(BF)

    return chain(
        body,
        (act, w_down),
        [VM, HBM],
        shape_of((rows, width), BF),
        VM,
        [pltpu.VMEM((hidden, width), BF), pltpu.SemaphoreType.DMA((TILES,))],
        name="down",
    )


def resid_back_kernel(
    x_ref, pa_ref, pb_ref, ob_ref, g_ref, ga_ref, gb_ref, go_ref, mixed_ref, wo_ref, gr_ref, gm_ref, sums_ref, og_ref, low
):
    rows, width = x_ref.shape
    padded, local = mixed_ref.shape
    resid = x_ref[...].astype(F32) + (pa_ref[...].astype(F32) + pb_ref[...].astype(F32)) + row_of(ob_ref)
    unit, inv = normal_unit(resid)
    grad = paired(ga_ref, gb_ref)
    total = go_ref[...].astype(F32) + norm_back(unit, inv, row_of(g_ref), grad)
    gr_ref[...] = total
    low[...] = jnp.concatenate([total, jnp.zeros((padded - rows, width), F32)], axis=0).astype(BF)
    sums_ref[...] = jnp.concatenate(
        [
            jnp.sum(total, axis=0, keepdims=True),
            jnp.sum(grad * unit, axis=0, keepdims=True),
            jnp.sum(grad, axis=0, keepdims=True),
            jnp.zeros((5, width), F32),
        ],
        axis=0,
    )
    for i in range(2):
        for at in range(0, width // 2, 256):
            start = i * width // 2 + at
            made = inner_rows(mixed_ref[...], low[:, start : start + 256])
            og_ref[i * local : (i + 1) * local, at : at + 256] = made.astype(BF)
    for at in range(0, local, 256):
        gm_ref[:, at : at + 256] = times_back(low[...], wo_ref[at : at + 256, :]).astype(BF)


def resid_back(chain, x, pa, pb, out_bias, gain, ga, gb, go, mixed, w_out):
    rows, width = x.shape
    padded, local = mixed.shape
    return chain(
        resid_back_kernel,
        (x, pa, pb, out_bias, gain, ga, gb, go, mixed, w_out),
        [VM] * 10,
        (
            shape_of((rows, width), F32),
            shape_of((padded, local), BF),
            shape_of((8, width), F32),
            shape_of((2 * local, width // 2), BF),
        ),
        (VM,) * 4,
        [pltpu.VMEM((padded, width), BF)],
        name="resid_back",
    )


def attend_back_kernel(q_ref, k_ref, v_ref, mixed_ref, gm_ref, lse_ref, out_ref, bias_ref, probs_s, slopes_s):
    padded, local = q_ref.shape
    mask = key_mask(padded)
    first = lane_halves()
    lane = lax.broadcasted_iota(jnp.int32, (1, 128), 1)

    def pair(p, carry):
        cols = pl.ds(pl.multiple_of(p * 128, 128), 128)
        keys, vals = k_ref[:, cols], v_ref[:, cols]
        zero = jnp.zeros_like(keys)
        own_k = (jnp.where(first, keys, zero), jnp.where(first, zero, keys))
        own_v = (jnp.where(first, vals, zero), jnp.where(first, zero, vals))
        for at, size in row_chunks(padded):
            query = q_ref[at : at + size, cols]
            grad = gm_ref[at : at + size, cols]
            both = grad.astype(F32) * mixed_ref[at : at + size, cols].astype(F32)
            logs = lse_ref[at : at + size, :]
            outs = []
            for h in range(2):
                own_lanes = first if h == 0 else jnp.logical_not(first)
                delta = jnp.sum(jnp.where(own_lanes, both, 0.0), axis=-1, keepdims=True)
                log = jnp.sum(jnp.where(lane == 2 * p + h, logs, 0.0), axis=-1, keepdims=True)
                probs = jnp.exp(times_back(query, own_k[h]) + mask - log)
                slope = (probs * (times_back(grad, own_v[h]) - delta)).astype(BF)
                probs_s[h, at : at + size, :] = probs.astype(BF)
                slopes_s[h, at : at + size, :] = slope
                outs.append(nn(slope, keys))
            out_ref[at : at + size, cols] = (jnp.where(first, outs[0], outs[1]) * HD ** (-0.5)).astype(BF)
        grad_t = gm_ref[:, cols].astype(F32).T.astype(BF)
        query_t = q_ref[:, cols].astype(F32).T.astype(BF)
        grad_k = [nn(query_t[HD * h : HD * h + HD], slopes_s[h]) for h in range(2)]
        grad_v = [nn(grad_t[HD * h : HD * h + HD], probs_s[h]) for h in range(2)]
        cols_k = pl.ds(pl.multiple_of(local + p * 128, 128), 128)
        cols_v = pl.ds(pl.multiple_of(2 * local + p * 128, 128), 128)
        out_ref[:, cols_k] = jnp.concatenate(grad_k, axis=0).T.astype(BF)
        out_ref[:, cols_v] = jnp.concatenate(grad_v, axis=0).T.astype(BF)
        return carry

    lax.fori_loop(0, local // 128, pair, 0)
    bias_ref[...] = jnp.sum(out_ref[...].astype(F32), axis=0, keepdims=True)


def attend_back(chain, q, k, v, mixed, gm, lse):
    padded, local = q.shape
    return chain(
        attend_back_kernel,
        (q, k, v, mixed, gm, lse),
        [VM] * 6,
        (shape_of((padded, 3 * local), BF), shape_of((1, 3 * local), F32)),
        (VM, VM),
        [pltpu.VMEM((2, padded, padded), BF), pltpu.VMEM((2, padded, padded), BF)],
        name="attend_back",
    )


def back_in(chain, grads, w3, rows):
    _, width, local = w3.shape
    size = width // TILES

    def body(g_ref, w_ref, *rest):
        out_ref, w_buf, sems = rest
        copies = [
            pltpu.make_async_copy(w_ref.at[:, pl.ds(i * size, size)], w_buf.at[i], sems.at[i]) for i in range(TILES)
        ]
        for copy in copies:
            copy.start()
        for i in range(TILES):
            copies[i].wait()
            total = times_back(g_ref[:, :local], w_buf[i, 0])
            for c in range(1, 3):
                total += times_back(g_ref[:, c * local : (c + 1) * local], w_buf[i, c])
            out_ref[:, i * size : (i + 1) * size] = total[:rows].astype(BF)

    return chain(
        body,
        (grads, w3),
        [VM, HBM],
        shape_of((rows, width), BF),
        VM,
        [pltpu.VMEM((TILES, 3, size, local), BF), pltpu.SemaphoreType.DMA((TILES,))],
        name="back_in",
    )


def images_back_kernel(x_ref, g_ref, gr_ref, ga_ref, gb_ref, bd_ref, bu_ref, s2_ref, bq_ref, out_ref, pack_ref):
    unit, inv = normal_unit(x_ref[...].astype(F32))
    grad = paired(ga_ref, gb_ref)
    out_ref[...] = (gr_ref[...] + norm_back(unit, inv, row_of(g_ref), grad)).astype(BF)
    width = x_ref.shape[1]
    hidden = bu_ref.shape[1]
    local = bq_ref.shape[1] // 3
    pack_ref[0:1, :] = jnp.sum(grad * unit, axis=0, keepdims=True)
    pack_ref[1:2, :] = jnp.sum(grad, axis=0, keepdims=True)
    pack_ref[2:5, :] = s2_ref[0:3, :]
    pack_ref[5:6, :] = bd_ref[...]
    for i in range(hidden // width):
        pack_ref[6 + i : 7 + i, :] = bu_ref[:, i * width : (i + 1) * width]
    after = 6 + hidden // width
    pack_ref[after : after + 1, :local] = bq_ref[:, :local]
    pack_ref[after : after + 1, local:] = bq_ref[:, 2 * local :]
    pack_ref[after + 1 :, :] = jnp.zeros((pack_ref.shape[0] - after - 1, width), F32)


def images_back(chain, x, gain, gr, ga, gb, bd, bu, s2, bq):
    return chain(
        images_back_kernel,
        (x, gain, gr, ga, gb, bd, bu, s2, bq),
        [VM] * 9,
        (shape_of(x.shape, BF), shape_of((16, x.shape[1]), F32)),
        (VM, VM),
        name="images_back",
    )


def block_out_kernel(x_ref, pa_ref, pb_ref, ob_ref, ma_ref, mb_ref, db_ref, out_ref):
    resid = x_ref[...].astype(F32) + (pa_ref[...].astype(F32) + pb_ref[...].astype(F32)) + row_of(ob_ref)
    out_ref[...] = (resid + paired(ma_ref, mb_ref) + row_of(db_ref)).astype(BF)


def block_out(chain, x, pa, pb, out_bias, ma, mb, down_bias):
    return chain(
        block_out_kernel,
        (x, pa, pb, out_bias, ma, mb, down_bias),
        [VM] * 7,
        shape_of(x.shape, BF), VM, name="block_out"
    )


def add_split_kernel(where_ref, k0_ref, k1_ref, r0_ref, r1_ref, send_ref, keep_ref):
    keep_ref[...] = (k0_ref[...].astype(F32) + r0_ref[...].astype(F32)).astype(BF)
    send_ref[...] = (k1_ref[...].astype(F32) + r1_ref[...].astype(F32)).astype(BF)


def add_split(chain, where, bit, keep, recv):
    rows, width = keep.shape
    half = rows // 2
    block = (half, width)
    own = pl.BlockSpec(block, lambda i, w: (side_of(w, bit), 0))
    other = pl.BlockSpec(block, lambda i, w: (1 - side_of(w, bit), 0))
    out = pl.BlockSpec(block, lambda i, w: (0, 0))
    return chain(
        add_split_kernel,
        (where, keep, keep, recv, recv),
        [own, other, own, other],
        (shape_of((half, width), BF),) * 2,
        (out, out),
        grid=(1,),
        name="add_split",
        prefetch=1,
        vmem=16,
    )


def add_kernel(a_ref, b_ref, out_ref):
    out_ref[...] = (a_ref[...].astype(F32) + b_ref[...].astype(F32)).astype(out_ref.dtype)


def add(chain, a, b):
    return chain(add_kernel, (a, b), [VM, VM], shape_of(a.shape, a.dtype), VM, name="add", vmem=16)


def join(chain, where, bit, own, other):
    half, width = own.shape

    def body(where_ref, own_ref, other_ref, out_ref):
        side = side_of(where_ref, bit)
        out_ref[pl.ds(pl.multiple_of(side * half, 16), half), :] = own_ref[...]
        out_ref[pl.ds(pl.multiple_of((1 - side) * half, 16), half), :] = other_ref[...]

    return chain(
        body,
        (where, own, other),
        [VM, VM],
        shape_of((2 * half, width), BF),
        VM,
        name="join",
        prefetch=1,
        vmem=16,
    )


class Home:
    def __init__(self, shape):
        self.shape, self.now = shape, None


def finish(chain, where, bits, flip, piece, homes):
    half, width = piece.shape
    parts = 4
    block = half // parts
    targets = list(dict.fromkeys(home for home, _ in homes))
    old = [home for home in targets if home.now is not None]

    def body(where_ref, piece_ref, *rest):
        outs = rest[len(old) : len(old) + len(targets)]
        made, sems = rest[-2:]
        which = side_of(where_ref, bits) ^ flip

        def write(number):
            home, row = homes[number]
            out_ref = outs[targets.index(home)]
            copies = []
            for i in range(parts):
                made[i * block : (i + 1) * block, :] = piece_ref[i * block : (i + 1) * block, :].astype(F32)
                if home.shape[1] == width:
                    place = out_ref.at[pl.ds(row + i * block, block)]
                else:
                    high = home.shape[0]
                    place = out_ref.at[pl.ds(i * block % high, block), pl.ds(i * block // high * width, width)]
                copies.append(pltpu.make_async_copy(made.at[pl.ds(i * block, block)], place, sems.at[i]))
                copies[-1].start()
            for copy in copies:
                copy.wait()

        for number in range(2):

            @pl.when(which == number)
            def _(number=number):
                write(number)

    made = chain(
        body,
        (where, piece, *(home.now for home in old)),
        [VM] + [HBM] * len(old),
        tuple(shape_of(home.shape, F32) for home in targets) + (shape_of((8, 128), F32),),
        (HBM,) * (len(targets) + 1),
        [pltpu.VMEM((half, width), F32), pltpu.SemaphoreType.DMA((parts,))],
        aliases={2 + i: targets.index(home) for i, home in enumerate(old)},
        name="finish",
        prefetch=1,
        vmem=16,
    )
    for home, now in zip(targets, made[:-1], strict=True):
        home.now = now
    chain.last = made[-1]


def unpack(chain, pack, hidden, local):
    width = pack.shape[1]
    steps = hidden // width

    def body(pack_ref, *outs):
        for i in range(6):
            outs[i][...] = pack_ref[i, :]
        for i in range(steps):
            outs[6][i * width : (i + 1) * width] = pack_ref[6 + i, :]
        for i in range(2):
            outs[7][i : i + 1, :] = pack_ref[6 + steps : 7 + steps, i * local : (i + 1) * local]

    line = shape_of((width,), F32)
    return chain(
        body,
        (pack,),
        [VM],
        (line,) * 6 + (shape_of((hidden,), F32), shape_of((2, local), F32)),
        (VM,) * 8,
        name="unpack",
    )


class Lane:
    def __init__(self, chain, where, order, homes):
        self.chain, self.where, self.homes = chain, where, homes
        self.bits = list(zip(*order, strict=True))
        self.keep = self.send = None
        self.stage = 0

    def begin(self, keep, send):
        self.keep, self.send = keep, send

    def over(self, bits, piece):
        pairs = [
            (2 * i + core, 2 * (i ^ (1 << bits[core])) + core) for i in range(lax.axis_size("dp")) for core in range(2)
        ]
        return lax.ppermute(piece, ("dp", "tensor"), pairs)

    def step(self):
        stage, bits, chain = self.stage, self.bits, self.chain
        self.stage += 1
        if stage < 2:
            recv = self.over(bits[stage], self.send)
            self.send, self.keep = add_split(chain, self.where, bits[stage + 1], self.keep, recv)
        elif stage == 2:
            self.keep = add(chain, self.keep, self.over(bits[2], self.send))
        elif stage == 3:
            self.keep = add(chain, self.keep, self.over((3, 3), self.keep))
        elif stage < 6:
            bit = bits[6 - stage]
            self.keep = join(chain, self.where, bit, self.keep, self.over(bit, self.keep))
        elif stage == 6:
            self.send = self.over(bits[0], self.keep)
            finish(chain, self.where, bits[0], 0, self.keep, self.homes)
        else:
            finish(chain, self.where, bits[0], 1, self.send, self.homes)


ORDERS = {
    "D0": ((0, 1, 2), (1, 0, 2)),
    "D1": ((0, 1, 2), (2, 0, 1)),
    "U0": ((2, 1, 0), (1, 0, 2)),
    "U1": ((1, 0, 2), (2, 1, 0)),
    "Q0": ((0, 1, 2), (0, 1, 2)),
    "Q1": ((1, 0, 2), (2, 1, 0)),
}
SCHEDULE = (
    "down", "resid_back", "U0", "attend_back", "q_send", "D0", "U0", "back_in", "D0", "D1", "U1", "D0",
    "U0", "q_keep", "Q1", "D0", "Q0", "U0", "U1", "images_back", "Q0", "D1", "U0", "U1", "Q1", "pack0",
    "Q0", "U1", "D1", "D0", "pack1", "Q0", "U0", "Q1", "U1", "U0", "D0", "Q1", "U1", "pack2", "D1",
    "Q0", "block_out", "D1", "pack3", "Q1", "Q0", "D0", "D0", "Q0", "Q1", "U1", "D1", "D1", "U1", "U0",
    "Q0", "unpack", "Q1", "D1", "Q1",
)


def shards_cube(
    images,
    image_mask,
    cotangent,
    ln1_gain,
    ln1_bias,
    w_qkv,
    qv_bias,
    w_out,
    out_bias,
    ln2_gain,
    ln2_bias,
    w_up,
    up_bias,
    w_down,
    down_bias,
):
    _, rows, width = images.shape
    local = w_qkv.shape[2]
    hidden = w_up.shape[1]
    x = images.reshape(rows, width)
    cot = cotangent.reshape(rows, width)
    where = jnp.stack([lax.axis_index("dp"), lax.axis_index("tensor")]).astype(jnp.int32)
    w3 = jnp.transpose(w_qkv, (1, 0, 2))
    chain = Chain()

    def swapped(piece):
        return lax.ppermute(piece, "tensor", [(0, 1), (1, 0)])

    downs, ups, outs = Home((hidden, width)), Home((width, hidden)), Home((local, width))
    projections = Home((3 * width, local))
    places = {
        "D0": ((downs, 0), (downs, hidden // 4)),
        "D1": ((downs, hidden // 2), (downs, 3 * hidden // 4)),
        "U0": ((ups, 0), (ups, width // 4)),
        "U1": ((ups, width // 2), (ups, 3 * width // 4)),
        "Q0": ((projections, 0), (projections, width)),
        "Q1": ((projections, 2 * width), (outs, 0)),
    }
    lanes = {name: Lane(chain, where, ORDERS[name], homes) for name, homes in places.items()}
    first = {name: lane.bits[0] for name, lane in lanes.items()}

    part, q, k, v, mixed, n1, lse, ga, go, bd = attend(
        chain, image_mask, ln1_gain, ln1_bias, qv_bias, x, w3, w_out, cot, w_down
    )
    part_b = swapped(part)
    bits = [first[name] for name in ("D0", "D1", "U0", "U1")]
    act, gn2, ds0, ds1, dk0, dk1, us0, us1, uk0, uk1, bu = feed(
        chain, where, bits, out_bias, ln2_gain, ln2_bias, up_bias, x, part, part_b, go, w_up, ga
    )
    for name, keep, send in (("D0", dk0, ds0), ("D1", dk1, ds1), ("U0", uk0, us0), ("U1", uk1, us1)):
        lanes[name].begin(keep, send)
    gn2_b = swapped(gn2)
    qkv = (first["Q0"], first["Q1"])
    have = {}

    def compute(name):
        if name == "down":
            have["mlp"] = down(chain, act, w_down)
            have["mlpb"] = swapped(have["mlp"])
        elif name == "resid_back":
            have["gr"], have["gm"], have["s2"], have["og"] = resid_back(
                chain, x, part, part_b, out_bias, ln2_gain, gn2, gn2_b, go, mixed, w_out
            )
        elif name == "attend_back":
            have["grads"], have["bq"] = attend_back(chain, q, k, v, mixed, have["gm"], lse)
        elif name == "q_send":
            have["qs"] = qkv_grad(chain, where, n1, have["grads"], have["og"], qkv, 1)
        elif name == "q_keep":
            kept = qkv_grad(chain, where, n1, have["grads"], have["og"], qkv, 0)
            for i in range(2):
                lanes["Q%d" % i].begin(kept[i], have["qs"][i])
        elif name == "back_in":
            have["gn1"] = back_in(chain, have["grads"], w3, rows)
            have["gn1b"] = swapped(have["gn1"])
        elif name == "images_back":
            have["out"], have["pack"] = images_back(
                chain, x, ln1_gain, have["gr"], have["gn1"], have["gn1b"], bd, bu, have["s2"], have["bq"]
            )
        elif name == "block_out":
            have["block"] = block_out(chain, x, part, part_b, out_bias, have["mlp"], have["mlpb"], down_bias)
        elif name[:4] == "pack":
            have["pack"] = add(chain, have["pack"], lax.ppermute(have["pack"], "dp", xor_pairs(1 << int(name[4]))))
        elif name == "unpack":
            have["small"] = unpack(chain, have["pack"], hidden, local)

    for name in SCHEDULE:
        if name in lanes:
            lanes[name].step()
        else:
            compute(name)
    small = have["small"]
    return (
        have["block"].reshape(images.shape),
        have["out"].reshape(images.shape),
        small[0],
        small[1],
        jnp.transpose(projections.now.reshape(3, width, local), (1, 0, 2)),
        small[7],
        outs.now,
        small[2],
        small[3],
        small[4],
        ups.now,
        small[6],
        downs.now,
        small[5],
    )


def shards(*args):
    images, w_up = args[0], args[11]
    cube = lax.axis_size("dp") == 16 and lax.axis_size("tensor") == 2
    if cube and images.shape[0] == 1 and w_up.shape[1] == 2 * w_up.shape[0]:
        return shards_cube(*args)
    return shards_any(*args)


def solution(mesh):
    in_specs = (
        P("dp", None, None),
        P("dp"),
        P("dp", None, None),
        P(),
        P(),
        P(None, None, "tensor"),
        P(None, "tensor"),
        P("tensor", None),
        P(),
        P(),
        P(),
        P(None, "tensor"),
        P("tensor"),
        P("tensor", None),
        P(),
    )
    out_specs = (
        P("dp", None, None),
        P("dp", None, None),
        P(),
        P(),
        P(None, None, "tensor"),
        P(None, "tensor"),
        P("tensor", None),
        P(),
        P(),
        P(),
        P(None, "tensor"),
        P("tensor"),
        P("tensor", None),
        P(),
    )
    return jax.shard_map(shards, mesh=mesh, in_specs=in_specs, out_specs=out_specs, check_vma=False)
```

```python
import jax
import jax.numpy as jnp
from jax import lax
from jax.experimental import pallas as pl
from jax.experimental.pallas import tpu as pltpu
from jax.sharding import PartitionSpec as P

HD = 64
VALID = 577
EPS = 1e-06
BF = jnp.bfloat16
F32 = jnp.float32


def stats(values):
    mean = jnp.mean(values, axis=-1, keepdims=True)
    centred = values - mean
    spread = jnp.mean(centred * centred, axis=-1, keepdims=True)
    inv = lax.rsqrt(spread + EPS)
    return centred * inv, inv


def norm_back(unit, inv, gain, grad):
    scaled = grad * gain
    mean_a = jnp.mean(scaled, axis=-1, keepdims=True)
    mean_b = jnp.mean(scaled * unit, axis=-1, keepdims=True)
    return inv * (scaled - mean_a - unit * mean_b)


def inner_rows(left, right):
    return lax.dot_general(
        left, right, (((0,), (0,)), ((), ())), preferred_element_type=F32
    )


def times_back(left, weight):
    return lax.dot_general(
        left, weight, (((1,), (1,)), ((), ())), preferred_element_type=F32
    )


def score_block(query, keyset):
    raw = jnp.einsum("qhd,khd->hqk", query, keyset, preferred_element_type=F32)
    live = jnp.arange(raw.shape[-1]) < VALID
    return jnp.where(live, raw * HD ** (-0.5), -1e30)


def attend_forward(query, keyset, valueset):
    scores = score_block(query, keyset)
    peak = jnp.max(scores, axis=-1, keepdims=True)
    expo = jnp.exp(scores - peak)
    total = jnp.sum(expo, axis=-1, keepdims=True)
    probs = (expo / total).astype(BF)
    mixed = jnp.einsum("hqk,khd->qhd", probs, valueset, preferred_element_type=F32)
    return mixed.astype(BF), peak[..., 0] + jnp.log(total[..., 0])


def attend_backward(query, keyset, valueset, grad_mixed, logsum):
    scores = score_block(query, keyset)
    probs = jnp.exp(scores - logsum[..., None])
    grad_probs = jnp.einsum("qhd,khd->hqk", grad_mixed, valueset, preferred_element_type=F32)
    delta = jnp.sum(probs * grad_probs, axis=-1, keepdims=True)
    grad_scores = (probs * (grad_probs - delta) * HD ** (-0.5)).astype(BF)
    low_probs = probs.astype(BF)
    grad_value = jnp.einsum("hqk,qhd->khd", low_probs, grad_mixed, preferred_element_type=F32)
    grad_query = jnp.einsum("hqk,khd->qhd", grad_scores, keyset, preferred_element_type=F32)
    grad_key = jnp.einsum("hqk,qhd->khd", grad_scores, query, preferred_element_type=F32)
    return jnp.stack([grad_query, grad_key, grad_value], axis=1).astype(BF)


def swap_sum(part):
    if lax.axis_size("tensor") == 2:
        other = lax.ppermute(part, "tensor", [(0, 1), (1, 0)])
        return part.astype(F32) + other.astype(F32)
    return lax.psum(part.astype(F32), "tensor")


def xor_pairs(bit):
    return [(i, i ^ bit) for i in range(lax.axis_size("dp"))]


def bits_of():
    count = lax.axis_size("dp")
    bits = []
    while count > 1:
        if count % 2:
            raise ValueError("dp")
        bits.append(1 << len(bits))
        count //= 2
    return bits


def sum_small(vector):
    for bit in bits_of():
        vector = vector + lax.ppermute(vector, "dp", xor_pairs(bit))
    return vector


def cut_thirds(rows, turn):
    unit = 128
    whole = rows // unit
    base = whole // 3
    counts = [base + (1 if (i - turn) % 3 < whole % 3 else 0) for i in range(3)]
    return [c * unit for c in counts]


def sum_over_dp(matrix, turn):
    bits = bits_of()
    index = lax.axis_index("dp")
    halving = bits[: min(3, len(bits) - 1)]
    swaps = bits[len(halving) :]
    pieces, orders, start = [], [], 0
    for lane, rows in enumerate(cut_thirds(matrix.shape[0], turn)):
        if rows == 0:
            continue
        pieces.append(lax.slice_in_dim(matrix, start, start + rows, axis=0))
        turned = lane % len(halving)
        orders.append(halving[turned:] + halving[:turned])
        start += rows
    for step in range(len(halving)):
        for lane in range(len(pieces)):
            piece, bit = pieces[lane], orders[lane][step]
            half = piece.shape[0] // 2
            side = (index // bit) & 1
            kept = lax.dynamic_slice_in_dim(piece, side * half, half, 0)
            sent = lax.dynamic_slice_in_dim(piece, (1 - side) * half, half, 0)
            pieces[lane] = kept + lax.ppermute(sent, "dp", xor_pairs(bit))
    for bit in swaps:
        for lane in range(len(pieces)):
            pieces[lane] = pieces[lane] + lax.ppermute(pieces[lane], "dp", xor_pairs(bit))
    for step in reversed(range(len(halving))):
        for lane in range(len(pieces)):
            piece, bit = pieces[lane], orders[lane][step]
            other = lax.ppermute(piece, "dp", xor_pairs(bit))
            side = (index // bit) & 1
            pieces[lane] = jnp.where(
                side == 0,
                jnp.concatenate([piece, other], axis=0),
                jnp.concatenate([other, piece], axis=0),
            )
    return jnp.concatenate(pieces, axis=0).astype(F32)


def shards_any(
    images,
    image_mask,
    cotangent,
    ln1_gain,
    ln1_bias,
    w_qkv,
    qv_bias,
    w_out,
    out_bias,
    ln2_gain,
    ln2_bias,
    w_up,
    up_bias,
    w_down,
    down_bias,
):
    count, seq, width = images.shape
    rows = count * seq
    local = w_qkv.shape[2]
    heads = local // HD
    gain1 = ln1_gain.astype(F32)
    gain2 = ln2_gain.astype(F32)
    inputs = images.reshape(rows, width).astype(F32)
    keep = image_mask.astype(BF)[:, None, None]
    grad_out = (cotangent * keep).reshape(rows, width)
    w_qkv_flat = w_qkv.reshape(width, 3 * local)
    bias_row = jnp.concatenate([qv_bias[0], jnp.zeros_like(qv_bias[0]), qv_bias[1]]).astype(F32)

    unit1, inv1 = stats(inputs)
    normed1 = (unit1 * gain1 + ln1_bias.astype(F32)).astype(BF)
    qkv = (jnp.dot(normed1, w_qkv_flat, preferred_element_type=F32) + bias_row).astype(BF)
    split = qkv.reshape(count, seq, 3, heads, HD)
    attended = [attend_forward(split[i, :, 0], split[i, :, 1], split[i, :, 2]) for i in range(count)]
    mixed = jnp.concatenate([a[0] for a in attended], axis=0).reshape(rows, local)
    attn = swap_sum(jnp.dot(mixed, w_out, preferred_element_type=F32).astype(BF))
    grad_act = times_back(grad_out, w_down)
    resid = inputs + attn + out_bias.astype(F32)
    unit2, inv2 = stats(resid)
    normed2 = (unit2 * gain2 + ln2_bias.astype(F32)).astype(BF)
    pre = jnp.dot(normed2, w_up, preferred_element_type=F32) + up_bias.astype(F32)
    cdf = 0.5 * (1.0 + lax.erf(pre * (0.5**0.5)))
    act = (pre * cdf).astype(BF)
    slope = cdf + pre * jnp.exp(-0.5 * pre * pre) * ((0.5 / jnp.pi) ** 0.5)
    grad_pre = (grad_act * slope).astype(BF)
    grad_wdown = inner_rows(act, grad_out).astype(BF)
    summed_wdown = sum_over_dp(grad_wdown, 0)
    grad_wup = inner_rows(normed2, grad_pre).astype(BF)
    summed_wup = sum_over_dp(grad_wup, 1)
    grad_normed2 = swap_sum(times_back(grad_pre, w_up).astype(BF))
    mlp = swap_sum(jnp.dot(act, w_down, preferred_element_type=F32).astype(BF))
    block_output = (resid + mlp + down_bias.astype(F32)).astype(BF).reshape(images.shape)
    grad_resid = grad_out.astype(F32) + norm_back(unit2, inv2, gain2, grad_normed2)
    resid_low = grad_resid.astype(BF)
    grad_wout = inner_rows(mixed, resid_low).astype(BF)
    summed_wout = sum_over_dp(grad_wout, 2)
    grad_mixed = times_back(resid_low, w_out).astype(BF).reshape(count, seq, heads, HD)
    grad_qkv = jnp.concatenate(
        [
            attend_backward(split[i, :, 0], split[i, :, 1], split[i, :, 2], grad_mixed[i], attended[i][1])
            for i in range(count)
        ],
        axis=0,
    ).reshape(rows, 3 * local)
    grad_wqkv = inner_rows(normed1, grad_qkv).astype(BF)
    summed_wqkv = sum_over_dp(grad_wqkv, 0).reshape(width, 3, local)
    bias_sums = jnp.sum(grad_qkv.astype(F32), axis=0)
    grad_normed1 = swap_sum(times_back(grad_qkv, w_qkv_flat).astype(BF))
    images_grad = (
        (grad_resid + norm_back(unit1, inv1, gain1, grad_normed1)).astype(BF).reshape(images.shape)
    )

    small = [
        jnp.sum(grad_normed1 * unit1, axis=0),
        jnp.sum(grad_normed1, axis=0),
        jnp.sum(grad_resid, axis=0),
        jnp.sum(grad_normed2 * unit2, axis=0),
        jnp.sum(grad_normed2, axis=0),
        jnp.sum(grad_out.astype(F32), axis=0),
        jnp.sum(grad_pre.astype(F32), axis=0),
        bias_sums[:local],
        bias_sums[2 * local :],
    ]
    flat = jnp.concatenate(small)
    length = flat.shape[0]
    padded = -(-length // 1024) * 1024
    flat = sum_small(jnp.pad(flat, (0, padded - length)).reshape(padded // 128, 128)).reshape(-1)
    out, at = [], 0
    for part in small:
        out.append(flat[at : at + part.shape[0]])
        at += part.shape[0]
    return (
        block_output,
        images_grad,
        out[0],
        out[1],
        summed_wqkv,
        jnp.stack([out[7], out[8]]),
        summed_wout,
        out[2],
        out[3],
        out[4],
        summed_wup,
        out[6],
        summed_wdown,
        out[5],
    )


CHUNKS = 2
ANY = pl.BlockSpec(memory_space=pl.ANY)
HBM = pl.BlockSpec(memory_space=pltpu.HBM)
VM = pl.BlockSpec(memory_space=pltpu.VMEM)
MIB = 1024 * 1024


def shape_of(shape, dtype):
    return jax.ShapeDtypeStruct(shape, dtype)


def nn(left, right):
    return jnp.dot(left, right, preferred_element_type=F32)


def normal_unit(values):
    mean = jnp.mean(values, axis=-1, keepdims=True)
    centred = values - mean
    spread = jnp.mean(centred * centred, axis=-1, keepdims=True)
    inv = lax.rsqrt(spread + EPS)
    return centred * inv, inv


def row_of(ref):
    return ref[...].astype(F32).reshape(1, ref.shape[0])


def side_of(where_ref, bits):
    bit = bits[0] if bits[0] == bits[1] else jnp.where(where_ref[1] == 0, bits[0], bits[1])
    return (where_ref[0] >> bit) & 1


class Chain:
    def __init__(self):
        self.last = None

    def __call__(
        self, body, args, in_specs, outs, out_specs, scratch=(), grid=(), vmem=40, aliases=None, name=None, prefetch=0, cost=0.001
    ):
        args, in_specs, run = list(args), list(in_specs), body
        if self.last is not None:
            spot = len(args)

            def run(*refs):
                body(*refs[:spot], *refs[spot + 1 :])

            args.append(self.last)
            in_specs.append(ANY)
        spec = pltpu.PrefetchScalarGridSpec(
            num_scalar_prefetch=prefetch,
            grid=grid,
            in_specs=in_specs,
            out_specs=out_specs,
            scratch_shapes=list(scratch),
        )
        made = pl.pallas_call(
            run,
            out_shape=outs,
            grid_spec=spec,
            input_output_aliases=aliases or {},
            compiler_params=pltpu.CompilerParams(vmem_limit_bytes=vmem * MIB),
            cost_estimate=pl.CostEstimate(flops=0, bytes_accessed=int(cost * 3e6), transcendentals=0),
            name=name,
        )(*args)
        self.last = made[0] if isinstance(made, (tuple, list)) else made
        return made


def row_chunks(rows):
    units, parts = rows // 16, CHUNKS
    cuts = [16 * (units * i // parts) for i in range(parts)] + [rows]
    return [(cuts[i], cuts[i + 1] - cuts[i]) for i in range(parts)]


def lane_halves():
    return lax.broadcasted_iota(jnp.int32, (1, 2 * HD), 1) < HD


def key_mask(length):
    return jnp.where(lax.broadcasted_iota(jnp.int32, (1, length), 1) < VALID, 0.0, -1e30)


def copier(sems):
    count = [0]

    def copy(source, target):
        made = pltpu.make_async_copy(source, target, sems.at[count[0]])
        count[0] += 1
        made.start()
        return made

    return copy


def attend_kernel(
    mask_ref, g_ref, s_ref, b_ref, x_ref, w_ref, wo_ref, cot_ref, wd_ref,
    part_ref, q_ref, k_ref, v_ref, mixed_ref, n1_ref, lse_ref, ga_ref, go_ref, bd_ref,
    x_b, w_b, wo_b, cot_b, wd_b, part_b, q_b, k_b, v_b, mixed_b, n1_b, lse_b, ga_b, go_b, sems,
):
    rows, width = x_ref.shape
    padded, local = q_ref.shape
    pairs = local // 128
    deep = wd_ref.shape[0] // pairs
    copy = copier(sems)
    get_x = copy(x_ref, x_b)
    get_w = [copy(w_ref.at[c], w_b.at[c]) for c in range(3)]
    get_cot = copy(cot_ref, cot_b)
    get_wd = [copy(wd_ref.at[pl.ds(i * deep, deep)], wd_b.at[i]) for i in range(pairs)]
    get_wo = copy(wo_ref, wo_b)
    puts = []
    get_x.wait()
    unit, _ = normal_unit(x_b[...].astype(F32))
    normed = unit * row_of(g_ref) + row_of(s_ref)
    n1_b[...] = jnp.concatenate([normed, jnp.zeros((padded - rows, width), F32)], axis=0).astype(BF)
    puts.append(copy(n1_b, n1_ref))
    lse_b[...] = jnp.zeros(lse_b.shape, F32)
    live = lax.broadcasted_iota(jnp.int32, (padded, 1), 0) < rows
    for c, (buf, ref, scale) in enumerate(((q_b, q_ref, HD ** (-0.5)), (k_b, k_ref, 1.0), (v_b, v_ref, 1.0))):
        get_w[c].wait()
        for at in range(0, local, 256):
            made = nn(n1_b[...], w_b[c, :, at : at + 256])
            if c != 1:
                made = made + b_ref[c // 2 : c // 2 + 1, at : at + 256].astype(F32)
            made = jnp.where(live, made, 0.0).astype(BF)
            buf[:, at : at + 256] = made * jnp.asarray(scale, BF)
        puts.append(copy(buf, ref))
    get_cot.wait()
    masked = cot_b[...].astype(F32) * mask_ref[0].astype(F32)
    go_b[...] = masked.astype(BF)
    puts.append(copy(go_b, go_ref))
    bd_ref[...] = jnp.sum(masked, axis=0, keepdims=True)
    for get in get_wd:
        get.wait()
    mask = key_mask(padded)
    first = lane_halves()
    lane = lax.broadcasted_iota(jnp.int32, (1, 128), 1)

    def pair(p, carry):
        cols = pl.ds(pl.multiple_of(p * 128, 128), 128)
        keys, vals = k_b[:, cols], v_b[:, cols]
        query = q_b[:, cols]
        zero, ones = jnp.zeros_like(keys), jnp.ones_like(vals)
        own_k = (jnp.where(first, keys, zero), jnp.where(first, zero, keys))
        own_v = (jnp.where(first, vals, ones), jnp.where(first, ones, vals))
        ga_b[:, pl.ds(pl.multiple_of(p * deep, deep), deep)] = times_back(go_b[...], wd_b[p]).astype(BF)
        outs = []
        logs = lse_b[...]
        for h in range(2):
            scores = times_back(query, own_k[h]) + mask
            peak = jnp.max(scores, axis=-1, keepdims=True)
            made = nn(jnp.exp(scores - peak).astype(BF), own_v[h])
            total = made[:, HD : HD + 1] if h == 0 else made[:, 0:1]
            outs.append(made * (1.0 / total))
            logs = jnp.where(lane == 2 * p + h, peak + jnp.log(total), logs)
        lse_b[...] = logs
        mixed_b[:, cols] = jnp.where(first, outs[0], outs[1]).astype(BF)
        return carry

    lax.fori_loop(0, pairs, pair, 0)
    puts += [copy(ga_b, ga_ref), copy(mixed_b, mixed_ref), copy(lse_b, lse_ref)]
    get_wo.wait()
    for at in range(0, width, 256):
        made = nn(mixed_b[...], wo_b[:, at : at + 256])
        part_b[:, at : at + 256] = made[:rows].astype(BF)
    puts.append(copy(part_b, part_ref))
    for put in puts:
        put.wait()


def attend(chain, mask, gain, shift, bias, x, w3, w_out, cot, w_down):
    rows, width = x.shape
    local = w3.shape[2]
    hidden = w_down.shape[0]
    padded = -(-rows // 16) * 16
    pairs = local // 128
    slab = ((rows, width), BF)
    wide = ((padded, local), BF)
    outs = (slab, wide, wide, wide, wide, ((padded, width), BF), ((padded, 128), F32), ((rows, hidden), BF), slab)
    held = (slab, ((3, width, local), BF), ((local, width), BF), slab, ((pairs, hidden // pairs, width), BF)) + outs
    return chain(
        attend_kernel,
        (mask, gain, shift, bias, x, w3, w_out, cot, w_down),
        [VM] * 3 + [HBM] * 5,
        tuple(shape_of(*out) for out in outs) + (shape_of((1, width), F32),),
        (HBM,) * len(outs) + (VM,),
        [pltpu.VMEM(*hold) for hold in held] + [pltpu.SemaphoreType.DMA((7 + pairs + len(outs),))],
        name="attend",
        vmem=60,
        prefetch=1,
    )


def gelu_pair(pre):
    bell = jnp.exp(-0.5 * pre * pre)
    near = 1.0 / (1.0 + (0.3275911 * 0.5**0.5) * jnp.abs(pre))
    poly = near * (
        0.254829592 + near * (-0.284496736 + near * (1.421413741 + near * (-1.453152027 + near * 1.061405429)))
    )
    tail = 0.5 * poly * bell
    cdf = jnp.where(pre < 0, tail, 1.0 - tail)
    return cdf, cdf + pre * bell * ((0.5 / jnp.pi) ** 0.5)


def feed_kernel(
    where_ref, ob_ref, g_ref, s_ref, ub_ref, x_ref, pa_ref, pb_ref, go_ref, wu_ref, ga_ref,
    act_ref, gn_ref, ds0_ref, ds1_ref, dk0_ref, dk1_ref, us0_ref, us1_ref, uk0_ref, uk1_ref, bu_ref,
    x_b, pa_b, pb_b, go_b, wu_b, ga_b, act_b, n2_b, down_b, up_b, gn_b, total, bias, sems, *, bits,
):
    rows, width = x_ref.shape
    hidden = wu_ref.shape[1]
    size = hidden // 4
    tall = width // 4
    sides = [side_of(where_ref, bit) for bit in bits]
    starts = [pl.multiple_of((2 * lane + (1 - sides[lane])) * size, size) for lane in range(2)]
    starts += [pl.multiple_of((2 * lane + sides[lane]) * size, size) for lane in range(2)]
    tops = [pl.multiple_of((2 * lane + (1 - sides[2 + lane])) * tall, tall) for lane in range(2)]
    tops += [pl.multiple_of((2 * lane + sides[2 + lane]) * tall, tall) for lane in range(2)]
    copy = copier(sems)
    gets = [copy(x_ref, x_b), copy(pa_ref, pa_b), copy(pb_ref, pb_b)]
    get_w, get_ga = [], []
    for c in range(4):
        get_w.append(copy(wu_ref.at[:, pl.ds(starts[c], size)], wu_b.at[c]))
        get_ga.append(copy(ga_ref.at[:, pl.ds(starts[c], size)], ga_b.at[c]))
        if c == 0:
            get_go = copy(go_ref, go_b)
    puts = []
    bias[...] = row_of(ub_ref)
    for get in gets:
        get.wait()
    resid = x_b[...].astype(F32) + (pa_b[...].astype(F32) + pb_b[...].astype(F32)) + row_of(ob_ref)
    unit, _ = normal_unit(resid)
    n2_b[...] = (unit * row_of(g_ref) + row_of(s_ref)).astype(BF)

    def front(c):
        get_w[c].wait()
        get_ga[c].wait()
        for at in range(0, size, 256):
            cols = pl.ds(pl.multiple_of(starts[c] + at, 256), 256)
            pre = nn(n2_b[...], wu_b[c, :, at : at + 256]) + bias[:, cols]
            cdf, slope = gelu_pair(pre)
            act_b[c, :, at : at + 256] = (pre * cdf).astype(BF)
            grad_pre = (ga_b[c, :, at : at + 256].astype(F32) * slope).astype(BF)
            ga_b[c, :, at : at + 256] = grad_pre
            bu_ref[:, cols] = jnp.sum(grad_pre.astype(F32), axis=0, keepdims=True)
        puts.append(copy(act_b.at[c], act_ref.at[:, pl.ds(starts[c], size)]))

    def back(c):
        if c == 0:
            get_go.wait()
        for at in range(0, width, 512):
            made = inner_rows(act_b[c], go_b[:, at : at + 512])
            down_b[c, :, at : at + 512] = made.astype(BF)
        puts.append(copy(down_b.at[c], (ds0_ref, ds1_ref, dk0_ref, dk1_ref)[c]))
        for piece in range(4):
            made = inner_rows(n2_b[:, pl.ds(tops[piece], tall)], ga_b[c])
            up_b[piece, :, pl.ds(starts[c], size)] = made.astype(BF)
        for at in range(0, width, 512):
            made = times_back(ga_b[c], wu_b[c, at : at + 512, :])
            if c:
                made = made + total[:, at : at + 512]
            if c < 3:
                total[:, at : at + 512] = made
            else:
                gn_b[:, at : at + 512] = made.astype(BF)

    for c in range(5):
        if c < 4:
            front(c)
        if c:
            back(c - 1)
    puts.append(copy(gn_b, gn_ref))
    for piece, ref in enumerate((us0_ref, us1_ref, uk0_ref, uk1_ref)):
        puts.append(copy(up_b.at[piece], ref))
    for put in puts:
        put.wait()


def feed(chain, where, bits, out_bias, gain, shift, up_bias, x, pa, pb, go, w_up, ga):
    rows, width = x.shape
    hidden = w_up.shape[1]

    def body(*refs):
        feed_kernel(*refs, bits=bits)

    slab = ((rows, width), BF)
    deep = ((4, rows, hidden // 4), BF)
    outs = (((rows, hidden), BF), slab) + (((hidden // 4, width), BF),) * 4 + (((width // 4, hidden), BF),) * 4
    held = (slab,) * 4 + (((4, width, hidden // 4), BF), deep, deep, slab, ((4, hidden // 4, width), BF))
    held += (((4, width // 4, hidden), BF), slab, ((rows, width), F32), ((1, hidden), F32))
    return chain(
        body,
        (where, out_bias, gain, shift, up_bias, x, pa, pb, go, w_up, ga),
        [VM] * 4 + [HBM] * 6,
        tuple(shape_of(*out) for out in outs) + (shape_of((1, hidden), F32),),
        (HBM,) * len(outs) + (VM,),
        [pltpu.VMEM(*hold) for hold in held] + [pltpu.SemaphoreType.DMA((12 + 4 + len(outs),))],
        name="feed",
        vmem=60,
        prefetch=1,
    )


def qkv_grad(chain, where, n1, grads, out_grad, bits, flip):
    width = n1.shape[1]
    local = grads.shape[1] // 3
    size = width // 4

    def body(where_ref, n1_ref, g_ref, o_ref, first_ref, second_ref):
        def product(ref, start):
            for i in range(4):
                made = inner_rows(n1_ref[:, i * size : (i + 1) * size], g_ref[:, pl.ds(start, local)])
                ref[i * size : (i + 1) * size, :] = made.astype(BF)

        product(first_ref, pl.multiple_of((side_of(where_ref, bits[0]) ^ flip) * local, local))
        which = side_of(where_ref, bits[1]) ^ flip

        @pl.when(which == 0)
        def _():
            product(second_ref, 2 * local)

        @pl.when(which == 1)
        def _():
            second_ref[...] = o_ref[...]

    return chain(
        body,
        (where, n1, grads, out_grad),
        [VM, VM, VM],
        (shape_of((width, local), BF),) * 2,
        (VM,) * 2,
        name="qkv_grad",
        prefetch=1,
    )


TILES = 4


def paired(own, other):
    return own[...].astype(F32) + other[...].astype(F32)


def down(chain, act, w_down):
    rows, hidden = act.shape
    width = w_down.shape[1]
    size = width // TILES
    deep = hidden // TILES

    def body(act_ref, w_ref, *rest):
        out_ref, w_buf, sems = rest
        copies = [
            pltpu.make_async_copy(w_ref.at[pl.ds(i * deep, deep)], w_buf.at[pl.ds(i * deep, deep)], sems.at[i])
            for i in range(TILES)
        ]
        for copy in copies:
            copy.start()
        for copy in copies:
            copy.wait()
        for i in range(TILES):
            out_ref[:, i * size : (i + 1) * size] = nn(act_ref[...], w_buf[:, i * size : (i + 1) * size]).astype(BF)

    return chain(
        body,
        (act, w_down),
        [VM, HBM],
        shape_of((rows, width), BF),
        VM,
        [pltpu.VMEM((hidden, width), BF), pltpu.SemaphoreType.DMA((TILES,))],
        name="down",
    )


def resid_back_kernel(
    x_ref, pa_ref, pb_ref, ob_ref, g_ref, ga_ref, gb_ref, go_ref, mixed_ref, wo_ref, gr_ref, gm_ref, sums_ref, og_ref, low
):
    rows, width = x_ref.shape
    padded, local = mixed_ref.shape
    resid = x_ref[...].astype(F32) + (pa_ref[...].astype(F32) + pb_ref[...].astype(F32)) + row_of(ob_ref)
    unit, inv = normal_unit(resid)
    grad = paired(ga_ref, gb_ref)
    total = go_ref[...].astype(F32) + norm_back(unit, inv, row_of(g_ref), grad)
    gr_ref[...] = total
    low[...] = jnp.concatenate([total, jnp.zeros((padded - rows, width), F32)], axis=0).astype(BF)
    sums_ref[...] = jnp.concatenate(
        [
            jnp.sum(total, axis=0, keepdims=True),
            jnp.sum(grad * unit, axis=0, keepdims=True),
            jnp.sum(grad, axis=0, keepdims=True),
            jnp.zeros((5, width), F32),
        ],
        axis=0,
    )
    for i in range(2):
        for at in range(0, width // 2, 256):
            start = i * width // 2 + at
            made = inner_rows(mixed_ref[...], low[:, start : start + 256])
            og_ref[i * local : (i + 1) * local, at : at + 256] = made.astype(BF)
    for at in range(0, local, 256):
        gm_ref[:, at : at + 256] = times_back(low[...], wo_ref[at : at + 256, :]).astype(BF)


def resid_back(chain, x, pa, pb, out_bias, gain, ga, gb, go, mixed, w_out):
    rows, width = x.shape
    padded, local = mixed.shape
    return chain(
        resid_back_kernel,
        (x, pa, pb, out_bias, gain, ga, gb, go, mixed, w_out),
        [VM] * 10,
        (
            shape_of((rows, width), F32),
            shape_of((padded, local), BF),
            shape_of((8, width), F32),
            shape_of((2 * local, width // 2), BF),
        ),
        (VM,) * 4,
        [pltpu.VMEM((padded, width), BF)],
        name="resid_back",
    )


def attend_back_kernel(q_ref, k_ref, v_ref, mixed_ref, gm_ref, lse_ref, out_ref, bias_ref, probs_s, slopes_s):
    padded, local = q_ref.shape
    mask = key_mask(padded)
    first = lane_halves()
    lane = lax.broadcasted_iota(jnp.int32, (1, 128), 1)

    def pair(p, carry):
        cols = pl.ds(pl.multiple_of(p * 128, 128), 128)
        keys, vals = k_ref[:, cols], v_ref[:, cols]
        zero = jnp.zeros_like(keys)
        own_k = (jnp.where(first, keys, zero), jnp.where(first, zero, keys))
        own_v = (jnp.where(first, vals, zero), jnp.where(first, zero, vals))
        for at, size in row_chunks(padded):
            query = q_ref[at : at + size, cols]
            grad = gm_ref[at : at + size, cols]
            both = grad.astype(F32) * mixed_ref[at : at + size, cols].astype(F32)
            logs = lse_ref[at : at + size, :]
            outs = []
            for h in range(2):
                own_lanes = first if h == 0 else jnp.logical_not(first)
                delta = jnp.sum(jnp.where(own_lanes, both, 0.0), axis=-1, keepdims=True)
                log = jnp.sum(jnp.where(lane == 2 * p + h, logs, 0.0), axis=-1, keepdims=True)
                probs = jnp.exp(times_back(query, own_k[h]) + mask - log)
                slope = (probs * (times_back(grad, own_v[h]) - delta)).astype(BF)
                probs_s[h, at : at + size, :] = probs.astype(BF)
                slopes_s[h, at : at + size, :] = slope
                outs.append(nn(slope, keys))
            out_ref[at : at + size, cols] = (jnp.where(first, outs[0], outs[1]) * HD ** (-0.5)).astype(BF)
        grad_t = gm_ref[:, cols].astype(F32).T.astype(BF)
        query_t = q_ref[:, cols].astype(F32).T.astype(BF)
        grad_k = [nn(query_t[HD * h : HD * h + HD], slopes_s[h]) for h in range(2)]
        grad_v = [nn(grad_t[HD * h : HD * h + HD], probs_s[h]) for h in range(2)]
        cols_k = pl.ds(pl.multiple_of(local + p * 128, 128), 128)
        cols_v = pl.ds(pl.multiple_of(2 * local + p * 128, 128), 128)
        out_ref[:, cols_k] = jnp.concatenate(grad_k, axis=0).T.astype(BF)
        out_ref[:, cols_v] = jnp.concatenate(grad_v, axis=0).T.astype(BF)
        return carry

    lax.fori_loop(0, local // 128, pair, 0)
    bias_ref[...] = jnp.sum(out_ref[...].astype(F32), axis=0, keepdims=True)


def attend_back(chain, q, k, v, mixed, gm, lse):
    padded, local = q.shape
    return chain(
        attend_back_kernel,
        (q, k, v, mixed, gm, lse),
        [VM] * 6,
        (shape_of((padded, 3 * local), BF), shape_of((1, 3 * local), F32)),
        (VM, VM),
        [pltpu.VMEM((2, padded, padded), BF), pltpu.VMEM((2, padded, padded), BF)],
        name="attend_back",
    )


def back_in(chain, grads, w3, rows):
    _, width, local = w3.shape
    size = width // TILES

    def body(g_ref, w_ref, *rest):
        out_ref, w_buf, sems = rest
        copies = [
            pltpu.make_async_copy(w_ref.at[:, pl.ds(i * size, size)], w_buf.at[i], sems.at[i]) for i in range(TILES)
        ]
        for copy in copies:
            copy.start()
        for i in range(TILES):
            copies[i].wait()
            total = times_back(g_ref[:, :local], w_buf[i, 0])
            for c in range(1, 3):
                total += times_back(g_ref[:, c * local : (c + 1) * local], w_buf[i, c])
            out_ref[:, i * size : (i + 1) * size] = total[:rows].astype(BF)

    return chain(
        body,
        (grads, w3),
        [VM, HBM],
        shape_of((rows, width), BF),
        VM,
        [pltpu.VMEM((TILES, 3, size, local), BF), pltpu.SemaphoreType.DMA((TILES,))],
        name="back_in",
    )


def images_back_kernel(x_ref, g_ref, gr_ref, ga_ref, gb_ref, bd_ref, bu_ref, s2_ref, bq_ref, out_ref, pack_ref):
    unit, inv = normal_unit(x_ref[...].astype(F32))
    grad = paired(ga_ref, gb_ref)
    out_ref[...] = (gr_ref[...] + norm_back(unit, inv, row_of(g_ref), grad)).astype(BF)
    width = x_ref.shape[1]
    hidden = bu_ref.shape[1]
    local = bq_ref.shape[1] // 3
    pack_ref[0:1, :] = jnp.sum(grad * unit, axis=0, keepdims=True)
    pack_ref[1:2, :] = jnp.sum(grad, axis=0, keepdims=True)
    pack_ref[2:5, :] = s2_ref[0:3, :]
    pack_ref[5:6, :] = bd_ref[...]
    for i in range(hidden // width):
        pack_ref[6 + i : 7 + i, :] = bu_ref[:, i * width : (i + 1) * width]
    after = 6 + hidden // width
    pack_ref[after : after + 1, :local] = bq_ref[:, :local]
    pack_ref[after : after + 1, local:] = bq_ref[:, 2 * local :]
    pack_ref[after + 1 :, :] = jnp.zeros((pack_ref.shape[0] - after - 1, width), F32)


def images_back(chain, x, gain, gr, ga, gb, bd, bu, s2, bq):
    return chain(
        images_back_kernel,
        (x, gain, gr, ga, gb, bd, bu, s2, bq),
        [VM] * 9,
        (shape_of(x.shape, BF), shape_of((16, x.shape[1]), F32)),
        (VM, VM),
        name="images_back",
    )


def block_out_kernel(x_ref, pa_ref, pb_ref, ob_ref, ma_ref, mb_ref, db_ref, out_ref):
    resid = x_ref[...].astype(F32) + (pa_ref[...].astype(F32) + pb_ref[...].astype(F32)) + row_of(ob_ref)
    out_ref[...] = (resid + paired(ma_ref, mb_ref) + row_of(db_ref)).astype(BF)


def block_out(chain, x, pa, pb, out_bias, ma, mb, down_bias):
    return chain(
        block_out_kernel,
        (x, pa, pb, out_bias, ma, mb, down_bias),
        [VM] * 7,
        shape_of(x.shape, BF), VM, name="block_out"
    )


def add_split_kernel(where_ref, k0_ref, k1_ref, r0_ref, r1_ref, send_ref, keep_ref):
    keep_ref[...] = (k0_ref[...].astype(F32) + r0_ref[...].astype(F32)).astype(BF)
    send_ref[...] = (k1_ref[...].astype(F32) + r1_ref[...].astype(F32)).astype(BF)


def add_split(chain, where, bit, keep, recv):
    rows, width = keep.shape
    half = rows // 2
    block = (half, width)
    own = pl.BlockSpec(block, lambda i, w: (side_of(w, bit), 0))
    other = pl.BlockSpec(block, lambda i, w: (1 - side_of(w, bit), 0))
    out = pl.BlockSpec(block, lambda i, w: (0, 0))
    return chain(
        add_split_kernel,
        (where, keep, keep, recv, recv),
        [own, other, own, other],
        (shape_of((half, width), BF),) * 2,
        (out, out),
        grid=(1,),
        name="add_split",
        prefetch=1,
        vmem=16,
    )


def add_kernel(a_ref, b_ref, out_ref):
    out_ref[...] = (a_ref[...].astype(F32) + b_ref[...].astype(F32)).astype(out_ref.dtype)


def add(chain, a, b):
    return chain(add_kernel, (a, b), [VM, VM], shape_of(a.shape, a.dtype), VM, name="add", vmem=16)


def join(chain, where, bit, own, other):
    half, width = own.shape

    def body(where_ref, own_ref, other_ref, out_ref):
        side = side_of(where_ref, bit)
        out_ref[pl.ds(pl.multiple_of(side * half, 16), half), :] = own_ref[...]
        out_ref[pl.ds(pl.multiple_of((1 - side) * half, 16), half), :] = other_ref[...]

    return chain(
        body,
        (where, own, other),
        [VM, VM],
        shape_of((2 * half, width), BF),
        VM,
        name="join",
        prefetch=1,
        vmem=16,
    )


class Home:
    def __init__(self, shape):
        self.shape, self.now = shape, None


def finish(chain, where, bits, flip, piece, homes):
    half, width = piece.shape
    parts = 4
    block = half // parts
    targets = list(dict.fromkeys(home for home, _ in homes))
    old = [home for home in targets if home.now is not None]

    def body(where_ref, piece_ref, *rest):
        outs = rest[len(old) : len(old) + len(targets)]
        made, sems = rest[-2:]
        which = side_of(where_ref, bits) ^ flip

        def write(number):
            home, row = homes[number]
            out_ref = outs[targets.index(home)]
            copies = []
            for i in range(parts):
                made[i * block : (i + 1) * block, :] = piece_ref[i * block : (i + 1) * block, :].astype(F32)
                if home.shape[1] == width:
                    place = out_ref.at[pl.ds(row + i * block, block)]
                else:
                    high = home.shape[0]
                    place = out_ref.at[pl.ds(i * block % high, block), pl.ds(i * block // high * width, width)]
                copies.append(pltpu.make_async_copy(made.at[pl.ds(i * block, block)], place, sems.at[i]))
                copies[-1].start()
            for copy in copies:
                copy.wait()

        for number in range(2):

            @pl.when(which == number)
            def _(number=number):
                write(number)

    made = chain(
        body,
        (where, piece, *(home.now for home in old)),
        [VM] + [HBM] * len(old),
        tuple(shape_of(home.shape, F32) for home in targets) + (shape_of((8, 128), F32),),
        (HBM,) * (len(targets) + 1),
        [pltpu.VMEM((half, width), F32), pltpu.SemaphoreType.DMA((parts,))],
        aliases={2 + i: targets.index(home) for i, home in enumerate(old)},
        name="finish",
        prefetch=1,
        vmem=16,
    )
    for home, now in zip(targets, made[:-1], strict=True):
        home.now = now
    chain.last = made[-1]


def unpack(chain, pack, hidden, local):
    width = pack.shape[1]
    steps = hidden // width

    def body(pack_ref, *outs):
        for i in range(6):
            outs[i][...] = pack_ref[i, :]
        for i in range(steps):
            outs[6][i * width : (i + 1) * width] = pack_ref[6 + i, :]
        for i in range(2):
            outs[7][i : i + 1, :] = pack_ref[6 + steps : 7 + steps, i * local : (i + 1) * local]

    line = shape_of((width,), F32)
    return chain(
        body,
        (pack,),
        [VM],
        (line,) * 6 + (shape_of((hidden,), F32), shape_of((2, local), F32)),
        (VM,) * 8,
        name="unpack",
    )


class Lane:
    def __init__(self, chain, where, order, homes):
        self.chain, self.where, self.homes = chain, where, homes
        self.bits = list(zip(*order, strict=True))
        self.keep = self.send = None
        self.stage = 0

    def begin(self, keep, send):
        self.keep, self.send = keep, send

    def over(self, bits, piece):
        pairs = [
            (2 * i + core, 2 * (i ^ (1 << bits[core])) + core) for i in range(lax.axis_size("dp")) for core in range(2)
        ]
        return lax.ppermute(piece, ("dp", "tensor"), pairs)

    def step(self):
        stage, bits, chain = self.stage, self.bits, self.chain
        self.stage += 1
        if stage < 2:
            recv = self.over(bits[stage], self.send)
            self.send, self.keep = add_split(chain, self.where, bits[stage + 1], self.keep, recv)
        elif stage == 2:
            self.keep = add(chain, self.keep, self.over(bits[2], self.send))
        elif stage == 3:
            self.keep = add(chain, self.keep, self.over((3, 3), self.keep))
        elif stage < 6:
            bit = bits[6 - stage]
            self.keep = join(chain, self.where, bit, self.keep, self.over(bit, self.keep))
        elif stage == 6:
            self.send = self.over(bits[0], self.keep)
            finish(chain, self.where, bits[0], 0, self.keep, self.homes)
        else:
            finish(chain, self.where, bits[0], 1, self.send, self.homes)


ORDERS = {
    "D0": ((1, 2, 0), (0, 2, 1)),
    "D1": ((2, 0, 1), (1, 0, 2)),
    "U0": ((2, 0, 1), (2, 1, 0)),
    "U1": ((1, 0, 2), (0, 1, 2)),
    "Q0": ((0, 1, 2), (0, 1, 2)),
    "Q1": ((1, 0, 2), (2, 1, 0)),
}
SCHEDULE = (
    "resid_back", "attend_back", "q_send", "D1", "back_in", "U0", "D0", "q_keep", "D1", "U0", "U1",
    "D1", "Q1", "D0", "Q0", "U1", "D1", "D0", "images_back", "U1", "D0", "Q0", "Q1", "U1", "U0",
    "pack0", "Q1", "D1", "U1", "D0", "U0", "pack1", "Q1", "Q0", "U0", "pack2", "D1", "Q1", "Q0", "U1",
    "down", "Q0", "U0", "Q1", "D0", "D0", "D1", "D1", "pack3", "U1", "D0", "Q0", "Q1", "U0", "unpack",
    "Q0", "U1", "block_out", "U0", "Q0", "Q1",
)


def shards_cube(
    images,
    image_mask,
    cotangent,
    ln1_gain,
    ln1_bias,
    w_qkv,
    qv_bias,
    w_out,
    out_bias,
    ln2_gain,
    ln2_bias,
    w_up,
    up_bias,
    w_down,
    down_bias,
):
    _, rows, width = images.shape
    local = w_qkv.shape[2]
    hidden = w_up.shape[1]
    x = images.reshape(rows, width)
    cot = cotangent.reshape(rows, width)
    where = jnp.stack([lax.axis_index("dp"), lax.axis_index("tensor")]).astype(jnp.int32)
    w3 = jnp.transpose(w_qkv, (1, 0, 2))
    chain = Chain()

    def swapped(piece):
        return lax.ppermute(piece, "tensor", [(0, 1), (1, 0)])

    downs, ups, outs = Home((hidden, width)), Home((width, hidden)), Home((local, width))
    projections = Home((3 * width, local))
    places = {
        "D0": ((downs, 0), (downs, hidden // 4)),
        "D1": ((downs, hidden // 2), (downs, 3 * hidden // 4)),
        "U0": ((ups, 0), (ups, width // 4)),
        "U1": ((ups, width // 2), (ups, 3 * width // 4)),
        "Q0": ((projections, 0), (projections, width)),
        "Q1": ((projections, 2 * width), (outs, 0)),
    }
    lanes = {name: Lane(chain, where, ORDERS[name], homes) for name, homes in places.items()}
    first = {name: lane.bits[0] for name, lane in lanes.items()}

    part, q, k, v, mixed, n1, lse, ga, go, bd = attend(
        chain, image_mask, ln1_gain, ln1_bias, qv_bias, x, w3, w_out, cot, w_down
    )
    part_b = swapped(part)
    bits = [first[name] for name in ("D0", "D1", "U0", "U1")]
    act, gn2, ds0, ds1, dk0, dk1, us0, us1, uk0, uk1, bu = feed(
        chain, where, bits, out_bias, ln2_gain, ln2_bias, up_bias, x, part, part_b, go, w_up, ga
    )
    for name, keep, send in (("D0", dk0, ds0), ("D1", dk1, ds1), ("U0", uk0, us0), ("U1", uk1, us1)):
        lanes[name].begin(keep, send)
    gn2_b = swapped(gn2)
    qkv = (first["Q0"], first["Q1"])
    have = {}

    def compute(name):
        if name == "down":
            have["mlp"] = down(chain, act, w_down)
            have["mlpb"] = swapped(have["mlp"])
        elif name == "resid_back":
            have["gr"], have["gm"], have["s2"], have["og"] = resid_back(
                chain, x, part, part_b, out_bias, ln2_gain, gn2, gn2_b, go, mixed, w_out
            )
        elif name == "attend_back":
            have["grads"], have["bq"] = attend_back(chain, q, k, v, mixed, have["gm"], lse)
        elif name == "q_send":
            have["qs"] = qkv_grad(chain, where, n1, have["grads"], have["og"], qkv, 1)
        elif name == "q_keep":
            kept = qkv_grad(chain, where, n1, have["grads"], have["og"], qkv, 0)
            for i in range(2):
                lanes["Q%d" % i].begin(kept[i], have["qs"][i])
        elif name == "back_in":
            have["gn1"] = back_in(chain, have["grads"], w3, rows)
            have["gn1b"] = swapped(have["gn1"])
        elif name == "images_back":
            have["out"], have["pack"] = images_back(
                chain, x, ln1_gain, have["gr"], have["gn1"], have["gn1b"], bd, bu, have["s2"], have["bq"]
            )
        elif name == "block_out":
            have["block"] = block_out(chain, x, part, part_b, out_bias, have["mlp"], have["mlpb"], down_bias)
        elif name[:4] == "pack":
            have["pack"] = add(chain, have["pack"], lax.ppermute(have["pack"], "dp", xor_pairs(1 << int(name[4]))))
        elif name == "unpack":
            have["small"] = unpack(chain, have["pack"], hidden, local)

    for name in SCHEDULE:
        if name in lanes:
            lanes[name].step()
        else:
            compute(name)
    small = have["small"]
    return (
        have["block"].reshape(images.shape),
        have["out"].reshape(images.shape),
        small[0],
        small[1],
        jnp.transpose(projections.now.reshape(3, width, local), (1, 0, 2)),
        small[7],
        outs.now,
        small[2],
        small[3],
        small[4],
        ups.now,
        small[6],
        downs.now,
        small[5],
    )


def shards(*args):
    images, w_up = args[0], args[11]
    cube = lax.axis_size("dp") == 16 and lax.axis_size("tensor") == 2
    if cube and images.shape[0] == 1 and w_up.shape[1] == 2 * w_up.shape[0]:
        return shards_cube(*args)
    return shards_any(*args)


def solution(mesh):
    in_specs = (
        P("dp", None, None),
        P("dp"),
        P("dp", None, None),
        P(),
        P(),
        P(None, None, "tensor"),
        P(None, "tensor"),
        P("tensor", None),
        P(),
        P(),
        P(),
        P(None, "tensor"),
        P("tensor"),
        P("tensor", None),
        P(),
    )
    out_specs = (
        P("dp", None, None),
        P("dp", None, None),
        P(),
        P(),
        P(None, None, "tensor"),
        P(None, "tensor"),
        P("tensor", None),
        P(),
        P(),
        P(),
        P(None, "tensor"),
        P("tensor"),
        P("tensor", None),
        P(),
    )
    return jax.shard_map(shards, mesh=mesh, in_specs=in_specs, out_specs=out_specs, check_vma=False)
```

```python
import jax
import jax.numpy as jnp
from jax import lax
from jax.experimental import pallas as pl
from jax.experimental.pallas import tpu as pltpu
from jax.sharding import PartitionSpec as P

HD = 64
VALID = 577
EPS = 1e-06
BF = jnp.bfloat16
F32 = jnp.float32


def stats(values):
    mean = jnp.mean(values, axis=-1, keepdims=True)
    centred = values - mean
    spread = jnp.mean(centred * centred, axis=-1, keepdims=True)
    inv = lax.rsqrt(spread + EPS)
    return centred * inv, inv


def norm_back(unit, inv, gain, grad):
    scaled = grad * gain
    mean_a = jnp.mean(scaled, axis=-1, keepdims=True)
    mean_b = jnp.mean(scaled * unit, axis=-1, keepdims=True)
    return inv * (scaled - mean_a - unit * mean_b)


def inner_rows(left, right):
    return lax.dot_general(
        left, right, (((0,), (0,)), ((), ())), preferred_element_type=F32
    )


def times_back(left, weight):
    return lax.dot_general(
        left, weight, (((1,), (1,)), ((), ())), preferred_element_type=F32
    )


def score_block(query, keyset):
    raw = jnp.einsum("qhd,khd->hqk", query, keyset, preferred_element_type=F32)
    live = jnp.arange(raw.shape[-1]) < VALID
    return jnp.where(live, raw * HD ** (-0.5), -1e30)


def attend_forward(query, keyset, valueset):
    scores = score_block(query, keyset)
    peak = jnp.max(scores, axis=-1, keepdims=True)
    expo = jnp.exp(scores - peak)
    total = jnp.sum(expo, axis=-1, keepdims=True)
    probs = (expo / total).astype(BF)
    mixed = jnp.einsum("hqk,khd->qhd", probs, valueset, preferred_element_type=F32)
    return mixed.astype(BF), peak[..., 0] + jnp.log(total[..., 0])


def attend_backward(query, keyset, valueset, grad_mixed, logsum):
    scores = score_block(query, keyset)
    probs = jnp.exp(scores - logsum[..., None])
    grad_probs = jnp.einsum("qhd,khd->hqk", grad_mixed, valueset, preferred_element_type=F32)
    delta = jnp.sum(probs * grad_probs, axis=-1, keepdims=True)
    grad_scores = (probs * (grad_probs - delta) * HD ** (-0.5)).astype(BF)
    low_probs = probs.astype(BF)
    grad_value = jnp.einsum("hqk,qhd->khd", low_probs, grad_mixed, preferred_element_type=F32)
    grad_query = jnp.einsum("hqk,khd->qhd", grad_scores, keyset, preferred_element_type=F32)
    grad_key = jnp.einsum("hqk,qhd->khd", grad_scores, query, preferred_element_type=F32)
    return jnp.stack([grad_query, grad_key, grad_value], axis=1).astype(BF)


def swap_sum(part):
    if lax.axis_size("tensor") == 2:
        other = lax.ppermute(part, "tensor", [(0, 1), (1, 0)])
        return part.astype(F32) + other.astype(F32)
    return lax.psum(part.astype(F32), "tensor")


def xor_pairs(bit):
    return [(i, i ^ bit) for i in range(lax.axis_size("dp"))]


def bits_of():
    count = lax.axis_size("dp")
    bits = []
    while count > 1:
        if count % 2:
            raise ValueError("dp")
        bits.append(1 << len(bits))
        count //= 2
    return bits


def sum_small(vector):
    for bit in bits_of():
        vector = vector + lax.ppermute(vector, "dp", xor_pairs(bit))
    return vector


def cut_thirds(rows, turn):
    unit = 128
    whole = rows // unit
    base = whole // 3
    counts = [base + (1 if (i - turn) % 3 < whole % 3 else 0) for i in range(3)]
    return [c * unit for c in counts]


def sum_over_dp(matrix, turn):
    bits = bits_of()
    index = lax.axis_index("dp")
    halving = bits[: min(3, len(bits) - 1)]
    swaps = bits[len(halving) :]
    pieces, orders, start = [], [], 0
    for lane, rows in enumerate(cut_thirds(matrix.shape[0], turn)):
        if rows == 0:
            continue
        pieces.append(lax.slice_in_dim(matrix, start, start + rows, axis=0))
        turned = lane % len(halving)
        orders.append(halving[turned:] + halving[:turned])
        start += rows
    for step in range(len(halving)):
        for lane in range(len(pieces)):
            piece, bit = pieces[lane], orders[lane][step]
            half = piece.shape[0] // 2
            side = (index // bit) & 1
            kept = lax.dynamic_slice_in_dim(piece, side * half, half, 0)
            sent = lax.dynamic_slice_in_dim(piece, (1 - side) * half, half, 0)
            pieces[lane] = kept + lax.ppermute(sent, "dp", xor_pairs(bit))
    for bit in swaps:
        for lane in range(len(pieces)):
            pieces[lane] = pieces[lane] + lax.ppermute(pieces[lane], "dp", xor_pairs(bit))
    for step in reversed(range(len(halving))):
        for lane in range(len(pieces)):
            piece, bit = pieces[lane], orders[lane][step]
            other = lax.ppermute(piece, "dp", xor_pairs(bit))
            side = (index // bit) & 1
            pieces[lane] = jnp.where(
                side == 0,
                jnp.concatenate([piece, other], axis=0),
                jnp.concatenate([other, piece], axis=0),
            )
    return jnp.concatenate(pieces, axis=0).astype(F32)


def shards_any(
    images,
    image_mask,
    cotangent,
    ln1_gain,
    ln1_bias,
    w_qkv,
    qv_bias,
    w_out,
    out_bias,
    ln2_gain,
    ln2_bias,
    w_up,
    up_bias,
    w_down,
    down_bias,
):
    count, seq, width = images.shape
    rows = count * seq
    local = w_qkv.shape[2]
    heads = local // HD
    gain1 = ln1_gain.astype(F32)
    gain2 = ln2_gain.astype(F32)
    inputs = images.reshape(rows, width).astype(F32)
    keep = image_mask.astype(BF)[:, None, None]
    grad_out = (cotangent * keep).reshape(rows, width)
    w_qkv_flat = w_qkv.reshape(width, 3 * local)
    bias_row = jnp.concatenate([qv_bias[0], jnp.zeros_like(qv_bias[0]), qv_bias[1]]).astype(F32)

    unit1, inv1 = stats(inputs)
    normed1 = (unit1 * gain1 + ln1_bias.astype(F32)).astype(BF)
    qkv = (jnp.dot(normed1, w_qkv_flat, preferred_element_type=F32) + bias_row).astype(BF)
    split = qkv.reshape(count, seq, 3, heads, HD)
    attended = [attend_forward(split[i, :, 0], split[i, :, 1], split[i, :, 2]) for i in range(count)]
    mixed = jnp.concatenate([a[0] for a in attended], axis=0).reshape(rows, local)
    attn = swap_sum(jnp.dot(mixed, w_out, preferred_element_type=F32).astype(BF))
    grad_act = times_back(grad_out, w_down)
    resid = inputs + attn + out_bias.astype(F32)
    unit2, inv2 = stats(resid)
    normed2 = (unit2 * gain2 + ln2_bias.astype(F32)).astype(BF)
    pre = jnp.dot(normed2, w_up, preferred_element_type=F32) + up_bias.astype(F32)
    cdf = 0.5 * (1.0 + lax.erf(pre * (0.5**0.5)))
    act = (pre * cdf).astype(BF)
    slope = cdf + pre * jnp.exp(-0.5 * pre * pre) * ((0.5 / jnp.pi) ** 0.5)
    grad_pre = (grad_act * slope).astype(BF)
    grad_wdown = inner_rows(act, grad_out).astype(BF)
    summed_wdown = sum_over_dp(grad_wdown, 0)
    grad_wup = inner_rows(normed2, grad_pre).astype(BF)
    summed_wup = sum_over_dp(grad_wup, 1)
    grad_normed2 = swap_sum(times_back(grad_pre, w_up).astype(BF))
    mlp = swap_sum(jnp.dot(act, w_down, preferred_element_type=F32).astype(BF))
    block_output = (resid + mlp + down_bias.astype(F32)).astype(BF).reshape(images.shape)
    grad_resid = grad_out.astype(F32) + norm_back(unit2, inv2, gain2, grad_normed2)
    resid_low = grad_resid.astype(BF)
    grad_wout = inner_rows(mixed, resid_low).astype(BF)
    summed_wout = sum_over_dp(grad_wout, 2)
    grad_mixed = times_back(resid_low, w_out).astype(BF).reshape(count, seq, heads, HD)
    grad_qkv = jnp.concatenate(
        [
            attend_backward(split[i, :, 0], split[i, :, 1], split[i, :, 2], grad_mixed[i], attended[i][1])
            for i in range(count)
        ],
        axis=0,
    ).reshape(rows, 3 * local)
    grad_wqkv = inner_rows(normed1, grad_qkv).astype(BF)
    summed_wqkv = sum_over_dp(grad_wqkv, 0).reshape(width, 3, local)
    bias_sums = jnp.sum(grad_qkv.astype(F32), axis=0)
    grad_normed1 = swap_sum(times_back(grad_qkv, w_qkv_flat).astype(BF))
    images_grad = (
        (grad_resid + norm_back(unit1, inv1, gain1, grad_normed1)).astype(BF).reshape(images.shape)
    )

    small = [
        jnp.sum(grad_normed1 * unit1, axis=0),
        jnp.sum(grad_normed1, axis=0),
        jnp.sum(grad_resid, axis=0),
        jnp.sum(grad_normed2 * unit2, axis=0),
        jnp.sum(grad_normed2, axis=0),
        jnp.sum(grad_out.astype(F32), axis=0),
        jnp.sum(grad_pre.astype(F32), axis=0),
        bias_sums[:local],
        bias_sums[2 * local :],
    ]
    flat = jnp.concatenate(small)
    length = flat.shape[0]
    padded = -(-length // 1024) * 1024
    flat = sum_small(jnp.pad(flat, (0, padded - length)).reshape(padded // 128, 128)).reshape(-1)
    out, at = [], 0
    for part in small:
        out.append(flat[at : at + part.shape[0]])
        at += part.shape[0]
    return (
        block_output,
        images_grad,
        out[0],
        out[1],
        summed_wqkv,
        jnp.stack([out[7], out[8]]),
        summed_wout,
        out[2],
        out[3],
        out[4],
        summed_wup,
        out[6],
        summed_wdown,
        out[5],
    )


CHUNKS = 2
ANY = pl.BlockSpec(memory_space=pl.ANY)
HBM = pl.BlockSpec(memory_space=pltpu.HBM)
VM = pl.BlockSpec(memory_space=pltpu.VMEM)
MIB = 1024 * 1024


def shape_of(shape, dtype):
    return jax.ShapeDtypeStruct(shape, dtype)


def nn(left, right):
    return jnp.dot(left, right, preferred_element_type=F32)


def normal_unit(values):
    mean = jnp.mean(values, axis=-1, keepdims=True)
    centred = values - mean
    spread = jnp.mean(centred * centred, axis=-1, keepdims=True)
    inv = lax.rsqrt(spread + EPS)
    return centred * inv, inv


def row_of(ref):
    return ref[...].astype(F32).reshape(1, ref.shape[0])


def side_of(where_ref, bits):
    bit = bits[0] if bits[0] == bits[1] else jnp.where(where_ref[1] == 0, bits[0], bits[1])
    return (where_ref[0] >> bit) & 1


class Chain:
    def __init__(self):
        self.last = None

    def __call__(
        self, body, args, in_specs, outs, out_specs, scratch=(), grid=(), vmem=40, aliases=None, name=None, prefetch=0, cost=0.001
    ):
        args, in_specs, run = list(args), list(in_specs), body
        if self.last is not None:
            spot = len(args)

            def run(*refs):
                body(*refs[:spot], *refs[spot + 1 :])

            args.append(self.last)
            in_specs.append(ANY)
        spec = pltpu.PrefetchScalarGridSpec(
            num_scalar_prefetch=prefetch,
            grid=grid,
            in_specs=in_specs,
            out_specs=out_specs,
            scratch_shapes=list(scratch),
        )
        made = pl.pallas_call(
            run,
            out_shape=outs,
            grid_spec=spec,
            input_output_aliases=aliases or {},
            compiler_params=pltpu.CompilerParams(vmem_limit_bytes=vmem * MIB),
            cost_estimate=pl.CostEstimate(flops=0, bytes_accessed=int(cost * 3e6), transcendentals=0),
            name=name,
        )(*args)
        self.last = made[0] if isinstance(made, (tuple, list)) else made
        return made


def row_chunks(rows):
    units, parts = rows // 16, CHUNKS
    cuts = [16 * (units * i // parts) for i in range(parts)] + [rows]
    return [(cuts[i], cuts[i + 1] - cuts[i]) for i in range(parts)]


def lane_halves():
    return lax.broadcasted_iota(jnp.int32, (1, 2 * HD), 1) < HD


def key_mask(length):
    return jnp.where(lax.broadcasted_iota(jnp.int32, (1, length), 1) < VALID, 0.0, -1e30)


def copier(sems):
    count = [0]

    def copy(source, target):
        made = pltpu.make_async_copy(source, target, sems.at[count[0]])
        count[0] += 1
        made.start()
        return made

    return copy


def attend_kernel(
    mask_ref, g_ref, s_ref, b_ref, x_ref, w_ref, wo_ref, cot_ref, wd_ref,
    part_ref, q_ref, k_ref, v_ref, mixed_ref, n1_ref, lse_ref, ga_ref, go_ref, bd_ref,
    x_b, w_b, wo_b, cot_b, wd_b, part_b, q_b, k_b, v_b, mixed_b, n1_b, lse_b, ga_b, go_b, sems,
):
    rows, width = x_ref.shape
    padded, local = q_ref.shape
    pairs = local // 128
    deep = wd_ref.shape[0] // pairs
    copy = copier(sems)
    get_x = copy(x_ref, x_b)
    get_w = [copy(w_ref.at[c], w_b.at[c]) for c in range(3)]
    get_cot = copy(cot_ref, cot_b)
    get_wd = [copy(wd_ref.at[pl.ds(i * deep, deep)], wd_b.at[i]) for i in range(pairs)]
    get_wo = copy(wo_ref, wo_b)
    puts = []
    get_x.wait()
    unit, _ = normal_unit(x_b[...].astype(F32))
    normed = unit * row_of(g_ref) + row_of(s_ref)
    n1_b[...] = jnp.concatenate([normed, jnp.zeros((padded - rows, width), F32)], axis=0).astype(BF)
    puts.append(copy(n1_b, n1_ref))
    lse_b[...] = jnp.zeros(lse_b.shape, F32)
    live = lax.broadcasted_iota(jnp.int32, (padded, 1), 0) < rows
    for c, (buf, ref, scale) in enumerate(((q_b, q_ref, HD ** (-0.5)), (k_b, k_ref, 1.0), (v_b, v_ref, 1.0))):
        get_w[c].wait()
        for at in range(0, local, 256):
            made = nn(n1_b[...], w_b[c, :, at : at + 256])
            if c != 1:
                made = made + b_ref[c // 2 : c // 2 + 1, at : at + 256].astype(F32)
            made = jnp.where(live, made, 0.0).astype(BF)
            buf[:, at : at + 256] = made * jnp.asarray(scale, BF)
        puts.append(copy(buf, ref))
    get_cot.wait()
    masked = cot_b[...].astype(F32) * mask_ref[0].astype(F32)
    go_b[...] = masked.astype(BF)
    puts.append(copy(go_b, go_ref))
    bd_ref[...] = jnp.sum(masked, axis=0, keepdims=True)
    for get in get_wd:
        get.wait()
    mask = key_mask(padded)
    first = lane_halves()
    lane = lax.broadcasted_iota(jnp.int32, (1, 128), 1)

    def pair(p, carry):
        cols = pl.ds(pl.multiple_of(p * 128, 128), 128)
        keys, vals = k_b[:, cols], v_b[:, cols]
        query = q_b[:, cols]
        zero, ones = jnp.zeros_like(keys), jnp.ones_like(vals)
        own_k = (jnp.where(first, keys, zero), jnp.where(first, zero, keys))
        own_v = (jnp.where(first, vals, ones), jnp.where(first, ones, vals))
        ga_b[:, pl.ds(pl.multiple_of(p * deep, deep), deep)] = times_back(go_b[...], wd_b[p]).astype(BF)
        outs = []
        logs = lse_b[...]
        for h in range(2):
            scores = times_back(query, own_k[h]) + mask
            peak = jnp.max(scores, axis=-1, keepdims=True)
            made = nn(jnp.exp(scores - peak).astype(BF), own_v[h])
            total = made[:, HD : HD + 1] if h == 0 else made[:, 0:1]
            outs.append(made * (1.0 / total))
            logs = jnp.where(lane == 2 * p + h, peak + jnp.log(total), logs)
        lse_b[...] = logs
        mixed_b[:, cols] = jnp.where(first, outs[0], outs[1]).astype(BF)
        return carry

    lax.fori_loop(0, pairs, pair, 0)
    puts += [copy(ga_b, ga_ref), copy(mixed_b, mixed_ref), copy(lse_b, lse_ref)]
    get_wo.wait()
    for at in range(0, width, 256):
        made = nn(mixed_b[...], wo_b[:, at : at + 256])
        part_b[:, at : at + 256] = made[:rows].astype(BF)
    puts.append(copy(part_b, part_ref))
    for put in puts:
        put.wait()


def attend(chain, mask, gain, shift, bias, x, w3, w_out, cot, w_down):
    rows, width = x.shape
    local = w3.shape[2]
    hidden = w_down.shape[0]
    padded = -(-rows // 16) * 16
    pairs = local // 128
    slab = ((rows, width), BF)
    wide = ((padded, local), BF)
    outs = (slab, wide, wide, wide, wide, ((padded, width), BF), ((padded, 128), F32), ((rows, hidden), BF), slab)
    held = (slab, ((3, width, local), BF), ((local, width), BF), slab, ((pairs, hidden // pairs, width), BF)) + outs
    return chain(
        attend_kernel,
        (mask, gain, shift, bias, x, w3, w_out, cot, w_down),
        [VM] * 3 + [HBM] * 5,
        tuple(shape_of(*out) for out in outs) + (shape_of((1, width), F32),),
        (HBM,) * len(outs) + (VM,),
        [pltpu.VMEM(*hold) for hold in held] + [pltpu.SemaphoreType.DMA((7 + pairs + len(outs),))],
        name="attend",
        vmem=60,
        prefetch=1,
    )


def gelu_pair(pre):
    cdf = 0.5 + 0.5 * lax.erf(pre * (0.5**0.5))
    return cdf, cdf + pre * jnp.exp(-0.5 * pre * pre) * ((0.5 / jnp.pi) ** 0.5)


def feed_kernel(
    where_ref, ob_ref, g_ref, s_ref, ub_ref, x_ref, pa_ref, pb_ref, go_ref, wu_ref, ga_ref,
    act_ref, gn_ref, ds0_ref, ds1_ref, dk0_ref, dk1_ref, us0_ref, us1_ref, uk0_ref, uk1_ref, bu_ref,
    x_b, pa_b, pb_b, go_b, wu_b, ga_b, act_b, n2_b, down_b, up_b, gn_b, total, bias, sems, *, bits,
):
    rows, width = x_ref.shape
    hidden = wu_ref.shape[1]
    size = hidden // 4
    tall = width // 4
    sides = [side_of(where_ref, bit) for bit in bits]
    starts = [pl.multiple_of((2 * lane + (1 - sides[lane])) * size, size) for lane in range(2)]
    starts += [pl.multiple_of((2 * lane + sides[lane]) * size, size) for lane in range(2)]
    tops = [pl.multiple_of((2 * lane + (1 - sides[2 + lane])) * tall, tall) for lane in range(2)]
    tops += [pl.multiple_of((2 * lane + sides[2 + lane]) * tall, tall) for lane in range(2)]
    copy = copier(sems)
    gets = [copy(x_ref, x_b), copy(pa_ref, pa_b), copy(pb_ref, pb_b)]
    get_w, get_ga = [], []
    for c in range(4):
        get_w.append(copy(wu_ref.at[:, pl.ds(starts[c], size)], wu_b.at[c]))
        get_ga.append(copy(ga_ref.at[:, pl.ds(starts[c], size)], ga_b.at[c]))
        if c == 0:
            get_go = copy(go_ref, go_b)
    puts = []
    bias[...] = row_of(ub_ref)
    for get in gets:
        get.wait()
    resid = x_b[...].astype(F32) + (pa_b[...].astype(F32) + pb_b[...].astype(F32)) + row_of(ob_ref)
    unit, _ = normal_unit(resid)
    n2_b[...] = (unit * row_of(g_ref) + row_of(s_ref)).astype(BF)

    def front(c):
        get_w[c].wait()
        get_ga[c].wait()
        for at in range(0, size, 256):
            cols = pl.ds(pl.multiple_of(starts[c] + at, 256), 256)
            pre = nn(n2_b[...], wu_b[c, :, at : at + 256]) + bias[:, cols]
            cdf, slope = gelu_pair(pre)
            act_b[c, :, at : at + 256] = (pre * cdf).astype(BF)
            grad_pre = (ga_b[c, :, at : at + 256].astype(F32) * slope).astype(BF)
            ga_b[c, :, at : at + 256] = grad_pre
            bu_ref[:, cols] = jnp.sum(grad_pre.astype(F32), axis=0, keepdims=True)
        puts.append(copy(act_b.at[c], act_ref.at[:, pl.ds(starts[c], size)]))

    def back(c):
        if c == 0:
            get_go.wait()
        for at in range(0, width, 512):
            made = inner_rows(act_b[c], go_b[:, at : at + 512])
            down_b[c, :, at : at + 512] = made.astype(BF)
        puts.append(copy(down_b.at[c], (ds0_ref, ds1_ref, dk0_ref, dk1_ref)[c]))
        for piece in range(4):
            made = inner_rows(n2_b[:, pl.ds(tops[piece], tall)], ga_b[c])
            up_b[piece, :, pl.ds(starts[c], size)] = made.astype(BF)
        for at in range(0, width, 512):
            made = times_back(ga_b[c], wu_b[c, at : at + 512, :])
            if c:
                made = made + total[:, at : at + 512]
            if c < 3:
                total[:, at : at + 512] = made
            else:
                gn_b[:, at : at + 512] = made.astype(BF)

    for c in range(5):
        if c < 4:
            front(c)
        if c:
            back(c - 1)
    puts.append(copy(gn_b, gn_ref))
    for piece, ref in enumerate((us0_ref, us1_ref, uk0_ref, uk1_ref)):
        puts.append(copy(up_b.at[piece], ref))
    for put in puts:
        put.wait()


def feed(chain, where, bits, out_bias, gain, shift, up_bias, x, pa, pb, go, w_up, ga):
    rows, width = x.shape
    hidden = w_up.shape[1]

    def body(*refs):
        feed_kernel(*refs, bits=bits)

    slab = ((rows, width), BF)
    deep = ((4, rows, hidden // 4), BF)
    outs = (((rows, hidden), BF), slab) + (((hidden // 4, width), BF),) * 4 + (((width // 4, hidden), BF),) * 4
    held = (slab,) * 4 + (((4, width, hidden // 4), BF), deep, deep, slab, ((4, hidden // 4, width), BF))
    held += (((4, width // 4, hidden), BF), slab, ((rows, width), F32), ((1, hidden), F32))
    return chain(
        body,
        (where, out_bias, gain, shift, up_bias, x, pa, pb, go, w_up, ga),
        [VM] * 4 + [HBM] * 6,
        tuple(shape_of(*out) for out in outs) + (shape_of((1, hidden), F32),),
        (HBM,) * len(outs) + (VM,),
        [pltpu.VMEM(*hold) for hold in held] + [pltpu.SemaphoreType.DMA((12 + 4 + len(outs),))],
        name="feed",
        vmem=60,
        prefetch=1,
    )


def qkv_grad(chain, where, n1, grads, out_grad, bits, flip):
    width = n1.shape[1]
    local = grads.shape[1] // 3
    size = width // 4

    def body(where_ref, n1_ref, g_ref, o_ref, first_ref, second_ref):
        def product(ref, start):
            for i in range(4):
                made = inner_rows(n1_ref[:, i * size : (i + 1) * size], g_ref[:, pl.ds(start, local)])
                ref[i * size : (i + 1) * size, :] = made.astype(BF)

        product(first_ref, pl.multiple_of((side_of(where_ref, bits[0]) ^ flip) * local, local))
        which = side_of(where_ref, bits[1]) ^ flip

        @pl.when(which == 0)
        def _():
            product(second_ref, 2 * local)

        @pl.when(which == 1)
        def _():
            second_ref[...] = o_ref[...]

    return chain(
        body,
        (where, n1, grads, out_grad),
        [VM, VM, VM],
        (shape_of((width, local), BF),) * 2,
        (VM,) * 2,
        name="qkv_grad",
        prefetch=1,
    )


TILES = 4


def paired(own, other):
    return own[...].astype(F32) + other[...].astype(F32)


def down(chain, act, w_down):
    rows, hidden = act.shape
    width = w_down.shape[1]
    size = width // TILES
    deep = hidden // TILES

    def body(act_ref, w_ref, *rest):
        out_ref, w_buf, sems = rest
        copies = [
            pltpu.make_async_copy(w_ref.at[pl.ds(i * deep, deep)], w_buf.at[pl.ds(i * deep, deep)], sems.at[i])
            for i in range(TILES)
        ]
        for copy in copies:
            copy.start()
        for copy in copies:
            copy.wait()
        for i in range(TILES):
            out_ref[:, i * size : (i + 1) * size] = nn(act_ref[...], w_buf[:, i * size : (i + 1) * size]).astype(BF)

    return chain(
        body,
        (act, w_down),
        [VM, HBM],
        shape_of((rows, width), BF),
        VM,
        [pltpu.VMEM((hidden, width), BF), pltpu.SemaphoreType.DMA((TILES,))],
        name="down",
    )


def resid_back_kernel(
    x_ref, pa_ref, pb_ref, ob_ref, g_ref, ga_ref, gb_ref, go_ref, mixed_ref, wo_ref, gr_ref, gm_ref, sums_ref, og_ref, low
):
    rows, width = x_ref.shape
    padded, local = mixed_ref.shape
    resid = x_ref[...].astype(F32) + (pa_ref[...].astype(F32) + pb_ref[...].astype(F32)) + row_of(ob_ref)
    unit, inv = normal_unit(resid)
    grad = paired(ga_ref, gb_ref)
    total = go_ref[...].astype(F32) + norm_back(unit, inv, row_of(g_ref), grad)
    gr_ref[...] = total
    low[...] = jnp.concatenate([total, jnp.zeros((padded - rows, width), F32)], axis=0).astype(BF)
    sums_ref[...] = jnp.concatenate(
        [
            jnp.sum(total, axis=0, keepdims=True),
            jnp.sum(grad * unit, axis=0, keepdims=True),
            jnp.sum(grad, axis=0, keepdims=True),
            jnp.zeros((5, width), F32),
        ],
        axis=0,
    )
    for i in range(2):
        for at in range(0, width // 2, 256):
            start = i * width // 2 + at
            made = inner_rows(mixed_ref[...], low[:, start : start + 256])
            og_ref[i * local : (i + 1) * local, at : at + 256] = made.astype(BF)
    for at in range(0, local, 256):
        gm_ref[:, at : at + 256] = times_back(low[...], wo_ref[at : at + 256, :]).astype(BF)


def resid_back(chain, x, pa, pb, out_bias, gain, ga, gb, go, mixed, w_out):
    rows, width = x.shape
    padded, local = mixed.shape
    return chain(
        resid_back_kernel,
        (x, pa, pb, out_bias, gain, ga, gb, go, mixed, w_out),
        [VM] * 10,
        (
            shape_of((rows, width), F32),
            shape_of((padded, local), BF),
            shape_of((8, width), F32),
            shape_of((2 * local, width // 2), BF),
        ),
        (VM,) * 4,
        [pltpu.VMEM((padded, width), BF)],
        name="resid_back",
    )


def attend_back_kernel(q_ref, k_ref, v_ref, mixed_ref, gm_ref, lse_ref, out_ref, bias_ref, probs_s, slopes_s):
    padded, local = q_ref.shape
    mask = key_mask(padded)
    first = lane_halves()
    lane = lax.broadcasted_iota(jnp.int32, (1, 128), 1)

    def pair(p, carry):
        cols = pl.ds(pl.multiple_of(p * 128, 128), 128)
        keys, vals = k_ref[:, cols], v_ref[:, cols]
        zero = jnp.zeros_like(keys)
        own_k = (jnp.where(first, keys, zero), jnp.where(first, zero, keys))
        own_v = (jnp.where(first, vals, zero), jnp.where(first, zero, vals))
        for at, size in row_chunks(padded):
            query = q_ref[at : at + size, cols]
            grad = gm_ref[at : at + size, cols]
            both = grad.astype(F32) * mixed_ref[at : at + size, cols].astype(F32)
            logs = lse_ref[at : at + size, :]
            outs = []
            for h in range(2):
                own_lanes = first if h == 0 else jnp.logical_not(first)
                delta = jnp.sum(jnp.where(own_lanes, both, 0.0), axis=-1, keepdims=True)
                log = jnp.sum(jnp.where(lane == 2 * p + h, logs, 0.0), axis=-1, keepdims=True)
                probs = jnp.exp(times_back(query, own_k[h]) + mask - log)
                slope = (probs * (times_back(grad, own_v[h]) - delta)).astype(BF)
                probs_s[h, at : at + size, :] = probs.astype(BF)
                slopes_s[h, at : at + size, :] = slope
                outs.append(nn(slope, keys))
            out_ref[at : at + size, cols] = (jnp.where(first, outs[0], outs[1]) * HD ** (-0.5)).astype(BF)
        grad_t = gm_ref[:, cols].astype(F32).T.astype(BF)
        query_t = q_ref[:, cols].astype(F32).T.astype(BF)
        grad_k = [nn(query_t[HD * h : HD * h + HD], slopes_s[h]) for h in range(2)]
        grad_v = [nn(grad_t[HD * h : HD * h + HD], probs_s[h]) for h in range(2)]
        cols_k = pl.ds(pl.multiple_of(local + p * 128, 128), 128)
        cols_v = pl.ds(pl.multiple_of(2 * local + p * 128, 128), 128)
        out_ref[:, cols_k] = jnp.concatenate(grad_k, axis=0).T.astype(BF)
        out_ref[:, cols_v] = jnp.concatenate(grad_v, axis=0).T.astype(BF)
        return carry

    lax.fori_loop(0, local // 128, pair, 0)
    bias_ref[...] = jnp.sum(out_ref[...].astype(F32), axis=0, keepdims=True)


def attend_back(chain, q, k, v, mixed, gm, lse):
    padded, local = q.shape
    return chain(
        attend_back_kernel,
        (q, k, v, mixed, gm, lse),
        [VM] * 6,
        (shape_of((padded, 3 * local), BF), shape_of((1, 3 * local), F32)),
        (VM, VM),
        [pltpu.VMEM((2, padded, padded), BF), pltpu.VMEM((2, padded, padded), BF)],
        name="attend_back",
    )


def back_in(chain, grads, w3, rows):
    _, width, local = w3.shape
    size = width // TILES

    def body(g_ref, w_ref, *rest):
        out_ref, w_buf, sems = rest
        copies = [
            pltpu.make_async_copy(w_ref.at[:, pl.ds(i * size, size)], w_buf.at[i], sems.at[i]) for i in range(TILES)
        ]
        for copy in copies:
            copy.start()
        for i in range(TILES):
            copies[i].wait()
            total = times_back(g_ref[:, :local], w_buf[i, 0])
            for c in range(1, 3):
                total += times_back(g_ref[:, c * local : (c + 1) * local], w_buf[i, c])
            out_ref[:, i * size : (i + 1) * size] = total[:rows].astype(BF)

    return chain(
        body,
        (grads, w3),
        [VM, HBM],
        shape_of((rows, width), BF),
        VM,
        [pltpu.VMEM((TILES, 3, size, local), BF), pltpu.SemaphoreType.DMA((TILES,))],
        name="back_in",
    )


def images_back_kernel(x_ref, g_ref, gr_ref, ga_ref, gb_ref, bd_ref, bu_ref, s2_ref, bq_ref, out_ref, pack_ref):
    unit, inv = normal_unit(x_ref[...].astype(F32))
    grad = paired(ga_ref, gb_ref)
    out_ref[...] = (gr_ref[...] + norm_back(unit, inv, row_of(g_ref), grad)).astype(BF)
    width = x_ref.shape[1]
    hidden = bu_ref.shape[1]
    local = bq_ref.shape[1] // 3
    pack_ref[0:1, :] = jnp.sum(grad * unit, axis=0, keepdims=True)
    pack_ref[1:2, :] = jnp.sum(grad, axis=0, keepdims=True)
    pack_ref[2:5, :] = s2_ref[0:3, :]
    pack_ref[5:6, :] = bd_ref[...]
    for i in range(hidden // width):
        pack_ref[6 + i : 7 + i, :] = bu_ref[:, i * width : (i + 1) * width]
    after = 6 + hidden // width
    pack_ref[after : after + 1, :local] = bq_ref[:, :local]
    pack_ref[after : after + 1, local:] = bq_ref[:, 2 * local :]
    pack_ref[after + 1 :, :] = jnp.zeros((pack_ref.shape[0] - after - 1, width), F32)


def images_back(chain, x, gain, gr, ga, gb, bd, bu, s2, bq):
    return chain(
        images_back_kernel,
        (x, gain, gr, ga, gb, bd, bu, s2, bq),
        [VM] * 9,
        (shape_of(x.shape, BF), shape_of((16, x.shape[1]), F32)),
        (VM, VM),
        name="images_back",
    )


def block_out_kernel(x_ref, pa_ref, pb_ref, ob_ref, ma_ref, mb_ref, db_ref, out_ref):
    resid = x_ref[...].astype(F32) + (pa_ref[...].astype(F32) + pb_ref[...].astype(F32)) + row_of(ob_ref)
    out_ref[...] = (resid + paired(ma_ref, mb_ref) + row_of(db_ref)).astype(BF)


def block_out(chain, x, pa, pb, out_bias, ma, mb, down_bias):
    return chain(
        block_out_kernel,
        (x, pa, pb, out_bias, ma, mb, down_bias),
        [VM] * 7,
        shape_of(x.shape, BF), VM, name="block_out"
    )


def add_split_kernel(where_ref, k0_ref, k1_ref, r0_ref, r1_ref, send_ref, keep_ref):
    keep_ref[...] = (k0_ref[...].astype(F32) + r0_ref[...].astype(F32)).astype(BF)
    send_ref[...] = (k1_ref[...].astype(F32) + r1_ref[...].astype(F32)).astype(BF)


def add_split(chain, where, bit, keep, recv):
    rows, width = keep.shape
    half = rows // 2
    block = (half, width)
    own = pl.BlockSpec(block, lambda i, w: (side_of(w, bit), 0))
    other = pl.BlockSpec(block, lambda i, w: (1 - side_of(w, bit), 0))
    out = pl.BlockSpec(block, lambda i, w: (0, 0))
    return chain(
        add_split_kernel,
        (where, keep, keep, recv, recv),
        [own, other, own, other],
        (shape_of((half, width), BF),) * 2,
        (out, out),
        grid=(1,),
        name="add_split",
        prefetch=1,
        vmem=16,
    )


def add_kernel(a_ref, b_ref, out_ref):
    out_ref[...] = (a_ref[...].astype(F32) + b_ref[...].astype(F32)).astype(out_ref.dtype)


def add(chain, a, b):
    return chain(add_kernel, (a, b), [VM, VM], shape_of(a.shape, a.dtype), VM, name="add", vmem=16)


def join(chain, where, bit, own, other):
    half, width = own.shape

    def body(where_ref, own_ref, other_ref, out_ref):
        side = side_of(where_ref, bit)
        out_ref[pl.ds(pl.multiple_of(side * half, 16), half), :] = own_ref[...]
        out_ref[pl.ds(pl.multiple_of((1 - side) * half, 16), half), :] = other_ref[...]

    return chain(
        body,
        (where, own, other),
        [VM, VM],
        shape_of((2 * half, width), BF),
        VM,
        name="join",
        prefetch=1,
        vmem=16,
    )


class Home:
    def __init__(self, shape):
        self.shape, self.now = shape, None


def finish(chain, where, bits, flip, piece, homes):
    half, width = piece.shape
    parts = 4
    block = half // parts
    targets = list(dict.fromkeys(home for home, _ in homes))
    old = [home for home in targets if home.now is not None]

    def body(where_ref, piece_ref, *rest):
        outs = rest[len(old) : len(old) + len(targets)]
        made, sems = rest[-2:]
        which = side_of(where_ref, bits) ^ flip

        def write(number):
            home, row = homes[number]
            out_ref = outs[targets.index(home)]
            copies = []
            for i in range(parts):
                made[i * block : (i + 1) * block, :] = piece_ref[i * block : (i + 1) * block, :].astype(F32)
                if home.shape[1] == width:
                    place = out_ref.at[pl.ds(row + i * block, block)]
                else:
                    high = home.shape[0]
                    place = out_ref.at[pl.ds(i * block % high, block), pl.ds(i * block // high * width, width)]
                copies.append(pltpu.make_async_copy(made.at[pl.ds(i * block, block)], place, sems.at[i]))
                copies[-1].start()
            for copy in copies:
                copy.wait()

        for number in range(2):

            @pl.when(which == number)
            def _(number=number):
                write(number)

    made = chain(
        body,
        (where, piece, *(home.now for home in old)),
        [VM] + [HBM] * len(old),
        tuple(shape_of(home.shape, F32) for home in targets) + (shape_of((8, 128), F32),),
        (HBM,) * (len(targets) + 1),
        [pltpu.VMEM((half, width), F32), pltpu.SemaphoreType.DMA((parts,))],
        aliases={2 + i: targets.index(home) for i, home in enumerate(old)},
        name="finish",
        prefetch=1,
        vmem=16,
    )
    for home, now in zip(targets, made[:-1], strict=True):
        home.now = now
    chain.last = made[-1]


def unpack(chain, pack, hidden, local):
    width = pack.shape[1]
    steps = hidden // width

    def body(pack_ref, *outs):
        for i in range(6):
            outs[i][...] = pack_ref[i, :]
        for i in range(steps):
            outs[6][i * width : (i + 1) * width] = pack_ref[6 + i, :]
        for i in range(2):
            outs[7][i : i + 1, :] = pack_ref[6 + steps : 7 + steps, i * local : (i + 1) * local]

    line = shape_of((width,), F32)
    return chain(
        body,
        (pack,),
        [VM],
        (line,) * 6 + (shape_of((hidden,), F32), shape_of((2, local), F32)),
        (VM,) * 8,
        name="unpack",
    )


class Lane:
    def __init__(self, chain, where, order, homes):
        self.chain, self.where, self.homes = chain, where, homes
        self.bits = list(zip(*order, strict=True))
        self.keep = self.send = None
        self.stage = 0

    def begin(self, keep, send):
        self.keep, self.send = keep, send

    def over(self, bits, piece):
        pairs = [
            (2 * i + core, 2 * (i ^ (1 << bits[core])) + core) for i in range(lax.axis_size("dp")) for core in range(2)
        ]
        return lax.ppermute(piece, ("dp", "tensor"), pairs)

    def step(self):
        stage, bits, chain = self.stage, self.bits, self.chain
        self.stage += 1
        if stage < 2:
            recv = self.over(bits[stage], self.send)
            self.send, self.keep = add_split(chain, self.where, bits[stage + 1], self.keep, recv)
        elif stage == 2:
            self.keep = add(chain, self.keep, self.over(bits[2], self.send))
        elif stage == 3:
            self.keep = add(chain, self.keep, self.over((3, 3), self.keep))
        elif stage < 6:
            bit = bits[6 - stage]
            self.keep = join(chain, self.where, bit, self.keep, self.over(bit, self.keep))
        elif stage == 6:
            self.send = self.over(bits[0], self.keep)
            finish(chain, self.where, bits[0], 0, self.keep, self.homes)
        else:
            finish(chain, self.where, bits[0], 1, self.send, self.homes)


ORDERS = {
    "D0": ((1, 2, 0), (0, 2, 1)),
    "D1": ((2, 0, 1), (1, 0, 2)),
    "U0": ((2, 0, 1), (2, 1, 0)),
    "U1": ((1, 0, 2), (0, 1, 2)),
    "Q0": ((0, 1, 2), (0, 1, 2)),
    "Q1": ((1, 0, 2), (2, 1, 0)),
}
SCHEDULE = (
    "resid_back", "attend_back", "q_send", "D1", "back_in", "U0", "D0", "q_keep", "D1", "U0", "U1",
    "D1", "Q1", "D0", "Q0", "U1", "D1", "D0", "images_back", "U1", "D0", "Q0", "Q1", "U1", "U0",
    "pack0", "Q1", "D1", "U1", "D0", "U0", "pack1", "Q1", "Q0", "U0", "pack2", "D1", "Q1", "Q0", "U1",
    "down", "Q0", "U0", "Q1", "D0", "D0", "D1", "D1", "pack3", "U1", "D0", "Q0", "Q1", "U0", "unpack",
    "Q0", "U1", "block_out", "U0", "Q0", "Q1",
)


def shards_cube(
    images,
    image_mask,
    cotangent,
    ln1_gain,
    ln1_bias,
    w_qkv,
    qv_bias,
    w_out,
    out_bias,
    ln2_gain,
    ln2_bias,
    w_up,
    up_bias,
    w_down,
    down_bias,
):
    _, rows, width = images.shape
    local = w_qkv.shape[2]
    hidden = w_up.shape[1]
    x = images.reshape(rows, width)
    cot = cotangent.reshape(rows, width)
    where = jnp.stack([lax.axis_index("dp"), lax.axis_index("tensor")]).astype(jnp.int32)
    w3 = jnp.transpose(w_qkv, (1, 0, 2))
    chain = Chain()

    def swapped(piece):
        return lax.ppermute(piece, "tensor", [(0, 1), (1, 0)])

    downs, ups, outs = Home((hidden, width)), Home((width, hidden)), Home((local, width))
    projections = Home((3 * width, local))
    places = {
        "D0": ((downs, 0), (downs, hidden // 4)),
        "D1": ((downs, hidden // 2), (downs, 3 * hidden // 4)),
        "U0": ((ups, 0), (ups, width // 4)),
        "U1": ((ups, width // 2), (ups, 3 * width // 4)),
        "Q0": ((projections, 0), (projections, width)),
        "Q1": ((projections, 2 * width), (outs, 0)),
    }
    lanes = {name: Lane(chain, where, ORDERS[name], homes) for name, homes in places.items()}
    first = {name: lane.bits[0] for name, lane in lanes.items()}

    part, q, k, v, mixed, n1, lse, ga, go, bd = attend(
        chain, image_mask, ln1_gain, ln1_bias, qv_bias, x, w3, w_out, cot, w_down
    )
    part_b = swapped(part)
    bits = [first[name] for name in ("D0", "D1", "U0", "U1")]
    act, gn2, ds0, ds1, dk0, dk1, us0, us1, uk0, uk1, bu = feed(
        chain, where, bits, out_bias, ln2_gain, ln2_bias, up_bias, x, part, part_b, go, w_up, ga
    )
    for name, keep, send in (("D0", dk0, ds0), ("D1", dk1, ds1), ("U0", uk0, us0), ("U1", uk1, us1)):
        lanes[name].begin(keep, send)
    gn2_b = swapped(gn2)
    qkv = (first["Q0"], first["Q1"])
    have = {}

    def compute(name):
        if name == "down":
            have["mlp"] = down(chain, act, w_down)
            have["mlpb"] = swapped(have["mlp"])
        elif name == "resid_back":
            have["gr"], have["gm"], have["s2"], have["og"] = resid_back(
                chain, x, part, part_b, out_bias, ln2_gain, gn2, gn2_b, go, mixed, w_out
            )
        elif name == "attend_back":
            have["grads"], have["bq"] = attend_back(chain, q, k, v, mixed, have["gm"], lse)
        elif name == "q_send":
            have["qs"] = qkv_grad(chain, where, n1, have["grads"], have["og"], qkv, 1)
        elif name == "q_keep":
            kept = qkv_grad(chain, where, n1, have["grads"], have["og"], qkv, 0)
            for i in range(2):
                lanes["Q%d" % i].begin(kept[i], have["qs"][i])
        elif name == "back_in":
            have["gn1"] = back_in(chain, have["grads"], w3, rows)
            have["gn1b"] = swapped(have["gn1"])
        elif name == "images_back":
            have["out"], have["pack"] = images_back(
                chain, x, ln1_gain, have["gr"], have["gn1"], have["gn1b"], bd, bu, have["s2"], have["bq"]
            )
        elif name == "block_out":
            have["block"] = block_out(chain, x, part, part_b, out_bias, have["mlp"], have["mlpb"], down_bias)
        elif name[:4] == "pack":
            have["pack"] = add(chain, have["pack"], lax.ppermute(have["pack"], "dp", xor_pairs(1 << int(name[4]))))
        elif name == "unpack":
            have["small"] = unpack(chain, have["pack"], hidden, local)

    for name in SCHEDULE:
        if name in lanes:
            lanes[name].step()
        else:
            compute(name)
    small = have["small"]
    return (
        have["block"].reshape(images.shape),
        have["out"].reshape(images.shape),
        small[0],
        small[1],
        jnp.transpose(projections.now.reshape(3, width, local), (1, 0, 2)),
        small[7],
        outs.now,
        small[2],
        small[3],
        small[4],
        ups.now,
        small[6],
        downs.now,
        small[5],
    )


def shards(*args):
    images, w_up = args[0], args[11]
    cube = lax.axis_size("dp") == 16 and lax.axis_size("tensor") == 2
    if cube and images.shape[0] == 1 and w_up.shape[1] == 2 * w_up.shape[0]:
        return shards_cube(*args)
    return shards_any(*args)


def solution(mesh):
    in_specs = (
        P("dp", None, None),
        P("dp"),
        P("dp", None, None),
        P(),
        P(),
        P(None, None, "tensor"),
        P(None, "tensor"),
        P("tensor", None),
        P(),
        P(),
        P(),
        P(None, "tensor"),
        P("tensor"),
        P("tensor", None),
        P(),
    )
    out_specs = (
        P("dp", None, None),
        P("dp", None, None),
        P(),
        P(),
        P(None, None, "tensor"),
        P(None, "tensor"),
        P("tensor", None),
        P(),
        P(),
        P(),
        P(None, "tensor"),
        P("tensor"),
        P("tensor", None),
        P(),
    )
    return jax.shard_map(shards, mesh=mesh, in_specs=in_specs, out_specs=out_specs, check_vma=False)
```
